32 devices in a mesh: cent: 8 (over z, y), grp: 4 (over x, core).
Axes of the slice: x: 2, y: 2, z: 4, core: 2. Of those that a mesh axis runs over, the one named last changes fastest.
Arguments:
- queries: bfloat16 [64, 32, 128], P('grp'), may hold values from -6 to 6
- centroids: bfloat16 [262144, 128], P('cent'), may hold values from -0.5 to 0.5
- candidates: int32 [4, 8, 2, 64], P('grp', 'cent'), may hold values from 0 to 16383, as said below
- token_codes: int32 [16384, 128], P(('cent', 'grp')), may hold values from 0 to 32767
- resid_words: int32 [16384, 32, 128], P(('cent', 'grp')), may hold values from 0 to 255
- lengths: int32 [16384], P(('cent', 'grp')), may hold values from 1 to 128
- levels: float32 [4, 128], replicated, may hold values from -0.3125 to 0.3125
Outputs:
- token_best: float32 [64, 32], P('grp')
- passage_scores: float32 [4, 8, 2, 64], P('grp', 'cent')
The draws below stay inside these ranges and needn't reach their ends.
Inputs may be any that keep to these rules, and one draw needn't show every extreme that they name: `candidates`: the entries of one [g, c] block are all different and name at most 8 passages of any one owner block (passages owner * 512 to owner * 512 + 511); one owner block gets exactly 8 from every [g, c] block.
All inputs are finite; a program needn't handle non-finite values.
Results may differ from the reference program's by a relative error of at most 0.0003.
Values may be sent and summed in bfloat16 or wider, within the bound.
No kernel may reach another device: no remote copies, remote signals or barrier semaphores. Data moves between devices by JAX's collectives and lax.ppermute only.
A program may use at most 128 MiB of HBM per device.

```python
import jax
import jax.numpy as jnp
from jax import lax

D = 128
QT = 32
CENT_DEV = 32768
PLEN = 128
NCAND = 64
QRY_DEV = 2
PASS_DEV = 512
GROUPS = 4
CSH = 8
NQ = 64
NCENT = 262144
NPASS = 16384
PACKED = 32
CAP = 8


def draw_candidates(key, part):
    base_key = jax.random.fold_in(key, 11)
    pair_count = QRY_DEV * NCAND
    owner_total = GROUPS * CSH
    token_total = owner_total * CAP
    hot_key, tier_key, block_key = jax.random.split(base_key, 3)
    popular_holder = jax.random.randint(hot_key, (), 0, owner_total)
    holder_levels = jax.random.randint(tier_key, (owner_total,), 0, 4)

    def one_block(source):
        source_key = jax.random.fold_in(block_key, source)
        noise_key, order_key, offset_key = jax.random.split(source_key, 3)
        token_numbers = jnp.arange(token_total, dtype=jnp.int32)
        token_holder = token_numbers // CAP
        random_jitter = jax.random.randint(noise_key, (token_total,), 0, 65536)
        extra_credit = jnp.where(token_holder == popular_holder, 262144, jnp.take(holder_levels, token_holder) * 16384)
        rank_weight = (random_jitter + extra_credit) * 4096 + token_numbers
        top_values, chosen = lax.top_k(rank_weight, pair_count)
        chosen = jax.random.permutation(order_key, chosen)
        chosen_owner = chosen // CAP
        chosen_slot = chosen % CAP
        offsets = jax.random.randint(offset_key, (owner_total,), 0, PASS_DEV)
        local_ids = (jnp.take(offsets, chosen_owner) + chosen_slot) % PASS_DEV
        return (chosen_owner * PASS_DEV + local_ids).astype(jnp.int32)
    blocks = jax.vmap(one_block)(jnp.arange(owner_total, dtype=jnp.int32))
    blocks = blocks.reshape(CSH, GROUPS, QRY_DEV, NCAND)
    return jnp.transpose(blocks, (1, 0, 2, 3))


def draw_lengths(key, part):
    base_key = jax.random.fold_in(key, 23)
    values = jax.random.randint(base_key, (NPASS,), 1, PLEN + 1)
    return values.at[0].set(PLEN).at[1].set(1).astype(jnp.int32)


def touch_ends(entries, stream_key, low, high):
    dims = entries.shape
    index_at = [jax.random.randint(jax.random.fold_in(stream_key, axis), (), 0, dims[axis]) for axis in range(len(dims))]
    entries = entries.at[tuple(index_at)].set(low)
    longest = dims.index(max(dims))
    index_at[longest] = (index_at[longest] + 1) % dims[longest]
    return entries.at[tuple(index_at)].set(high)


def block_levels(rng, shape, cuts, smallest, largest):
    factor_of = 1.0
    for dim, shards_of in cuts:
        draws = jax.random.uniform(jax.random.fold_in(jax.random.fold_in(rng, 6), dim), (shards_of,), jnp.float32, smallest / len(cuts), largest / len(cuts))
        factor_of = factor_of * jnp.repeat(jnp.exp(draws), shape[dim] // shards_of).reshape((-1,) + (1,) * (len(shape) - 1 - dim))
    return factor_of


def gaussian(stream_key, extent, spread, reach, cuts=(), kind=jnp.bfloat16):
    factor_of = block_levels(stream_key, extent, cuts, -0.22, 0.18) if cuts else 1.0
    values = jax.random.normal(stream_key, extent, jnp.float32) * spread * factor_of
    return jnp.minimum(jnp.maximum(values, -reach), reach).astype(kind)


def setup_inputs(seed: int = 0) -> dict:
    key_of = jax.random.split(jax.random.key(seed), 8)
    queries = gaussian(key_of[0], (NQ, QT, D), 1.0, 6.0, ((0, 4),))
    centroids = gaussian(key_of[1], (NCENT, D), D ** -0.5, 0.5, ((0, 8),))
    candidates = draw_candidates(jax.random.fold_in(key_of[7], 71), 0)
    token_codes = touch_ends(jax.random.randint(key_of[3], (NPASS, PLEN), 0, CENT_DEV), jax.random.fold_in(key_of[3], 1), 0, CENT_DEV - 1).astype(jnp.int32)
    resid_words = touch_ends(jax.random.randint(key_of[4], (NPASS, PACKED, D), 0, 256), jax.random.fold_in(key_of[4], 1), 0, 255).astype(jnp.int32)
    lengths = draw_lengths(jax.random.fold_in(key_of[7], 71), 0)
    levels = gaussian(key_of[6], (4, D), 0.05, 0.3125, (), jnp.float32)
    return dict(queries=queries, centroids=centroids, candidates=candidates, token_codes=token_codes, resid_words=resid_words, lengths=lengths, levels=levels)


def unpack_levels(words, levels):
    fields = []
    for shift_index in range(4):
        fields.append(jnp.bitwise_and(jnp.right_shift(words, 2 * shift_index), 3))
    stacked = jnp.stack(fields, axis=2)
    level_codes = stacked.reshape(words.shape[0], words.shape[1] * 4, words.shape[2])
    result = jnp.zeros(level_codes.shape, jnp.float32)
    for level_index in range(4):
        result = result + jnp.where(level_codes == level_index, levels[level_index], 0.0)
    return result

def dequantize(centroid_rows, words, levels):
    dequantized = centroid_rows.astype(jnp.float32) + unpack_levels(words, levels)
    inverse_norm = lax.rsqrt(lax.optimization_barrier(jnp.sum(dequantized * dequantized, axis=-1, keepdims=True)) + 1e-06)
    return (dequantized * inverse_norm).astype(jnp.bfloat16)

def reference(queries, centroids, candidates, token_codes, resid_words, lengths, levels):
    query_count = queries.shape[0]
    flat_queries = queries.reshape(query_count * QT, D).astype(jnp.float32)
    wide_table = centroids.astype(jnp.float32)
    block_size = min(CENT_DEV, 2048)
    block_total = centroids.shape[0] // block_size

    def block_step(block_index, running_best):
        start = (block_index * block_size).astype(jnp.int32)
        centroid_block = lax.dynamic_slice_in_dim(wide_table, start, block_size, 0)
        scores = jnp.dot(flat_queries, centroid_block.T, preferred_element_type=jnp.float32)
        return jnp.maximum(running_best, lax.optimization_barrier(jnp.max(scores, axis=1)))
    initial = jnp.full((query_count * QT,), -jnp.inf, jnp.float32)
    token_best = lax.fori_loop(0, block_total, block_step, initial).reshape(query_count, QT)
    cand_rows = candidates.reshape(query_count, NCAND)

    def one_query(inputs):
        query_tokens, cand_ids = inputs
        owners = cand_ids // PASS_DEV
        shard_index = owners // GROUPS
        global_codes = (jnp.take(token_codes, cand_ids, axis=0) + (shard_index * CENT_DEV)[:, None]).astype(jnp.int32)
        centroid_rows = jnp.take(centroids, global_codes, axis=0)
        embedded = dequantize(centroid_rows, jnp.take(resid_words, cand_ids, axis=0), levels)
        scores = jnp.einsum('qd,spd->sqp', query_tokens.astype(jnp.float32), embedded.astype(jnp.float32))
        position = lax.broadcasted_iota(jnp.int32, scores.shape, 2)
        inside = position < jnp.take(lengths, cand_ids)[:, None, None]
        maxima = lax.optimization_barrier(jnp.max(jnp.where(inside, scores, -1000000000.0), axis=2))
        return lax.optimization_barrier(jnp.sum(maxima, axis=1)) / QT
    passage_scores = lax.map(one_query, (queries, cand_rows))
    return (token_best, passage_scores.reshape(GROUPS, CSH, QRY_DEV, NCAND))
```

```python
import functools

import jax
import jax.numpy as jnp
from jax import lax
from jax.experimental import pallas as pl
from jax.experimental.pallas import tpu as pltpu
from jax.sharding import PartitionSpec as P

MASKED = -1000000000.0
LANES = 128
SUB = 8
FIELDS = 4
BLOCKS = 8
MIB = 1 << 20


def transposed_by_eye(row):
    size = row.shape[1]
    down = lax.broadcasted_iota(jnp.int32, (size, size), 0)
    across = lax.broadcasted_iota(jnp.int32, (size, size), 1)
    return jnp.sum(jnp.where(down == across, row, 0.0), axis=1, keepdims=True)


def best_kernel(owner_shift, capacity, q_ref, cand_ref, cent_ref, best_ref, target_ref, qt_ref, acc_ref):
    step = pl.program_id(0)
    rows = 512

    @pl.when(step == 0)
    def _():
        qt_ref[...] = jnp.transpose(q_ref[...].astype(jnp.float32)).astype(jnp.bfloat16)
        acc_ref[...] = jnp.full(acc_ref.shape, -jnp.inf, jnp.float32)
        owners = jnp.right_shift(cand_ref[...], owner_shift).astype(jnp.float32)
        pairs = owners.shape[1]
        earlier = lax.broadcasted_iota(jnp.int32, (pairs, pairs), 0) < lax.broadcasted_iota(
            jnp.int32, (pairs, pairs), 1
        )
        same = transposed_by_eye(owners) == owners
        slots = jnp.sum(jnp.where(same & earlier, 1.0, 0.0), axis=0, keepdims=True)
        target_ref[...] = (owners * capacity + slots).astype(jnp.int32)

    def tile(index, best):
        block = cent_ref[pl.ds(pl.multiple_of(index * rows, rows), rows), :]
        scores = jnp.dot(block, qt_ref[...], preferred_element_type=jnp.float32)
        return jnp.maximum(best, jnp.max(scores.reshape(rows // SUB, SUB, scores.shape[1]), axis=0))

    acc_ref[...] = lax.fori_loop(0, cent_ref.shape[0] // rows, tile, acc_ref[...])

    @pl.when(step == pl.num_programs(0) - 1)
    def _():
        best = jnp.max(acc_ref[...], axis=0, keepdims=True)
        width = best_ref.shape[1]
        for index in range(best_ref.shape[0]):
            best_ref[index : index + 1, :] = best[:, index * width : (index + 1) * width]


def centroid_best(queries, cand_row, centroids, pass_dev, capacity):
    group_rows, query_len, width = queries.shape
    tokens = group_rows * query_len
    cent_dev = centroids.shape[0]
    block = min(cent_dev, 4096)
    pairs = cand_row.shape[1]
    return pl.pallas_call(
        functools.partial(best_kernel, pass_dev.bit_length() - 1, capacity),
        grid=(cent_dev // block,),
        in_specs=[
            pl.BlockSpec((tokens, width), lambda i: (0, 0)),
            pl.BlockSpec((1, pairs), lambda i: (0, 0)),
            pl.BlockSpec((block, width), lambda i: (i, 0)),
        ],
        out_specs=[
            pl.BlockSpec((group_rows, query_len), lambda i: (0, 0)),
            pl.BlockSpec((1, pairs), lambda i: (0, 0)),
        ],
        out_shape=[
            jax.ShapeDtypeStruct((group_rows, query_len), jnp.float32),
            jax.ShapeDtypeStruct((1, pairs), jnp.int32),
        ],
        scratch_shapes=[
            pltpu.VMEM((width, tokens), jnp.bfloat16),
            pltpu.VMEM((SUB, tokens), jnp.float32),
        ],
        compiler_params=pltpu.CompilerParams(vmem_limit_bytes=24 * MIB),
        cost_estimate=pl.CostEstimate(
            flops=2 * tokens * cent_dev * width, bytes_accessed=2 * cent_dev * width, transcendentals=0
        ),
        name="centroid_best",
    )(queries.reshape(tokens, width), cand_row, centroids)


def score_kernel(
    sizes,
    me_ref,
    cand_ref,
    levels_ref,
    query_ref,
    cent_hbm,
    words_hbm,
    codes_hbm,
    lens_hbm,
    out_ref,
    staged,
    table,
    words,
    query_t,
    embed,
    maxima,
    ids_vmem,
    ids,
    codes,
    lens,
    work,
    work_quad,
    item_pass,
    item_len,
    item_lane,
    table_sem,
    words_sem,
    small_sem,
):
    group_count, cent_count, per_device, query_len, capacity, pass_dev, cand_count = sizes
    sources, pairs = cand_ref.shape
    items = sources * capacity
    tiles = words.shape[1] // SUB
    tile_tokens = SUB * FIELDS
    quad_sources = LANES // (per_device * query_len)
    quads = sources // quad_sources
    per_bits = per_device.bit_length() - 1
    tile_bits = tiles.bit_length() - 1
    parts = table_sem.shape[0]
    part_rows = staged.shape[0] // parts
    word_parts = words_sem.shape[0]
    part_pass = pass_dev // word_parts

    def table_copy(part):
        rows = pl.ds(part * part_rows, part_rows)
        return pltpu.make_async_copy(cent_hbm.at[rows, :], staged.at[rows, :], table_sem.at[part])

    def words_copy(part):
        rows = pl.ds(part * part_pass, part_pass)
        return pltpu.make_async_copy(words_hbm.at[rows], words.at[rows], words_sem.at[part])

    lens_copy = pltpu.make_async_copy(lens_hbm, lens, small_sem.at[0])
    codes_copy = pltpu.make_async_copy(codes_hbm, codes, small_sem.at[1])
    lens_copy.start()
    for part in range(parts):
        table_copy(part).start()
    codes_copy.start()
    for part in range(word_parts):
        words_copy(part).start()

    first = me_ref[0] * pass_dev
    local = cand_ref[...] - first
    mine = (local >= 0) & (local < pass_dev)
    earlier = lax.broadcasted_iota(jnp.int32, (pairs, pairs), 0) < lax.broadcasted_iota(
        jnp.int32, (pairs, pairs), 1
    )
    slots = jnp.dot(
        mine.astype(jnp.bfloat16), earlier.astype(jnp.bfloat16), preferred_element_type=jnp.float32
    )
    which = lax.broadcasted_iota(jnp.int32, local.shape, 1) >= cand_count
    tagged = (local * per_device + which.astype(jnp.int32) + 1).astype(jnp.float32)
    lane = lax.broadcasted_iota(jnp.int32, ids_vmem.shape, 1)
    found = jnp.zeros(ids_vmem.shape, jnp.float32)
    for slot in range(capacity):
        chosen = jnp.sum(jnp.where(mine & (slots == slot), tagged, 0.0), axis=1, keepdims=True)
        found = jnp.where(lane == slot, chosen, found)
    ids_vmem[...] = found.astype(jnp.int32)
    ids_copy = pltpu.make_async_copy(ids_vmem, ids, small_sem.at[2])
    ids_copy.start()

    def turn(quad, carry):
        block = query_ref[pl.ds(pl.multiple_of(quad * LANES, LANES), LANES), :]
        query_t[quad] = jnp.transpose(block.astype(jnp.float32)).astype(jnp.bfloat16)
        return carry

    lax.fori_loop(0, quads, turn, 0)
    maxima[...] = jnp.full(maxima.shape, MASKED, jnp.float32)
    embed[...] = jnp.zeros(embed.shape, embed.dtype)
    lens_copy.wait()
    ids_copy.wait()

    item_pass[items] = 0
    item_len[items] = 0
    item_lane[items] = -1
    spare = items * tiles

    def fill(quad, count):
        start = count
        group = quad // (cent_count // quad_sources)
        cent = (quad % (cent_count // quad_sources)) * quad_sources
        for part in range(quad_sources):
            source = (cent + part) * group_count + group
            for slot in range(capacity):
                tag = ids[source, slot] - 1
                item = source * capacity + slot
                real = tag >= 0
                held = jnp.maximum(tag, 0)
                passage = jnp.right_shift(held, per_bits)
                length = lens[passage]
                item_pass[item] = passage
                item_len[item] = length
                item_lane[item] = part * per_device + jnp.bitwise_and(held, per_device - 1)
                for tile in range(tiles):
                    work[count + tile] = item * tiles + tile
                count = count + jnp.where(real, jnp.right_shift(length + tile_tokens - 1, tile_tokens.bit_length() - 1), 0)
        for index in range(BLOCKS):
            work[count + index] = spare
        count = (count + BLOCKS - 1) // BLOCKS * BLOCKS
        for index in range(quad_sources * capacity * tiles // BLOCKS):
            work_quad[start // BLOCKS + index] = quad
        return count

    total = lax.fori_loop(0, quads, fill, 0)
    chunks = total // BLOCKS

    for part in range(parts):
        table_copy(part).wait()
        step_rows = 256

        def widen(index, carry, part=part):
            rows = pl.ds(pl.multiple_of(part * part_rows + index * step_rows, step_rows), step_rows)
            table[rows, :] = staged[rows, :].astype(jnp.float32)
            return carry

        lax.fori_loop(0, part_rows // step_rows, widen, 0)
    codes_copy.wait()
    for part in range(word_parts):
        words_copy(part).wait()

    sub = lax.broadcasted_iota(jnp.int32, (SUB, LANES), 0)
    position = jnp.concatenate([sub * FIELDS + field for field in range(FIELDS)], axis=0)
    lane_group = lax.broadcasted_iota(jnp.int32, (1, LANES), 1) // query_len
    level = [levels_ref[index : index + 1, :] for index in range(FIELDS)]

    def score(chunk):
        scores = jnp.dot(embed[...], query_t[work_quad[chunk]], preferred_element_type=jnp.float32)
        for index in range(BLOCKS):
            entry = work[chunk * BLOCKS + index]
            item, tile = jnp.right_shift(entry, tile_bits), jnp.bitwise_and(entry, tiles - 1)
            block = scores[index * tile_tokens : (index + 1) * tile_tokens]
            kept = jnp.where(position < item_len[item] - tile * tile_tokens, block, MASKED)
            best = jnp.max(kept, axis=0, keepdims=True)
            maxima[tile, pl.ds(item, 1), :] = jnp.where(lane_group == item_lane[item], best, 0.0)

    def decode(chunk):
        for index in range(BLOCKS):
            entry = work[chunk * BLOCKS + index]
            item, tile = jnp.right_shift(entry, tile_bits), jnp.bitwise_and(entry, tiles - 1)
            passage = item_pass[item]
            word = words[passage, pl.ds(pl.multiple_of(tile * SUB, SUB), SUB), :]
            dense = []
            for field in range(FIELDS):
                rows = jnp.zeros((SUB, LANES), jnp.float32)
                for row in range(SUB):
                    code = codes[passage, tile * tile_tokens + row * FIELDS + field]
                    rows = jnp.where(sub == row, table[pl.ds(code, SUB, stride=0), :], rows)
                low = jnp.bitwise_and(word, 1 << (2 * field)) != 0
                high = jnp.bitwise_and(word, 2 << (2 * field)) != 0
                residual = jnp.where(
                    high, jnp.where(low, level[3], level[2]), jnp.where(low, level[1], level[0])
                )
                dense.append(rows + residual)
            dense = jnp.concatenate(dense, axis=0)
            inverse = lax.rsqrt(jnp.sum(dense * dense, axis=1, keepdims=True) + 1e-06)
            embed[index * tile_tokens : (index + 1) * tile_tokens, :] = (dense * inverse).astype(jnp.bfloat16)

    @pl.when(chunks > 0)
    def _():
        decode(0)

        def both(chunk, carry):
            score(chunk - 1)
            decode(chunk)
            return carry

        lax.fori_loop(1, chunks, both, 0)
        score(chunks - 1)

    best = maxima[0, :items, :]
    for tile in range(1, tiles):
        best = jnp.maximum(best, maxima[tile, :items, :])
    sums = jnp.sum(best, axis=1, keepdims=True) / query_len
    width = out_ref.shape[1]
    item_down = lax.broadcasted_iota(jnp.int32, (items, width), 0)
    item_slot = lax.broadcasted_iota(jnp.int32, (items, width), 1)
    spread = jnp.where(item_down % capacity == item_slot, sums, 0.0)
    source_down = lax.broadcasted_iota(jnp.int32, (sources, items), 0)
    item_across = lax.broadcasted_iota(jnp.int32, (sources, items), 1)
    gather = (item_across // capacity == source_down).astype(jnp.float32)
    out_ref[...] = jnp.dot(
        gather, spread, precision=lax.Precision.HIGHEST, preferred_element_type=jnp.float32
    )


def owner_scores(me, cand_all, query_all, centroids, token_codes, resid_words, lengths, levels, sizes):
    capacity = sizes[4]
    sources, pairs = cand_all.shape
    cent_dev, width = centroids.shape
    pass_dev, plen = token_codes.shape
    packed = resid_words.shape[1]
    tiles = packed // SUB
    items = sources * capacity
    quads = query_all.shape[0] // LANES
    work_size = items * tiles + (quads + 1) * BLOCKS
    any_space = pl.BlockSpec(memory_space=pl.ANY)
    vmem = pl.BlockSpec(memory_space=pltpu.VMEM)
    tokens = items * plen
    return pl.pallas_call(
        functools.partial(score_kernel, sizes),
        in_specs=[pl.BlockSpec(memory_space=pltpu.SMEM), vmem, vmem, vmem] + [any_space] * 4,
        out_specs=vmem,
        out_shape=jax.ShapeDtypeStruct((sources, capacity), jnp.float32),
        scratch_shapes=[
            pltpu.VMEM((cent_dev, width), jnp.bfloat16),
            pltpu.VMEM((cent_dev + SUB, width), jnp.float32),
            pltpu.VMEM((pass_dev, packed, width), jnp.int32),
            pltpu.VMEM((quads, width, LANES), jnp.bfloat16),
            pltpu.VMEM((BLOCKS * SUB * FIELDS, width), jnp.bfloat16),
            pltpu.VMEM((tiles, items + SUB, LANES), jnp.float32),
            pltpu.VMEM((sources, LANES), jnp.int32),
            pltpu.SMEM((sources, LANES), jnp.int32),
            pltpu.SMEM((pass_dev, plen), jnp.int32),
            pltpu.SMEM((pass_dev,), jnp.int32),
            pltpu.SMEM((work_size,), jnp.int32),
            pltpu.SMEM((work_size // BLOCKS + items * tiles // quads,), jnp.int32),
            pltpu.SMEM((items + 1,), jnp.int32),
            pltpu.SMEM((items + 1,), jnp.int32),
            pltpu.SMEM((items + 1,), jnp.int32),
            pltpu.SemaphoreType.DMA((8,)),
            pltpu.SemaphoreType.DMA((4,)),
            pltpu.SemaphoreType.DMA((3,)),
        ],
        compiler_params=pltpu.CompilerParams(vmem_limit_bytes=48 * MIB),
        cost_estimate=pl.CostEstimate(
            flops=2 * tokens * width * LANES, bytes_accessed=2 * cent_dev * width * 2, transcendentals=tokens
        ),
        name="owner_scores",
    )(me, cand_all, levels, query_all, centroids, resid_words, token_codes, lengths)


def finish_kernel(best_ref, back_ref, target_ref, best_out, score_out):
    best = best_ref[0]
    for index in range(1, best_ref.shape[0]):
        best = jnp.maximum(best, best_ref[index])
    best_out[...] = best
    owners, capacity = back_ref.shape
    target = target_ref[...]
    owner = lax.broadcasted_iota(jnp.int32, (owners, target.shape[1]), 0)
    found = jnp.zeros(owner.shape, jnp.float32)
    for slot in range(capacity):
        found = found + jnp.where(owner * capacity + slot == target, back_ref[:, slot : slot + 1], 0.0)
    scores = jnp.sum(found, axis=0, keepdims=True)
    width = score_out.shape[1]
    for index in range(score_out.shape[0]):
        score_out[index : index + 1, :] = scores[:, index * width : (index + 1) * width]


def finish(best_all, back, target, per_device, cand_count):
    vmem = pl.BlockSpec(memory_space=pltpu.VMEM)
    return pl.pallas_call(
        finish_kernel,
        in_specs=[vmem] * 3,
        out_specs=[vmem] * 2,
        out_shape=[
            jax.ShapeDtypeStruct(best_all.shape[1:], jnp.float32),
            jax.ShapeDtypeStruct((per_device, cand_count), jnp.float32),
        ],
        name="finish",
    )(best_all, back, target)


def shards(queries, centroids, candidates, token_codes, resid_words, lengths, levels):
    group_rows, query_len, width = queries.shape
    pass_dev = token_codes.shape[0]
    per_device, cand_count = candidates.shape[2:]
    pair_count = per_device * cand_count
    cent_count = lax.axis_size("cent")
    group_count = lax.axis_size("grp")
    devices = cent_count * group_count
    capacity = max(2, 2 * pair_count // devices)
    sizes = (group_count, cent_count, per_device, query_len, capacity, pass_dev, cand_count)
    cand_row = candidates.reshape(1, pair_count)
    cand_all = lax.all_gather(cand_row, ("cent", "grp"), axis=0, tiled=True)
    query_all = lax.all_gather(queries, "grp", axis=0, tiled=True)
    me = (lax.axis_index("cent") * group_count + lax.axis_index("grp")).astype(jnp.int32).reshape(1)
    best, target = centroid_best(queries, cand_row, centroids, pass_dev, capacity)
    best_all = lax.all_gather(best, "cent", axis=0, tiled=False)
    query_rows = query_all.reshape(group_count * group_rows * query_len, width)
    totals = owner_scores(
        me, cand_all, query_rows, centroids, token_codes, resid_words, lengths, levels, sizes
    )
    back = lax.all_to_all(totals, ("cent", "grp"), split_axis=0, concat_axis=0, tiled=True)
    token_best, scores = finish(best_all, back, target, per_device, cand_count)
    return (token_best, scores.reshape(1, 1, per_device, cand_count))


def solution(mesh):
    placed = (
        P("grp", None, None),
        P("cent", None),
        P("grp", "cent", None, None),
        P(("cent", "grp"), None),
        P(("cent", "grp"), None, None),
        P(("cent", "grp")),
        P(),
    )
    return jax.shard_map(
        shards,
        mesh=mesh,
        in_specs=placed,
        out_specs=(P("grp", None), P("grp", "cent", None, None)),
        check_vma=False,
    )
```

```python
import functools

import jax
import jax.numpy as jnp
from jax import lax
from jax.experimental import pallas as pl
from jax.experimental.pallas import tpu as pltpu
from jax.sharding import PartitionSpec as P

MASKED = -1000000000.0
LANES = 128
SUB = 8
FIELDS = 4
BLOCKS = 16
ALIGN = 8
MIB = 1 << 20


def transposed_by_eye(row):
    size = row.shape[1]
    down = lax.broadcasted_iota(jnp.int32, (size, size), 0)
    across = lax.broadcasted_iota(jnp.int32, (size, size), 1)
    return jnp.sum(jnp.where(down == across, row, 0.0), axis=1, keepdims=True)


def one_row(rows):
    return jnp.concatenate([rows[index : index + 1, :] for index in range(rows.shape[0])], axis=1)


def send_kernel(q_ref, cand_ref, ids_ref, sent_ref):
    ids_ref[...] = jnp.broadcast_to(one_row(cand_ref[...]), ids_ref.shape)
    for index in range(sent_ref.shape[0]):
        sent_ref[index] = q_ref[...]


def send_blocks(query_rows, cand, devices, group_count):
    vmem = pl.BlockSpec(memory_space=pltpu.VMEM)
    return pl.pallas_call(
        send_kernel,
        in_specs=[vmem] * 2,
        out_specs=[vmem] * 2,
        out_shape=[
            jax.ShapeDtypeStruct((devices, cand.size), jnp.int32),
            jax.ShapeDtypeStruct((group_count,) + query_rows.shape, query_rows.dtype),
        ],
        name="send_blocks",
    )(query_rows, cand)


def best_kernel(owner_shift, capacity, q_ref, cand_ref, cent_ref, best_ref, target_ref, qt_ref, acc_ref):
    step = pl.program_id(0)
    rows = min(cent_ref.shape[0], 2048)

    @pl.when(step == 0)
    def _():
        qt_ref[...] = jnp.transpose(q_ref[...].astype(jnp.float32)).astype(jnp.bfloat16)
        acc_ref[...] = jnp.full(acc_ref.shape, -jnp.inf, jnp.float32)
        owners = jnp.right_shift(one_row(cand_ref[...]), owner_shift).astype(jnp.float32)
        pairs = owners.shape[1]
        earlier = lax.broadcasted_iota(jnp.int32, (pairs, pairs), 0) < lax.broadcasted_iota(
            jnp.int32, (pairs, pairs), 1
        )
        same = transposed_by_eye(owners) == owners
        slots = jnp.sum(jnp.where(same & earlier, 1.0, 0.0), axis=0, keepdims=True)
        target_ref[...] = (owners * capacity + slots).astype(jnp.int32)

    def tile(index, best):
        block = cent_ref[pl.ds(pl.multiple_of(index * rows, rows), rows), :]
        scores = jnp.dot(block, qt_ref[...], preferred_element_type=jnp.float32)
        return jnp.maximum(best, jnp.max(scores.reshape(rows // SUB, SUB, scores.shape[1]), axis=0))

    acc_ref[...] = lax.fori_loop(0, cent_ref.shape[0] // rows, tile, acc_ref[...])

    @pl.when(step == pl.num_programs(0) - 1)
    def _():
        best = jnp.max(acc_ref[...], axis=0, keepdims=True)
        for index in range(best_ref.shape[0]):
            best_ref[index : index + 1, :] = best[:, index * LANES : (index + 1) * LANES]


def centroid_best(query_rows, cand, centroids, pass_dev, capacity):
    tokens, width = query_rows.shape
    cent_dev = centroids.shape[0]
    block = min(cent_dev, 4096)
    pairs = cand.size
    return pl.pallas_call(
        functools.partial(best_kernel, pass_dev.bit_length() - 1, capacity),
        grid=(cent_dev // block,),
        in_specs=[
            pl.BlockSpec((tokens, width), lambda i: (0, 0)),
            pl.BlockSpec(cand.shape, lambda i: (0, 0)),
            pl.BlockSpec((block, width), lambda i: (i, 0)),
        ],
        out_specs=[
            pl.BlockSpec((tokens // LANES, LANES), lambda i: (0, 0)),
            pl.BlockSpec((1, pairs), lambda i: (0, 0)),
        ],
        out_shape=[
            jax.ShapeDtypeStruct((tokens // LANES, LANES), jnp.float32),
            jax.ShapeDtypeStruct((1, pairs), jnp.int32),
        ],
        scratch_shapes=[
            pltpu.VMEM((width, tokens), jnp.bfloat16),
            pltpu.VMEM((SUB, tokens), jnp.float32),
        ],
        compiler_params=pltpu.CompilerParams(vmem_limit_bytes=56 * MIB),
        cost_estimate=pl.CostEstimate(
            flops=2 * tokens * cent_dev * width, bytes_accessed=2 * cent_dev * width, transcendentals=0
        ),
        name="centroid_best",
    )(query_rows, cand, centroids)


def score_kernel(
    sizes,
    me_ref,
    cand_ref,
    best_ref,
    levels_ref,
    query_ref,
    cent_hbm,
    words_hbm,
    codes_hbm,
    lens_hbm,
    out_ref,
    staged,
    table,
    words,
    query_t,
    embed,
    maxima,
    ids_vmem,
    ids,
    codes,
    lens,
    work,
    work_quad,
    item_pass,
    item_len,
    item_lane,
    table_sem,
    words_sem,
    small_sem,
):
    group_count, cent_count, per_device, query_len, capacity, pass_dev, cand_count = sizes
    sources, pairs = cand_ref.shape
    items = sources * capacity
    tiles = words.shape[1] // SUB
    tile_tokens = SUB * FIELDS
    quad_sources = LANES // (per_device * query_len)
    quads = sources // quad_sources
    per_bits = per_device.bit_length() - 1
    tile_bits = tiles.bit_length() - 1
    part_rows = staged.shape[0] // quads
    word_parts = words_sem.shape[0]
    part_pass = pass_dev // word_parts

    def table_copy(part):
        rows = pl.ds(pl.multiple_of(part * part_rows, part_rows), part_rows)
        return pltpu.make_async_copy(cent_hbm.at[rows, :], staged.at[rows, :], table_sem.at[part])

    def words_copy(part):
        rows = pl.ds(part * part_pass, part_pass)
        return pltpu.make_async_copy(words_hbm.at[rows], words.at[rows], words_sem.at[part])

    def start_table(part, carry):
        table_copy(part).start()
        return carry

    lens_copy = pltpu.make_async_copy(lens_hbm, lens, small_sem.at[0])
    codes_copy = pltpu.make_async_copy(codes_hbm, codes, small_sem.at[1])
    lens_copy.start()
    lax.fori_loop(0, quads, start_table, 0)
    codes_copy.start()
    for part in range(word_parts):
        words_copy(part).start()

    first = me_ref[0] * pass_dev
    local = cand_ref[...] - first
    mine = (local >= 0) & (local < pass_dev)
    earlier = lax.broadcasted_iota(jnp.int32, (pairs, pairs), 0) < lax.broadcasted_iota(
        jnp.int32, (pairs, pairs), 1
    )
    slots = jnp.dot(
        mine.astype(jnp.bfloat16), earlier.astype(jnp.bfloat16), preferred_element_type=jnp.float32
    )
    which = lax.broadcasted_iota(jnp.int32, local.shape, 1) >= cand_count
    tagged = (local * per_device + which.astype(jnp.int32) + 1).astype(jnp.float32)
    lane = lax.broadcasted_iota(jnp.int32, ids_vmem.shape, 1)
    found = jnp.zeros(ids_vmem.shape, jnp.float32)
    for slot in range(capacity):
        chosen = jnp.sum(jnp.where(mine & (slots == slot), tagged, 0.0), axis=1, keepdims=True)
        found = jnp.where(lane == slot, chosen, found)
    ids_vmem[...] = found.astype(jnp.int32)
    ids_copy = pltpu.make_async_copy(ids_vmem, ids, small_sem.at[2])
    ids_copy.start()

    maxima[...] = jnp.full(maxima.shape, MASKED, jnp.float32)
    embed[...] = jnp.zeros(embed.shape, embed.dtype)
    lens_copy.wait()
    ids_copy.wait()

    item_pass[items] = 0
    item_len[items] = 0
    item_lane[items] = -1
    spare = items * tiles

    def prepare(quad, count):
        table_copy(quad).wait()
        rows = pl.ds(pl.multiple_of(quad * part_rows, part_rows), part_rows)
        table[rows, :] = staged[rows, :].astype(jnp.float32)
        block = query_ref[pl.ds(pl.multiple_of(quad * LANES, LANES), LANES), :]
        query_t[quad] = jnp.transpose(block.astype(jnp.float32)).astype(jnp.bfloat16)
        start = count
        group = quad // (cent_count // quad_sources)
        cent = (quad % (cent_count // quad_sources)) * quad_sources
        for part in range(quad_sources):
            source = (cent + part) * group_count + group
            for slot in range(capacity):
                tag = ids[source, slot] - 1
                item = source * capacity + slot
                real = tag >= 0
                held = jnp.maximum(tag, 0)
                passage = jnp.right_shift(held, per_bits)
                length = lens[passage]
                item_pass[item] = passage
                item_len[item] = length
                item_lane[item] = part * per_device + jnp.bitwise_and(held, per_device - 1)
                for tile in range(tiles):
                    work[count + tile] = item * tiles + tile
                count = count + jnp.where(real, jnp.right_shift(length + tile_tokens - 1, tile_tokens.bit_length() - 1), 0)
        for index in range(ALIGN):
            work[count + index] = spare
        count = (count + ALIGN - 1) // ALIGN * ALIGN
        for index in range(quad_sources * capacity * tiles // ALIGN):
            work_quad[start // ALIGN + index] = quad
        return count

    total = lax.fori_loop(0, quads, prepare, 0)
    for index in range(BLOCKS):
        work[total + index] = spare
    for index in range(BLOCKS // ALIGN):
        work_quad[total // ALIGN + index] = 0
    chunks = (total + BLOCKS - 1) // BLOCKS
    codes_copy.wait()
    for part in range(word_parts):
        words_copy(part).wait()

    sub = lax.broadcasted_iota(jnp.int32, (SUB, LANES), 0)
    position = jnp.concatenate([sub * FIELDS + field for field in range(FIELDS)], axis=0)
    lane_group = lax.broadcasted_iota(jnp.int32, (1, LANES), 1) // query_len
    level = [levels_ref[index : index + 1, :] for index in range(FIELDS)]

    def score(chunk):
        scores = []
        for part in range(BLOCKS // ALIGN):
            rows = embed[part * ALIGN * tile_tokens : (part + 1) * ALIGN * tile_tokens, :]
            quad = work_quad[chunk * (BLOCKS // ALIGN) + part]
            scores.append(jnp.dot(rows, query_t[quad], preferred_element_type=jnp.float32))
        for index in range(BLOCKS):
            entry = work[chunk * BLOCKS + index]
            item, tile = jnp.right_shift(entry, tile_bits), jnp.bitwise_and(entry, tiles - 1)
            inner = index % ALIGN
            block = scores[index // ALIGN][inner * tile_tokens : (inner + 1) * tile_tokens]
            kept = jnp.where(position < item_len[item] - tile * tile_tokens, block, MASKED)
            best = jnp.max(kept, axis=0, keepdims=True)
            maxima[tile, pl.ds(item, 1), :] = jnp.where(lane_group == item_lane[item], best, 0.0)

    def decode(chunk):
        for index in range(BLOCKS):
            entry = work[chunk * BLOCKS + index]
            item, tile = jnp.right_shift(entry, tile_bits), jnp.bitwise_and(entry, tiles - 1)
            passage = item_pass[item]
            word = words[passage, pl.ds(pl.multiple_of(tile * SUB, SUB), SUB), :]
            dense = []
            start = passage * (tiles * tile_tokens) + tile * tile_tokens
            for field in range(FIELDS):
                rows = jnp.zeros((SUB, LANES), jnp.float32)
                for row in range(SUB):
                    code = codes[start + (row * FIELDS + field)]
                    rows = jnp.where(sub == row, table[pl.ds(code, SUB, stride=0), :], rows)
                low = jnp.bitwise_and(word, 1 << (2 * field)) != 0
                high = jnp.bitwise_and(word, 2 << (2 * field)) != 0
                residual = jnp.where(
                    high, jnp.where(low, level[3], level[2]), jnp.where(low, level[1], level[0])
                )
                dense.append(rows + residual)
            dense = jnp.concatenate(dense, axis=0)
            inverse = lax.rsqrt(jnp.sum(dense * dense, axis=1, keepdims=True) + 1e-06)
            embed[index * tile_tokens : (index + 1) * tile_tokens, :] = (dense * inverse).astype(jnp.bfloat16)

    @pl.when(chunks > 0)
    def _():
        decode(0)

        def both(chunk, carry):
            score(chunk - 1)
            decode(chunk)
            return carry

        lax.fori_loop(1, chunks, both, 0)
        score(chunks - 1)

    best = maxima[0, :items, :]
    for tile in range(1, tiles):
        best = jnp.maximum(best, maxima[tile, :items, :])
    sums = jnp.sum(best, axis=1, keepdims=True) / query_len
    item_down = lax.broadcasted_iota(jnp.int32, (items, LANES), 0)
    item_slot = lax.broadcasted_iota(jnp.int32, (items, LANES), 1)
    spread = jnp.where(item_down % capacity == item_slot, sums, 0.0)
    source_down = lax.broadcasted_iota(jnp.int32, (sources, items), 0)
    item_across = lax.broadcasted_iota(jnp.int32, (sources, items), 1)
    gather = (item_across // capacity == source_down).astype(jnp.float32)
    by_source = jnp.dot(
        gather, spread, precision=lax.Precision.HIGHEST, preferred_element_type=jnp.float32
    )
    rows_best = best_ref.shape[0]
    for source in range(sources):
        out_ref[source, :rows_best, :] = best_ref[...]
        out_ref[source, rows_best : rows_best + 1, :] = by_source[source : source + 1, :]


def owner_scores(me, cand_all, best, query_all, centroids, token_codes, resid_words, lengths, levels, sizes):
    capacity = sizes[4]
    sources, pairs = cand_all.shape
    cent_dev, width = centroids.shape
    pass_dev, plen = token_codes.shape
    packed = resid_words.shape[1]
    tiles = packed // SUB
    items = sources * capacity
    quads = query_all.shape[0] // LANES
    work_size = items * tiles + quads * ALIGN + BLOCKS
    reply_rows = (best.shape[0] + SUB) // SUB * SUB
    any_space = pl.BlockSpec(memory_space=pl.ANY)
    vmem = pl.BlockSpec(memory_space=pltpu.VMEM)
    tokens = items * plen
    return pl.pallas_call(
        functools.partial(score_kernel, sizes),
        in_specs=[pl.BlockSpec(memory_space=pltpu.SMEM), vmem, vmem, vmem, vmem] + [any_space] * 4,
        out_specs=vmem,
        out_shape=jax.ShapeDtypeStruct((sources, reply_rows, LANES), jnp.float32),
        scratch_shapes=[
            pltpu.VMEM((cent_dev, width), jnp.bfloat16),
            pltpu.VMEM((cent_dev + SUB, width), jnp.float32),
            pltpu.VMEM((pass_dev, packed, width), jnp.int32),
            pltpu.VMEM((quads, width, LANES), jnp.bfloat16),
            pltpu.VMEM((BLOCKS * SUB * FIELDS, width), jnp.bfloat16),
            pltpu.VMEM((tiles, items + SUB, LANES), jnp.float32),
            pltpu.VMEM((sources, LANES), jnp.int32),
            pltpu.SMEM((sources, LANES), jnp.int32),
            pltpu.SMEM((pass_dev * plen,), jnp.int32),
            pltpu.SMEM((pass_dev,), jnp.int32),
            pltpu.SMEM((work_size,), jnp.int32),
            pltpu.SMEM((work_size // ALIGN + items * tiles // quads,), jnp.int32),
            pltpu.SMEM((items + 1,), jnp.int32),
            pltpu.SMEM((items + 1,), jnp.int32),
            pltpu.SMEM((items + 1,), jnp.int32),
            pltpu.SemaphoreType.DMA((quads,)),
            pltpu.SemaphoreType.DMA((4,)),
            pltpu.SemaphoreType.DMA((3,)),
        ],
        compiler_params=pltpu.CompilerParams(vmem_limit_bytes=56 * MIB),
        cost_estimate=pl.CostEstimate(
            flops=2 * tokens * width * LANES, bytes_accessed=2 * cent_dev * width * 2, transcendentals=tokens
        ),
        name="owner_scores",
    )(me, cand_all, best, levels, query_all, centroids, resid_words, token_codes.reshape(pass_dev * plen), lengths)


def finish_kernel(sizes, me_ref, back_ref, target_ref, best_out, score_out):
    group_count, cent_count, _, query_len, capacity, _, _ = sizes
    group = jnp.bitwise_and(me_ref[0], group_count - 1)
    rows_best = best_out.shape[0] * query_len // LANES
    best = back_ref[group, :rows_best, :]
    for cent in range(1, cent_count):
        best = jnp.maximum(best, back_ref[cent * group_count + group, :rows_best, :])
    for index in range(best_out.shape[0]):
        row, lane = divmod(index * query_len, LANES)
        best_out[index : index + 1, :] = best[row : row + 1, lane : lane + query_len]
    back = back_ref[...]
    row = lax.broadcasted_iota(jnp.int32, back.shape, 1)
    back = jnp.sum(jnp.where(row == rows_best, back, 0.0), axis=1)
    target = target_ref[...]
    owner = lax.broadcasted_iota(jnp.int32, (back.shape[0], target.shape[1]), 0)
    found = jnp.zeros(owner.shape, jnp.float32)
    for slot in range(capacity):
        found = found + jnp.where(owner * capacity + slot == target, back[:, slot : slot + 1], 0.0)
    scores = jnp.sum(found, axis=0, keepdims=True)
    width = score_out.shape[1]
    for index in range(score_out.shape[0]):
        score_out[index : index + 1, :] = scores[:, index * width : (index + 1) * width]


def finish(me, back, target, group_rows, sizes):
    _, _, per_device, query_len, _, _, cand_count = sizes
    vmem = pl.BlockSpec(memory_space=pltpu.VMEM)
    return pl.pallas_call(
        functools.partial(finish_kernel, sizes),
        in_specs=[pl.BlockSpec(memory_space=pltpu.SMEM), vmem, vmem],
        out_specs=[vmem] * 2,
        out_shape=[
            jax.ShapeDtypeStruct((group_rows, query_len), jnp.float32),
            jax.ShapeDtypeStruct((per_device, cand_count), jnp.float32),
        ],
        name="finish",
    )(me, back, target)


def shards(queries, centroids, candidates, token_codes, resid_words, lengths, levels):
    group_rows, query_len, width = queries.shape
    pass_dev = token_codes.shape[0]
    per_device, cand_count = candidates.shape[2:]
    pair_count = per_device * cand_count
    cent_count = lax.axis_size("cent")
    group_count = lax.axis_size("grp")
    devices = cent_count * group_count
    capacity = max(2, 2 * pair_count // devices)
    sizes = (group_count, cent_count, per_device, query_len, capacity, pass_dev, cand_count)
    cand = candidates.reshape(per_device, cand_count)
    query_rows = queries.reshape(group_rows * query_len, width)
    me = (lax.axis_index("cent") * group_count + lax.axis_index("grp")).astype(jnp.int32).reshape(1)
    ids_sent, rows_sent = send_blocks(query_rows, cand, devices, group_count)
    cand_all = lax.all_to_all(ids_sent, ("cent", "grp"), split_axis=0, concat_axis=0, tiled=True)
    query_all = lax.all_to_all(rows_sent, "grp", split_axis=0, concat_axis=0, tiled=True)
    best, target = centroid_best(query_rows, cand, centroids, pass_dev, capacity)
    query_all = query_all.reshape(group_count * group_rows * query_len, width)
    reply = owner_scores(
        me, cand_all, best, query_all, centroids, token_codes, resid_words, lengths, levels, sizes
    )
    back = lax.all_to_all(reply, ("cent", "grp"), split_axis=0, concat_axis=0, tiled=True)
    token_best, scores = finish(me, back, target, group_rows, sizes)
    return (token_best, scores.reshape(1, 1, per_device, cand_count))


def solution(mesh):
    placed = (
        P("grp", None, None),
        P("cent", None),
        P("grp", "cent", None, None),
        P(("cent", "grp"), None),
        P(("cent", "grp"), None, None),
        P(("cent", "grp")),
        P(),
    )
    return jax.shard_map(
        shards,
        mesh=mesh,
        in_specs=placed,
        out_specs=(P("grp", None), P("grp", "cent", None, None)),
        check_vma=False,
    )
```

```python
import functools

import jax
import jax.numpy as jnp
from jax import lax
from jax.experimental import pallas as pl
from jax.experimental.pallas import tpu as pltpu
from jax.sharding import PartitionSpec as P

MASKED = -1000000000.0
LANES = 128
SUB = 8
FIELDS = 4
BLOCKS = 16
ALIGN = 8
DIGITS = 3
DIGIT_ROWS = 16
MIB = 1 << 20


def transposed_by_eye(row):
    size = row.shape[1]
    down = lax.broadcasted_iota(jnp.int32, (size, size), 0)
    across = lax.broadcasted_iota(jnp.int32, (size, size), 1)
    return jnp.sum(jnp.where(down == across, row, 0.0), axis=1, keepdims=True)


def one_row(rows):
    return jnp.concatenate([rows[index : index + 1, :] for index in range(rows.shape[0])], axis=1)


def send_kernel(group_bits, me_ref, q_ref, cand_ref, sent_ref):
    own_rows = sent_ref.shape[1] - DIGIT_ROWS
    start = jnp.right_shift(me_ref[0], group_bits) * own_rows
    rows = q_ref[pl.ds(pl.multiple_of(start, own_rows), own_rows), :]
    ids = one_row(cand_ref[...])
    digits = [jnp.bitwise_and(jnp.right_shift(ids, 8 * index), 255) for index in range(DIGITS)]
    digits.append(jnp.zeros((DIGIT_ROWS - DIGITS, ids.shape[1]), jnp.int32))
    digits = jnp.concatenate(digits, axis=0).astype(jnp.float32).astype(jnp.bfloat16)
    for index in range(sent_ref.shape[0]):
        sent_ref[index, :own_rows, :] = rows
        sent_ref[index, own_rows:, :] = digits


def send_blocks(me, query_rows, cand, devices, own_rows, group_count):
    width = query_rows.shape[1]
    vmem = pl.BlockSpec(memory_space=pltpu.VMEM)
    return pl.pallas_call(
        functools.partial(send_kernel, group_count.bit_length() - 1),
        in_specs=[pl.BlockSpec(memory_space=pltpu.SMEM), vmem, vmem],
        out_specs=vmem,
        out_shape=jax.ShapeDtypeStruct((devices, own_rows + DIGIT_ROWS, width), jnp.bfloat16),
        name="send_blocks",
    )(me, query_rows, cand)


def best_kernel(owner_shift, capacity, q_ref, cand_ref, cent_ref, best_ref, target_ref, qt_ref, acc_ref):
    step = pl.program_id(0)
    rows = min(cent_ref.shape[0], 4096)

    @pl.when(step == 0)
    def _():
        qt_ref[...] = jnp.transpose(q_ref[...].astype(jnp.float32)).astype(jnp.bfloat16)
        acc_ref[...] = jnp.full(acc_ref.shape, -jnp.inf, jnp.float32)
        owners = jnp.right_shift(one_row(cand_ref[...]), owner_shift).astype(jnp.float32)
        pairs = owners.shape[1]
        earlier = lax.broadcasted_iota(jnp.int32, (pairs, pairs), 0) < lax.broadcasted_iota(
            jnp.int32, (pairs, pairs), 1
        )
        same = transposed_by_eye(owners) == owners
        slots = jnp.sum(jnp.where(same & earlier, 1.0, 0.0), axis=0, keepdims=True)
        target_ref[...] = (owners * capacity + slots).astype(jnp.int32)

    def tile(index, best):
        block = cent_ref[pl.ds(pl.multiple_of(index * rows, rows), rows), :]
        scores = jnp.dot(block, qt_ref[...], preferred_element_type=jnp.float32)
        return jnp.maximum(best, jnp.max(scores.reshape(rows // SUB, SUB, scores.shape[1]), axis=0))

    acc_ref[...] = lax.fori_loop(0, cent_ref.shape[0] // rows, tile, acc_ref[...])

    @pl.when(step == pl.num_programs(0) - 1)
    def _():
        best = jnp.max(acc_ref[...], axis=0, keepdims=True)
        for index in range(best_ref.shape[0]):
            best_ref[index : index + 1, :] = best[:, index * LANES : (index + 1) * LANES]


def centroid_best(query_rows, cand, centroids, pass_dev, capacity):
    tokens, width = query_rows.shape
    cent_dev = centroids.shape[0]
    block = min(cent_dev, 4096)
    pairs = cand.size
    return pl.pallas_call(
        functools.partial(best_kernel, pass_dev.bit_length() - 1, capacity),
        grid=(cent_dev // block,),
        in_specs=[
            pl.BlockSpec((tokens, width), lambda i: (0, 0)),
            pl.BlockSpec(cand.shape, lambda i: (0, 0)),
            pl.BlockSpec((block, width), lambda i: (i, 0)),
        ],
        out_specs=[
            pl.BlockSpec((tokens // LANES, LANES), lambda i: (0, 0)),
            pl.BlockSpec((1, pairs), lambda i: (0, 0)),
        ],
        out_shape=[
            jax.ShapeDtypeStruct((tokens // LANES, LANES), jnp.float32),
            jax.ShapeDtypeStruct((1, pairs), jnp.int32),
        ],
        scratch_shapes=[
            pltpu.VMEM((width, tokens), jnp.bfloat16),
            pltpu.VMEM((SUB, tokens), jnp.float32),
        ],
        compiler_params=pltpu.CompilerParams(vmem_limit_bytes=56 * MIB),
        cost_estimate=pl.CostEstimate(
            flops=2 * tokens * cent_dev * width, bytes_accessed=2 * cent_dev * width, transcendentals=0
        ),
        name="centroid_best",
    )(query_rows, cand, centroids)


def score_kernel(
    sizes,
    me_ref,
    sent_ref,
    best_ref,
    levels_ref,
    cent_hbm,
    words_hbm,
    codes_hbm,
    lens_hbm,
    out_ref,
    staged,
    table,
    words,
    query_t,
    dense,
    embed,
    maxima,
    ids_vmem,
    ids,
    codes,
    lens,
    work,
    work_quad,
    item_pass,
    item_len,
    item_lane,
    table_sem,
    words_sem,
    small_sem,
):
    group_count, cent_count, per_device, query_len, capacity, pass_dev, cand_count = sizes
    sources, sent_rows, pairs = sent_ref.shape
    own_rows = sent_rows - DIGIT_ROWS
    items = sources * capacity
    tiles = words.shape[1] // SUB
    tile_tokens = SUB * FIELDS
    quad_sources = LANES // (per_device * query_len)
    quads = sources // quad_sources
    per_bits = per_device.bit_length() - 1
    tile_bits = tiles.bit_length() - 1
    part_rows = staged.shape[0] // quads
    word_parts = words_sem.shape[0]
    part_pass = pass_dev // word_parts

    def table_copy(part):
        rows = pl.ds(pl.multiple_of(part * part_rows, part_rows), part_rows)
        return pltpu.make_async_copy(cent_hbm.at[rows, :], staged.at[rows, :], table_sem.at[part])

    def words_copy(part):
        rows = pl.ds(part * part_pass, part_pass)
        return pltpu.make_async_copy(words_hbm.at[rows], words.at[rows], words_sem.at[part])

    def start_table(part, carry):
        table_copy(part).start()
        return carry

    lens_copy = pltpu.make_async_copy(lens_hbm, lens, small_sem.at[0])
    codes_copy = pltpu.make_async_copy(codes_hbm, codes, small_sem.at[1])
    lens_copy.start()
    lax.fori_loop(0, quads, start_table, 0)
    codes_copy.start()
    for part in range(word_parts):
        words_copy(part).start()

    digits = sent_ref[:, own_rows:, :].astype(jnp.float32)
    place = lax.broadcasted_iota(jnp.int32, digits.shape, 1)
    scale = jnp.where(place < DIGITS, jnp.left_shift(1, 8 * jnp.minimum(place, DIGITS - 1)), 0)
    first = me_ref[0] * pass_dev
    local = jnp.sum(digits * scale.astype(jnp.float32), axis=1).astype(jnp.int32) - first
    mine = (local >= 0) & (local < pass_dev)
    earlier = lax.broadcasted_iota(jnp.int32, (pairs, pairs), 0) < lax.broadcasted_iota(
        jnp.int32, (pairs, pairs), 1
    )
    slots = jnp.dot(
        mine.astype(jnp.bfloat16), earlier.astype(jnp.bfloat16), preferred_element_type=jnp.float32
    )
    which = lax.broadcasted_iota(jnp.int32, local.shape, 1) >= cand_count
    tagged = (local * per_device + which.astype(jnp.int32) + 1).astype(jnp.float32)
    lane = lax.broadcasted_iota(jnp.int32, ids_vmem.shape, 1)
    found = jnp.zeros(ids_vmem.shape, jnp.float32)
    for slot in range(capacity):
        chosen = jnp.sum(jnp.where(mine & (slots == slot), tagged, 0.0), axis=1, keepdims=True)
        found = jnp.where(lane == slot, chosen, found)
    ids_vmem[...] = found.astype(jnp.int32)
    ids_copy = pltpu.make_async_copy(ids_vmem, ids, small_sem.at[2])
    ids_copy.start()

    maxima[...] = jnp.full(maxima.shape, MASKED, jnp.float32)
    lens_copy.wait()
    ids_copy.wait()

    item_pass[items] = 0
    item_len[items] = 0
    item_lane[items] = -1
    spare = items * tiles

    def prepare(quad, count):
        table_copy(quad).wait()
        rows = pl.ds(pl.multiple_of(quad * part_rows, part_rows), part_rows)
        table[rows, :] = staged[rows, :].astype(jnp.float32)
        block = [sent_ref[quad * quad_sources + part, :own_rows, :] for part in range(quad_sources)]
        block = jnp.concatenate(block, axis=0).astype(jnp.float32)
        query_t[quad] = jnp.transpose(block).astype(jnp.bfloat16)
        start = count
        for part in range(quad_sources):
            source = quad * quad_sources + part
            for slot in range(capacity):
                tag = ids[source, slot] - 1
                item = source * capacity + slot
                real = tag >= 0
                held = jnp.maximum(tag, 0)
                passage = jnp.right_shift(held, per_bits)
                length = lens[passage]
                item_pass[item] = passage
                item_len[item] = length
                item_lane[item] = part * per_device + jnp.bitwise_and(held, per_device - 1)
                for tile in range(tiles):
                    work[count + tile] = item * tiles + tile
                count = count + jnp.where(real, jnp.right_shift(length + tile_tokens - 1, tile_tokens.bit_length() - 1), 0)
        for index in range(ALIGN):
            work[count + index] = spare
        count = (count + ALIGN - 1) // ALIGN * ALIGN
        for index in range(quad_sources * capacity * tiles // ALIGN):
            work_quad[start // ALIGN + index] = quad
        return count

    total = lax.fori_loop(0, quads, prepare, 0)
    for index in range(2 * BLOCKS):
        work[total + index] = spare
    for index in range(2 * BLOCKS // ALIGN):
        work_quad[total // ALIGN + index] = 0
    chunks = jnp.maximum((total + BLOCKS - 1) // BLOCKS, 2)
    codes_copy.wait()
    for part in range(word_parts):
        words_copy(part).wait()

    sub = lax.broadcasted_iota(jnp.int32, (SUB, LANES), 0)
    position = jnp.concatenate([sub * FIELDS + field for field in range(FIELDS)], axis=0)
    lane_group = lax.broadcasted_iota(jnp.int32, (1, LANES), 1) // query_len
    level = [levels_ref[index : index + 1, :] for index in range(FIELDS)]

    def score(chunk):
        scores = []
        for part in range(BLOCKS // ALIGN):
            rows = embed[part * ALIGN * tile_tokens : (part + 1) * ALIGN * tile_tokens, :]
            quad = work_quad[chunk * (BLOCKS // ALIGN) + part]
            scores.append(jnp.dot(rows, query_t[quad], preferred_element_type=jnp.float32))
        for index in range(BLOCKS):
            entry = work[chunk * BLOCKS + index]
            item, tile = jnp.right_shift(entry, tile_bits), jnp.bitwise_and(entry, tiles - 1)
            inner = index % ALIGN
            block = scores[index // ALIGN][inner * tile_tokens : (inner + 1) * tile_tokens]
            kept = jnp.where(position < item_len[item] - tile * tile_tokens, block, MASKED)
            best = jnp.max(kept, axis=0, keepdims=True)
            maxima[tile, pl.ds(item, 1), :] = jnp.where(lane_group == item_lane[item], best, 0.0)

    def decode(chunk):
        for index in range(BLOCKS):
            entry = work[chunk * BLOCKS + index]
            item, tile = jnp.right_shift(entry, tile_bits), jnp.bitwise_and(entry, tiles - 1)
            passage = item_pass[item]
            start = passage * (tiles * tile_tokens) + tile * tile_tokens
            word = words[passage, pl.ds(pl.multiple_of(tile * SUB, SUB), SUB), :]
            for field in range(FIELDS):
                rows = jnp.zeros((SUB, LANES), jnp.float32)
                for row in range(SUB):
                    code = codes[start + (row * FIELDS + field)]
                    rows = jnp.where(sub == row, table[pl.ds(code, SUB, stride=0), :], rows)
                low = jnp.bitwise_and(word, 1 << (2 * field)) != 0
                high = jnp.bitwise_and(word, 2 << (2 * field)) != 0
                residual = jnp.where(
                    high, jnp.where(low, level[3], level[2]), jnp.where(low, level[1], level[0])
                )
                base = index * tile_tokens + field * SUB
                dense[base : base + SUB, :] = rows + residual

    def normalize():
        for index in range(BLOCKS):
            rows = slice(index * tile_tokens, (index + 1) * tile_tokens)
            block = dense[rows, :]
            inverse = lax.rsqrt(jnp.sum(block * block, axis=1, keepdims=True) + 1e-06)
            embed[rows, :] = (block * inverse).astype(jnp.bfloat16)

    decode(0)
    normalize()
    decode(1)

    def step(chunk, carry):
        score(chunk - 2)
        normalize()
        decode(chunk)
        return carry

    lax.fori_loop(2, chunks, step, 0)
    score(chunks - 2)
    normalize()
    score(chunks - 1)

    best = maxima[0, :items, :]
    for tile in range(1, tiles):
        best = jnp.maximum(best, maxima[tile, :items, :])
    sums = jnp.sum(best, axis=1, keepdims=True) / query_len
    item_down = lax.broadcasted_iota(jnp.int32, (items, LANES), 0)
    item_slot = lax.broadcasted_iota(jnp.int32, (items, LANES), 1)
    spread = jnp.where(item_down % capacity == item_slot, sums, 0.0)
    source_down = lax.broadcasted_iota(jnp.int32, (sources, items), 0)
    item_across = lax.broadcasted_iota(jnp.int32, (sources, items), 1)
    gather = (item_across // capacity == source_down).astype(jnp.float32)
    by_source = jnp.dot(
        gather, spread, precision=lax.Precision.HIGHEST, preferred_element_type=jnp.float32
    )
    rows_best = best_ref.shape[0]
    for source in range(sources):
        out_ref[source, :rows_best, :] = best_ref[...]
        out_ref[source, rows_best : rows_best + 1, :] = by_source[source : source + 1, :]


def owner_scores(me, sent, best, centroids, token_codes, resid_words, lengths, levels, sizes):
    capacity = sizes[4]
    sources, sent_rows, _ = sent.shape
    cent_dev, width = centroids.shape
    pass_dev, plen = token_codes.shape
    packed = resid_words.shape[1]
    tiles = packed // SUB
    items = sources * capacity
    quads = sources * (sent_rows - DIGIT_ROWS) // LANES
    work_size = items * tiles + quads * ALIGN + 2 * BLOCKS
    reply_rows = (best.shape[0] + SUB) // SUB * SUB
    any_space = pl.BlockSpec(memory_space=pl.ANY)
    vmem = pl.BlockSpec(memory_space=pltpu.VMEM)
    tokens = items * plen
    return pl.pallas_call(
        functools.partial(score_kernel, sizes),
        in_specs=[pl.BlockSpec(memory_space=pltpu.SMEM), vmem, vmem, vmem] + [any_space] * 4,
        out_specs=vmem,
        out_shape=jax.ShapeDtypeStruct((sources, reply_rows, LANES), jnp.float32),
        scratch_shapes=[
            pltpu.VMEM((cent_dev, width), jnp.bfloat16),
            pltpu.VMEM((cent_dev + SUB, width), jnp.float32),
            pltpu.VMEM((pass_dev, packed, width), jnp.int32),
            pltpu.VMEM((quads, width, LANES), jnp.bfloat16),
            pltpu.VMEM((BLOCKS * SUB * FIELDS, width), jnp.float32),
            pltpu.VMEM((BLOCKS * SUB * FIELDS, width), jnp.bfloat16),
            pltpu.VMEM((tiles, items + SUB, LANES), jnp.float32),
            pltpu.VMEM((sources, LANES), jnp.int32),
            pltpu.SMEM((sources, LANES), jnp.int32),
            pltpu.SMEM((pass_dev * plen,), jnp.int32),
            pltpu.SMEM((pass_dev,), jnp.int32),
            pltpu.SMEM((work_size,), jnp.int32),
            pltpu.SMEM((work_size // ALIGN + items * tiles // quads,), jnp.int32),
            pltpu.SMEM((items + 1,), jnp.int32),
            pltpu.SMEM((items + 1,), jnp.int32),
            pltpu.SMEM((items + 1,), jnp.int32),
            pltpu.SemaphoreType.DMA((quads,)),
            pltpu.SemaphoreType.DMA((4,)),
            pltpu.SemaphoreType.DMA((3,)),
        ],
        compiler_params=pltpu.CompilerParams(vmem_limit_bytes=56 * MIB),
        cost_estimate=pl.CostEstimate(
            flops=2 * tokens * width * LANES, bytes_accessed=2 * cent_dev * width * 2, transcendentals=tokens
        ),
        name="owner_scores",
    )(me, sent, best, levels, centroids, resid_words, token_codes.reshape(pass_dev * plen), lengths)


def finish_kernel(sizes, me_ref, back_ref, target_ref, best_out, score_out):
    group_count, cent_count, _, query_len, capacity, _, _ = sizes
    group = jnp.bitwise_and(me_ref[0], group_count - 1)
    rows_best = best_out.shape[0] * query_len // LANES
    best = back_ref[group, :rows_best, :]
    for cent in range(1, cent_count):
        best = jnp.maximum(best, back_ref[cent * group_count + group, :rows_best, :])
    for index in range(best_out.shape[0]):
        row, lane = divmod(index * query_len, LANES)
        best_out[index : index + 1, :] = best[row : row + 1, lane : lane + query_len]
    back = back_ref[...]
    row = lax.broadcasted_iota(jnp.int32, back.shape, 1)
    back = jnp.sum(jnp.where(row == rows_best, back, 0.0), axis=1)
    target = target_ref[...]
    owner = lax.broadcasted_iota(jnp.int32, (back.shape[0], target.shape[1]), 0)
    found = jnp.zeros(owner.shape, jnp.float32)
    for slot in range(capacity):
        found = found + jnp.where(owner * capacity + slot == target, back[:, slot : slot + 1], 0.0)
    scores = jnp.sum(found, axis=0, keepdims=True)
    width = score_out.shape[1]
    for index in range(score_out.shape[0]):
        score_out[index : index + 1, :] = scores[:, index * width : (index + 1) * width]


def finish(me, back, target, group_rows, sizes):
    _, _, per_device, query_len, _, _, cand_count = sizes
    vmem = pl.BlockSpec(memory_space=pltpu.VMEM)
    return pl.pallas_call(
        functools.partial(finish_kernel, sizes),
        in_specs=[pl.BlockSpec(memory_space=pltpu.SMEM), vmem, vmem],
        out_specs=[vmem] * 2,
        out_shape=[
            jax.ShapeDtypeStruct((group_rows, query_len), jnp.float32),
            jax.ShapeDtypeStruct((per_device, cand_count), jnp.float32),
        ],
        name="finish",
    )(me, back, target)


def shards(queries, centroids, candidates, token_codes, resid_words, lengths, levels):
    group_rows, query_len, width = queries.shape
    pass_dev = token_codes.shape[0]
    per_device, cand_count = candidates.shape[2:]
    pair_count = per_device * cand_count
    cent_count = lax.axis_size("cent")
    group_count = lax.axis_size("grp")
    devices = cent_count * group_count
    capacity = max(2, 2 * pair_count // devices)
    sizes = (group_count, cent_count, per_device, query_len, capacity, pass_dev, cand_count)
    cand = candidates.reshape(per_device, cand_count)
    query_rows = queries.reshape(group_rows * query_len, width)
    me = (lax.axis_index("cent") * group_count + lax.axis_index("grp")).astype(jnp.int32).reshape(1)
    own_rows = per_device * query_len
    sent = send_blocks(me, query_rows, cand, devices, own_rows, group_count)
    sent = lax.all_to_all(sent, ("cent", "grp"), split_axis=0, concat_axis=0, tiled=True)
    best, target = centroid_best(query_rows, cand, centroids, pass_dev, capacity)
    reply = owner_scores(
        me, sent, best, centroids, token_codes, resid_words, lengths, levels, sizes
    )
    back = lax.all_to_all(reply, ("cent", "grp"), split_axis=0, concat_axis=0, tiled=True)
    token_best, scores = finish(me, back, target, group_rows, sizes)
    return (token_best, scores.reshape(1, 1, per_device, cand_count))


def solution(mesh):
    placed = (
        P("grp", None, None),
        P("cent", None),
        P("grp", "cent", None, None),
        P(("cent", "grp"), None),
        P(("cent", "grp"), None, None),
        P(("cent", "grp")),
        P(),
    )
    return jax.shard_map(
        shards,
        mesh=mesh,
        in_specs=placed,
        out_specs=(P("grp", None), P("grp", "cent", None, None)),
        check_vma=False,
    )
```

```python
import functools

import jax
import jax.numpy as jnp
from jax import lax
from jax.experimental import pallas as pl
from jax.experimental.pallas import tpu as pltpu
from jax.sharding import PartitionSpec as P

MASKED = -1000000000.0
LANES = 128
SUB = 8
FIELDS = 4
BLOCKS = 16
ALIGN = 8
PARTS = 8
MIB = 1 << 20


def transposed_by_eye(row):
    size = row.shape[1]
    down = lax.broadcasted_iota(jnp.int32, (size, size), 0)
    across = lax.broadcasted_iota(jnp.int32, (size, size), 1)
    return jnp.sum(jnp.where(down == across, row, 0.0), axis=1, keepdims=True)


def one_row(rows):
    return jnp.concatenate([rows[index : index + 1, :] for index in range(rows.shape[0])], axis=1)


def best_kernel(owner_shift, capacity, q_ref, cand_ref, cent_hbm, best_ref, target_ref, staged, sems):
    rows = staged.shape[0] // PARTS

    def table_copy(part):
        piece = pl.ds(pl.multiple_of(part * rows, rows), rows)
        return pltpu.make_async_copy(cent_hbm.at[piece, :], staged.at[piece, :], sems.at[part])

    for part in range(PARTS):
        table_copy(part).start()
    query_t = jnp.transpose(q_ref[...].astype(jnp.float32)).astype(jnp.bfloat16)
    owners = jnp.right_shift(one_row(cand_ref[...]), owner_shift).astype(jnp.float32)
    pairs = owners.shape[1]
    earlier = lax.broadcasted_iota(jnp.int32, (pairs, pairs), 0) < lax.broadcasted_iota(
        jnp.int32, (pairs, pairs), 1
    )
    same = transposed_by_eye(owners) == owners
    slots = jnp.sum(jnp.where(same & earlier, 1.0, 0.0), axis=0, keepdims=True)
    target_ref[...] = (owners * capacity + slots).astype(jnp.int32)

    def tile(part, best):
        table_copy(part).wait()
        block = staged[pl.ds(pl.multiple_of(part * rows, rows), rows), :]
        scores = jnp.dot(block, query_t, preferred_element_type=jnp.float32)
        return jnp.maximum(best, jnp.max(scores.reshape(rows // SUB, SUB, scores.shape[1]), axis=0))

    best = lax.fori_loop(0, PARTS, tile, jnp.full((SUB, q_ref.shape[0]), -jnp.inf, jnp.float32))
    best = jnp.max(best, axis=0, keepdims=True)
    for index in range(best_ref.shape[0]):
        best_ref[index : index + 1, :] = best[:, index * LANES : (index + 1) * LANES]


def centroid_best(query_rows, cand, centroids, pass_dev, capacity):
    tokens, width = query_rows.shape
    cent_dev = centroids.shape[0]
    vmem = pl.BlockSpec(memory_space=pltpu.VMEM)
    return pl.pallas_call(
        functools.partial(best_kernel, pass_dev.bit_length() - 1, capacity),
        in_specs=[vmem, vmem, pl.BlockSpec(memory_space=pl.ANY)],
        out_specs=[vmem] * 2,
        out_shape=[
            jax.ShapeDtypeStruct((tokens // LANES, LANES), jnp.float32),
            jax.ShapeDtypeStruct((1, cand.size), jnp.int32),
        ],
        scratch_shapes=[
            pltpu.VMEM((cent_dev, width), jnp.bfloat16),
            pltpu.SemaphoreType.DMA((PARTS,)),
        ],
        compiler_params=pltpu.CompilerParams(vmem_limit_bytes=56 * MIB),
        cost_estimate=pl.CostEstimate(
            flops=2 * tokens * cent_dev * width, bytes_accessed=2 * cent_dev * width, transcendentals=0
        ),
        name="centroid_best",
    )(query_rows, cand, centroids)


def score_kernel(
    sizes,
    me_ref,
    cand_ref,
    best_ref,
    levels_ref,
    cent_hbm,
    words_hbm,
    codes_hbm,
    lens_hbm,
    *rest,
):
    group_count, cent_count, per_device, query_len, capacity, pass_dev, cand_count = sizes
    query_hbm = rest[:group_count]
    (
        out_ref, staged, table, words, query_rows, query_t, dense, embed, maxima, ids_vmem, ids, codes, lens,
        work, work_quad, item_pass, item_len, item_lane, table_sem, words_sem, query_sem, small_sem,
    ) = rest[group_count:]
    sources = cand_ref.shape[0]
    pairs = per_device * cand_count
    items = sources * capacity
    tiles = words.shape[1] // SUB
    tile_tokens = SUB * FIELDS
    quad_sources = LANES // (per_device * query_len)
    quads = sources // quad_sources
    group_quads = cent_count // quad_sources
    per_bits = per_device.bit_length() - 1
    tile_bits = tiles.bit_length() - 1
    part_rows = staged.shape[0] // quads
    word_parts = words_sem.shape[0]
    part_pass = pass_dev // word_parts

    def table_copy(part):
        rows = pl.ds(pl.multiple_of(part * part_rows, part_rows), part_rows)
        return pltpu.make_async_copy(cent_hbm.at[rows, :], staged.at[rows, :], table_sem.at[part])

    def words_copy(part):
        rows = pl.ds(part * part_pass, part_pass)
        return pltpu.make_async_copy(words_hbm.at[rows], words.at[rows], words_sem.at[part])

    def start_table(part, carry):
        table_copy(part).start()
        return carry

    group = jnp.bitwise_and(me_ref[0], group_count - 1)

    def query_copy(apart):
        return pltpu.make_async_copy(
            query_hbm[apart], query_rows.at[jnp.bitwise_xor(group, apart)], query_sem.at[apart]
        )

    lens_copy = pltpu.make_async_copy(lens_hbm, lens, small_sem.at[0])
    codes_copy = pltpu.make_async_copy(codes_hbm, codes, small_sem.at[1])
    lens_copy.start()
    for apart in range(group_count):
        query_copy(apart).start()
    lax.fori_loop(0, quads, start_table, 0)
    codes_copy.start()
    for part in range(word_parts):
        words_copy(part).start()

    place = lax.broadcasted_iota(jnp.int32, cand_ref.shape, 1)
    local = [
        jnp.sum(jnp.where(place == index, cand_ref[...].astype(jnp.float32), 0.0), axis=1)
        for index in range(per_device)
    ]
    first = me_ref[0] * pass_dev
    local = jnp.concatenate(local, axis=1).astype(jnp.int32) - first
    mine = (local >= 0) & (local < pass_dev)
    earlier = lax.broadcasted_iota(jnp.int32, (pairs, pairs), 0) < lax.broadcasted_iota(
        jnp.int32, (pairs, pairs), 1
    )
    slots = jnp.dot(
        mine.astype(jnp.bfloat16), earlier.astype(jnp.bfloat16), preferred_element_type=jnp.float32
    )
    which = lax.broadcasted_iota(jnp.int32, local.shape, 1) >= cand_count
    tagged = (local * per_device + which.astype(jnp.int32) + 1).astype(jnp.float32)
    lane = lax.broadcasted_iota(jnp.int32, ids_vmem.shape, 1)
    found = jnp.zeros(ids_vmem.shape, jnp.float32)
    for slot in range(capacity):
        chosen = jnp.sum(jnp.where(mine & (slots == slot), tagged, 0.0), axis=1, keepdims=True)
        found = jnp.where(lane == slot, chosen, found)
    ids_vmem[...] = found.astype(jnp.int32)
    ids_copy = pltpu.make_async_copy(ids_vmem, ids, small_sem.at[2])
    ids_copy.start()

    maxima[...] = jnp.full(maxima.shape, MASKED, jnp.float32)
    lens_copy.wait()
    ids_copy.wait()
    for apart in range(group_count):
        query_copy(apart).wait()

    item_pass[items] = 0
    item_len[items] = 0
    item_lane[items] = -1
    spare = items * tiles

    def prepare(quad, count):
        table_copy(quad).wait()
        rows = pl.ds(pl.multiple_of(quad * part_rows, part_rows), part_rows)
        table[rows, :] = staged[rows, :].astype(jnp.float32)
        block = query_rows[quad // group_quads, pl.ds(quad % group_quads * LANES, LANES), :]
        query_t[quad] = jnp.transpose(block.astype(jnp.float32)).astype(jnp.bfloat16)
        start = count
        for part in range(quad_sources):
            cent = quad % group_quads * quad_sources + part
            source = cent * group_count + quad // group_quads
            for slot in range(capacity):
                tag = ids[source, slot] - 1
                item = source * capacity + slot
                real = tag >= 0
                held = jnp.maximum(tag, 0)
                passage = jnp.right_shift(held, per_bits)
                length = lens[passage]
                item_pass[item] = passage
                item_len[item] = length
                item_lane[item] = part * per_device + jnp.bitwise_and(held, per_device - 1)
                for tile in range(tiles):
                    work[count + tile] = item * tiles + tile
                count = count + jnp.where(real, jnp.right_shift(length + tile_tokens - 1, tile_tokens.bit_length() - 1), 0)
        for index in range(ALIGN):
            work[count + index] = spare
        count = (count + ALIGN - 1) // ALIGN * ALIGN
        for index in range(quad_sources * capacity * tiles // ALIGN):
            work_quad[start // ALIGN + index] = quad
        return count

    total = lax.fori_loop(0, quads, prepare, 0)
    for index in range(2 * BLOCKS):
        work[total + index] = spare
    for index in range(2 * BLOCKS // ALIGN):
        work_quad[total // ALIGN + index] = 0
    chunks = jnp.maximum((total + BLOCKS - 1) // BLOCKS, 2)
    codes_copy.wait()
    for part in range(word_parts):
        words_copy(part).wait()

    sub = lax.broadcasted_iota(jnp.int32, (SUB, LANES), 0)
    position = jnp.concatenate([sub * FIELDS + field for field in range(FIELDS)], axis=0)
    lane_group = lax.broadcasted_iota(jnp.int32, (1, LANES), 1) // query_len
    level = [levels_ref[index : index + 1, :] for index in range(FIELDS)]

    def score(chunk):
        scores = []
        for part in range(BLOCKS // ALIGN):
            rows = embed[part * ALIGN * tile_tokens : (part + 1) * ALIGN * tile_tokens, :]
            quad = work_quad[chunk * (BLOCKS // ALIGN) + part]
            scores.append(jnp.dot(rows, query_t[quad], preferred_element_type=jnp.float32))
        for index in range(BLOCKS):
            entry = work[chunk * BLOCKS + index]
            item, tile = jnp.right_shift(entry, tile_bits), jnp.bitwise_and(entry, tiles - 1)
            inner = index % ALIGN
            block = scores[index // ALIGN][inner * tile_tokens : (inner + 1) * tile_tokens]
            kept = jnp.where(position < item_len[item] - tile * tile_tokens, block, MASKED)
            best = jnp.max(kept, axis=0, keepdims=True)
            maxima[tile, pl.ds(item, 1), :] = jnp.where(lane_group == item_lane[item], best, 0.0)

    def decode(chunk):
        for index in range(BLOCKS):
            entry = work[chunk * BLOCKS + index]
            item, tile = jnp.right_shift(entry, tile_bits), jnp.bitwise_and(entry, tiles - 1)
            passage = item_pass[item]
            start = passage * (tiles * tile_tokens) + tile * tile_tokens
            word = words[passage, pl.ds(pl.multiple_of(tile * SUB, SUB), SUB), :]
            for field in range(FIELDS):
                rows = jnp.zeros((SUB, LANES), jnp.float32)
                for row in range(SUB):
                    code = codes[start + (row * FIELDS + field)]
                    rows = jnp.where(sub == row, table[pl.ds(code, SUB, stride=0), :], rows)
                low = jnp.bitwise_and(word, 1 << (2 * field)) != 0
                high = jnp.bitwise_and(word, 2 << (2 * field)) != 0
                residual = jnp.where(
                    high, jnp.where(low, level[3], level[2]), jnp.where(low, level[1], level[0])
                )
                base = index * tile_tokens + field * SUB
                dense[base : base + SUB, :] = rows + residual

    def normalize():
        for index in range(BLOCKS):
            rows = slice(index * tile_tokens, (index + 1) * tile_tokens)
            block = dense[rows, :]
            inverse = lax.rsqrt(jnp.sum(block * block, axis=1, keepdims=True) + 1e-06)
            embed[rows, :] = (block * inverse).astype(jnp.bfloat16)

    decode(0)
    normalize()
    decode(1)

    def step(chunk, carry):
        score(chunk - 2)
        normalize()
        decode(chunk)
        return carry

    lax.fori_loop(2, chunks, step, 0)
    score(chunks - 2)
    normalize()
    score(chunks - 1)

    best = maxima[0, :items, :]
    for tile in range(1, tiles):
        best = jnp.maximum(best, maxima[tile, :items, :])
    sums = jnp.sum(best, axis=1, keepdims=True) / query_len
    item_down = lax.broadcasted_iota(jnp.int32, (items, LANES), 0)
    item_slot = lax.broadcasted_iota(jnp.int32, (items, LANES), 1)
    spread = jnp.where(item_down % capacity == item_slot, sums, 0.0)
    source_down = lax.broadcasted_iota(jnp.int32, (sources, items), 0)
    item_across = lax.broadcasted_iota(jnp.int32, (sources, items), 1)
    gather = (item_across // capacity == source_down).astype(jnp.float32)
    by_source = jnp.dot(
        gather, spread, precision=lax.Precision.HIGHEST, preferred_element_type=jnp.float32
    )
    best_lanes = best_ref.shape[0] * LANES
    for source in range(sources):
        for index in range(best_ref.shape[0]):
            out_ref[source, :, index * LANES : (index + 1) * LANES] = best_ref[index : index + 1, :]
        out_ref[source, :, best_lanes:] = by_source[source : source + 1, :]


def owner_scores(me, cand_all, query_parts, best, centroids, token_codes, resid_words, lengths, levels, sizes):
    capacity = sizes[4]
    sources = cand_all.shape[0]
    group_count = len(query_parts)
    group_rows = query_parts[0].shape[0]
    cent_dev, width = centroids.shape
    pass_dev, plen = token_codes.shape
    packed = resid_words.shape[1]
    tiles = packed // SUB
    items = sources * capacity
    quads = group_count * group_rows // LANES
    work_size = items * tiles + quads * ALIGN + 2 * BLOCKS
    any_space = pl.BlockSpec(memory_space=pl.ANY)
    vmem = pl.BlockSpec(memory_space=pltpu.VMEM)
    tokens = items * plen
    return pl.pallas_call(
        functools.partial(score_kernel, sizes),
        in_specs=[pl.BlockSpec(memory_space=pltpu.SMEM), vmem, vmem, vmem] + [any_space] * (4 + group_count),
        out_specs=vmem,
        out_shape=jax.ShapeDtypeStruct((sources, 1, best.size + LANES), jnp.float32),
        scratch_shapes=[
            pltpu.VMEM((cent_dev, width), jnp.bfloat16),
            pltpu.VMEM((cent_dev + SUB, width), jnp.float32),
            pltpu.VMEM((pass_dev, packed, width), jnp.int32),
            pltpu.VMEM((group_count, group_rows, width), jnp.bfloat16),
            pltpu.VMEM((quads, width, LANES), jnp.bfloat16),
            pltpu.VMEM((BLOCKS * SUB * FIELDS, width), jnp.float32),
            pltpu.VMEM((BLOCKS * SUB * FIELDS, width), jnp.bfloat16),
            pltpu.VMEM((tiles, items + SUB, LANES), jnp.float32),
            pltpu.VMEM((sources, LANES), jnp.int32),
            pltpu.SMEM((sources, LANES), jnp.int32),
            pltpu.SMEM((pass_dev * plen,), jnp.int32),
            pltpu.SMEM((pass_dev,), jnp.int32),
            pltpu.SMEM((work_size,), jnp.int32),
            pltpu.SMEM((work_size // ALIGN + items * tiles // quads,), jnp.int32),
            pltpu.SMEM((items + 1,), jnp.int32),
            pltpu.SMEM((items + 1,), jnp.int32),
            pltpu.SMEM((items + 1,), jnp.int32),
            pltpu.SemaphoreType.DMA((quads,)),
            pltpu.SemaphoreType.DMA((4,)),
            pltpu.SemaphoreType.DMA((group_count,)),
            pltpu.SemaphoreType.DMA((3,)),
        ],
        compiler_params=pltpu.CompilerParams(vmem_limit_bytes=42 * MIB),
        cost_estimate=pl.CostEstimate(
            flops=2 * tokens * width * LANES, bytes_accessed=2 * cent_dev * width * 2, transcendentals=tokens
        ),
        name="owner_scores",
    )(
        me, cand_all, best, levels, centroids, resid_words, token_codes.reshape(pass_dev * plen), lengths, *query_parts
    )


def finish_kernel(sizes, me_ref, back_ref, target_ref, best_out, score_out):
    group_count, cent_count, _, query_len, capacity, _, _ = sizes
    group = jnp.bitwise_and(me_ref[0], group_count - 1)
    best_lanes = best_out.shape[0] * query_len
    best = back_ref[group, :, :best_lanes]
    for cent in range(1, cent_count):
        best = jnp.maximum(best, back_ref[cent * group_count + group, :, :best_lanes])
    for index in range(best_out.shape[0]):
        best_out[index : index + 1, :] = best[:, index * query_len : (index + 1) * query_len]
    back = back_ref[:, 0, best_lanes:]
    target = target_ref[...]
    owner = lax.broadcasted_iota(jnp.int32, (back.shape[0], target.shape[1]), 0)
    found = jnp.zeros(owner.shape, jnp.float32)
    for slot in range(capacity):
        found = found + jnp.where(owner * capacity + slot == target, back[:, slot : slot + 1], 0.0)
    scores = jnp.sum(found, axis=0, keepdims=True)
    width = score_out.shape[1]
    for index in range(score_out.shape[0]):
        score_out[index : index + 1, :] = scores[:, index * width : (index + 1) * width]


def finish(me, back, target, group_rows, sizes):
    _, _, per_device, query_len, _, _, cand_count = sizes
    vmem = pl.BlockSpec(memory_space=pltpu.VMEM)
    return pl.pallas_call(
        functools.partial(finish_kernel, sizes),
        in_specs=[pl.BlockSpec(memory_space=pltpu.SMEM), vmem, vmem],
        out_specs=[vmem] * 2,
        out_shape=[
            jax.ShapeDtypeStruct((group_rows, query_len), jnp.float32),
            jax.ShapeDtypeStruct((per_device, cand_count), jnp.float32),
        ],
        name="finish",
    )(me, back, target)


def shards(queries, centroids, candidates, token_codes, resid_words, lengths, levels):
    group_rows, query_len, width = queries.shape
    pass_dev = token_codes.shape[0]
    per_device, cand_count = candidates.shape[2:]
    pair_count = per_device * cand_count
    cent_count = lax.axis_size("cent")
    group_count = lax.axis_size("grp")
    devices = cent_count * group_count
    capacity = max(2, 2 * pair_count // devices)
    sizes = (group_count, cent_count, per_device, query_len, capacity, pass_dev, cand_count)
    cand = candidates.reshape(per_device, cand_count)
    query_rows = queries.reshape(group_rows * query_len, width)
    me = (lax.axis_index("cent") * group_count + lax.axis_index("grp")).astype(jnp.int32).reshape(1)
    cand_all = lax.all_to_all(
        jnp.broadcast_to(cand, (devices,) + cand.shape), ("cent", "grp"), split_axis=0, concat_axis=0, tiled=True
    )
    query_parts = [query_rows]
    for apart in range(1, group_count):
        pairs = [(index, index ^ apart) for index in range(group_count)]
        query_parts.append(lax.ppermute(query_rows, "grp", pairs))
    best, target = centroid_best(query_rows, cand, centroids, pass_dev, capacity)
    reply = owner_scores(
        me, cand_all, query_parts, best, centroids, token_codes, resid_words, lengths, levels, sizes
    )
    back = lax.all_to_all(reply, ("cent", "grp"), split_axis=0, concat_axis=0, tiled=True)
    token_best, scores = finish(me, back, target, group_rows, sizes)
    return (token_best, scores.reshape(1, 1, per_device, cand_count))


def solution(mesh):
    placed = (
        P("grp", None, None),
        P("cent", None),
        P("grp", "cent", None, None),
        P(("cent", "grp"), None),
        P(("cent", "grp"), None, None),
        P(("cent", "grp")),
        P(),
    )
    return jax.shard_map(
        shards,
        mesh=mesh,
        in_specs=placed,
        out_specs=(P("grp", None), P("grp", "cent", None, None)),
        check_vma=False,
    )
```

```python
import functools

import jax
import jax.numpy as jnp
from jax import lax
from jax.experimental import pallas as pl
from jax.experimental.pallas import tpu as pltpu
from jax.sharding import PartitionSpec as P

MASKED = -1000000000.0
LANES = 128
SUB = 8
FIELDS = 4
BLOCKS = 16
ALIGN = 8
TILE = 1024
MIB = 1 << 20


def transposed_by_eye(row):
    size = row.shape[1]
    down = lax.broadcasted_iota(jnp.int32, (size, size), 0)
    across = lax.broadcasted_iota(jnp.int32, (size, size), 1)
    return jnp.sum(jnp.where(down == across, row, 0.0), axis=1, keepdims=True)


def one_row(rows):
    return jnp.concatenate([rows[index : index + 1, :] for index in range(rows.shape[0])], axis=1)


def ids_kernel(cand_ref, ids_ref):
    ids_ref[...] = jnp.broadcast_to(one_row(cand_ref[...]), ids_ref.shape)


def ids_for_all(cand, devices):
    vmem = pl.BlockSpec(memory_space=pltpu.VMEM)
    return pl.pallas_call(
        ids_kernel,
        in_specs=[vmem],
        out_specs=vmem,
        out_shape=jax.ShapeDtypeStruct((devices, cand.size), jnp.int32),
        name="ids_for_all",
    )(cand)


def score_kernel(
    sizes,
    me_ref,
    cand_ref,
    own_ref,
    levels_ref,
    cent_hbm,
    words_hbm,
    codes_hbm,
    lens_hbm,
    *rest,
):
    group_count, cent_count, per_device, query_len, capacity, pass_dev, cand_count = sizes
    query_hbm = rest[:group_count]
    (
        out_ref, staged, table, words, query_rows, query_t, own_t, dense, embed, maxima, ids_vmem, ids, codes, lens,
        work, work_quad, item_pass, item_len, item_lane, table_sem, words_sem, query_sem, small_sem,
    ) = rest[group_count:]
    sources = cand_ref.shape[0]
    pairs = per_device * cand_count
    items = sources * capacity
    tiles = words.shape[1] // SUB
    tile_tokens = SUB * FIELDS
    quad_sources = LANES // (per_device * query_len)
    quads = sources // quad_sources
    group_quads = cent_count // quad_sources
    per_bits = per_device.bit_length() - 1
    tile_bits = tiles.bit_length() - 1
    part_rows = staged.shape[0] // quads
    word_parts = words_sem.shape[0]
    part_pass = pass_dev // word_parts

    def table_copy(part):
        rows = pl.ds(pl.multiple_of(part * part_rows, part_rows), part_rows)
        return pltpu.make_async_copy(cent_hbm.at[rows, :], staged.at[rows, :], table_sem.at[part])

    def words_copy(part):
        rows = pl.ds(part * part_pass, part_pass)
        return pltpu.make_async_copy(words_hbm.at[rows], words.at[rows], words_sem.at[part])

    def start_table(part, carry):
        table_copy(part).start()
        return carry

    group = jnp.bitwise_and(me_ref[0], group_count - 1)

    def query_copy(apart):
        return pltpu.make_async_copy(
            query_hbm[apart], query_rows.at[jnp.bitwise_xor(group, apart)], query_sem.at[apart]
        )

    lens_copy = pltpu.make_async_copy(lens_hbm, lens, small_sem.at[0])
    codes_copy = pltpu.make_async_copy(codes_hbm, codes, small_sem.at[1])
    lens_copy.start()
    for apart in range(group_count):
        query_copy(apart).start()
    lax.fori_loop(0, quads, start_table, 0)
    codes_copy.start()
    for part in range(word_parts):
        words_copy(part).start()

    first = me_ref[0] * pass_dev
    local = cand_ref[...] - first
    mine = (local >= 0) & (local < pass_dev)
    earlier = lax.broadcasted_iota(jnp.int32, (pairs, pairs), 0) < lax.broadcasted_iota(
        jnp.int32, (pairs, pairs), 1
    )
    slots = jnp.dot(
        mine.astype(jnp.bfloat16), earlier.astype(jnp.bfloat16), preferred_element_type=jnp.float32
    )
    which = lax.broadcasted_iota(jnp.int32, local.shape, 1) >= cand_count
    tagged = (local * per_device + which.astype(jnp.int32) + 1).astype(jnp.float32)
    lane = lax.broadcasted_iota(jnp.int32, ids_vmem.shape, 1)
    found = jnp.zeros(ids_vmem.shape, jnp.float32)
    for slot in range(capacity):
        chosen = jnp.sum(jnp.where(mine & (slots == slot), tagged, 0.0), axis=1, keepdims=True)
        found = jnp.where(lane == slot, chosen, found)
    ids_vmem[...] = found.astype(jnp.int32)
    ids_copy = pltpu.make_async_copy(ids_vmem, ids, small_sem.at[2])
    ids_copy.start()

    maxima[...] = jnp.full(maxima.shape, MASKED, jnp.float32)
    own_t[...] = jnp.transpose(own_ref[...].astype(jnp.float32)).astype(jnp.bfloat16)
    lens_copy.wait()
    ids_copy.wait()
    for apart in range(group_count):
        query_copy(apart).wait()

    item_pass[items] = 0
    item_len[items] = 0
    item_lane[items] = -1
    spare = items * tiles

    def prepare(quad, count):
        table_copy(quad).wait()
        rows = pl.ds(pl.multiple_of(quad * part_rows, part_rows), part_rows)
        table[rows, :] = staged[rows, :].astype(jnp.float32)
        block = query_rows[quad // group_quads, pl.ds(quad % group_quads * LANES, LANES), :]
        query_t[quad] = jnp.transpose(block.astype(jnp.float32)).astype(jnp.bfloat16)
        start = count
        for part in range(quad_sources):
            cent = quad % group_quads * quad_sources + part
            source = cent * group_count + quad // group_quads
            for slot in range(capacity):
                tag = ids[source, slot] - 1
                item = source * capacity + slot
                real = tag >= 0
                held = jnp.maximum(tag, 0)
                passage = jnp.right_shift(held, per_bits)
                length = lens[passage]
                item_pass[item] = passage
                item_len[item] = length
                item_lane[item] = part * per_device + jnp.bitwise_and(held, per_device - 1)
                for tile in range(tiles):
                    work[count + tile] = item * tiles + tile
                count = count + jnp.where(real, jnp.right_shift(length + tile_tokens - 1, tile_tokens.bit_length() - 1), 0)
        for index in range(ALIGN):
            work[count + index] = spare
        count = (count + ALIGN - 1) // ALIGN * ALIGN
        for index in range(quad_sources * capacity * tiles // ALIGN):
            work_quad[start // ALIGN + index] = quad
        return count

    total = lax.fori_loop(0, quads, prepare, 0)
    for index in range(2 * BLOCKS):
        work[total + index] = spare
    for index in range(2 * BLOCKS // ALIGN):
        work_quad[total // ALIGN + index] = 0
    chunks = jnp.maximum((total + BLOCKS - 1) // BLOCKS, 2)
    codes_copy.wait()
    for part in range(word_parts):
        words_copy(part).wait()

    sub = lax.broadcasted_iota(jnp.int32, (SUB, LANES), 0)
    position = jnp.concatenate([sub * FIELDS + field for field in range(FIELDS)], axis=0)
    lane_group = lax.broadcasted_iota(jnp.int32, (1, LANES), 1) // query_len
    level = [levels_ref[index : index + 1, :] for index in range(FIELDS)]

    def score(chunk):
        scores = []
        for part in range(BLOCKS // ALIGN):
            rows = embed[part * ALIGN * tile_tokens : (part + 1) * ALIGN * tile_tokens, :]
            quad = work_quad[chunk * (BLOCKS // ALIGN) + part]
            scores.append(jnp.dot(rows, query_t[quad], preferred_element_type=jnp.float32))
        for index in range(BLOCKS):
            entry = work[chunk * BLOCKS + index]
            item, tile = jnp.right_shift(entry, tile_bits), jnp.bitwise_and(entry, tiles - 1)
            inner = index % ALIGN
            block = scores[index // ALIGN][inner * tile_tokens : (inner + 1) * tile_tokens]
            kept = jnp.where(position < item_len[item] - tile * tile_tokens, block, MASKED)
            best = jnp.max(kept, axis=0, keepdims=True)
            maxima[tile, pl.ds(item, 1), :] = jnp.where(lane_group == item_lane[item], best, 0.0)

    def decode(chunk):
        for index in range(BLOCKS):
            entry = work[chunk * BLOCKS + index]
            item, tile = jnp.right_shift(entry, tile_bits), jnp.bitwise_and(entry, tiles - 1)
            passage = item_pass[item]
            start = passage * (tiles * tile_tokens) + tile * tile_tokens
            word = words[passage, pl.ds(pl.multiple_of(tile * SUB, SUB), SUB), :]
            for field in range(FIELDS):
                rows = jnp.zeros((SUB, LANES), jnp.float32)
                for row in range(SUB):
                    code = codes[start + (row * FIELDS + field)]
                    rows = jnp.where(sub == row, table[pl.ds(code, SUB, stride=0), :], rows)
                low = jnp.bitwise_and(word, 1 << (2 * field)) != 0
                high = jnp.bitwise_and(word, 2 << (2 * field)) != 0
                residual = jnp.where(
                    high, jnp.where(low, level[3], level[2]), jnp.where(low, level[1], level[0])
                )
                base = index * tile_tokens + field * SUB
                dense[base : base + SUB, :] = rows + residual

    def normalize():
        for index in range(BLOCKS):
            rows = slice(index * tile_tokens, (index + 1) * tile_tokens)
            block = dense[rows, :]
            inverse = lax.rsqrt(jnp.sum(block * block, axis=1, keepdims=True) + 1e-06)
            embed[rows, :] = (block * inverse).astype(jnp.bfloat16)

    tile_rows = min(staged.shape[0], TILE)
    best_tiles = staged.shape[0] // tile_rows

    def centroid_tile(index, best):
        block = staged[pl.ds(pl.multiple_of(index * tile_rows, tile_rows), tile_rows), :]
        scores = jnp.dot(block, own_t[...], preferred_element_type=jnp.float32)
        return jnp.maximum(best, jnp.max(scores.reshape(tile_rows // SUB, SUB, scores.shape[1]), axis=0))

    decode(0)
    normalize()
    decode(1)

    def step(chunk, carry):
        score(chunk - 2)
        normalize()
        decode(chunk)
        return carry

    def step_with_tile(chunk, best):
        step(chunk, 0)
        return centroid_tile(chunk - 2, best)

    token_best = jnp.full((SUB, own_t.shape[1]), -jnp.inf, jnp.float32)
    shared = jnp.minimum(chunks, best_tiles + 2)
    token_best = lax.fori_loop(2, shared, step_with_tile, token_best)
    lax.fori_loop(shared, chunks, step, 0)
    score(chunks - 2)
    normalize()
    score(chunks - 1)
    token_best = lax.fori_loop(shared - 2, best_tiles, centroid_tile, token_best)
    token_best = jnp.max(token_best, axis=0, keepdims=True)

    best = maxima[0, :items, :]
    for tile in range(1, tiles):
        best = jnp.maximum(best, maxima[tile, :items, :])
    sums = jnp.sum(best, axis=1, keepdims=True) / query_len
    item_down = lax.broadcasted_iota(jnp.int32, (items, LANES), 0)
    item_slot = lax.broadcasted_iota(jnp.int32, (items, LANES), 1)
    spread = jnp.where(item_down % capacity == item_slot, sums, 0.0)
    source_down = lax.broadcasted_iota(jnp.int32, (sources, items), 0)
    item_across = lax.broadcasted_iota(jnp.int32, (sources, items), 1)
    gather = (item_across // capacity == source_down).astype(jnp.float32)
    by_source = jnp.dot(
        gather, spread, precision=lax.Precision.HIGHEST, preferred_element_type=jnp.float32
    )
    best_lanes = token_best.shape[1]
    for source in range(sources):
        out_ref[source, :, :best_lanes] = token_best
        out_ref[source, :, best_lanes:] = by_source[source : source + 1, :]


def owner_scores(me, cand_all, query_parts, centroids, token_codes, resid_words, lengths, levels, sizes):
    capacity = sizes[4]
    sources = cand_all.shape[0]
    group_count = len(query_parts)
    group_rows = query_parts[0].shape[0]
    cent_dev, width = centroids.shape
    pass_dev, plen = token_codes.shape
    packed = resid_words.shape[1]
    tiles = packed // SUB
    items = sources * capacity
    quads = group_count * group_rows // LANES
    work_size = items * tiles + quads * ALIGN + 2 * BLOCKS
    any_space = pl.BlockSpec(memory_space=pl.ANY)
    vmem = pl.BlockSpec(memory_space=pltpu.VMEM)
    tokens = items * plen
    return pl.pallas_call(
        functools.partial(score_kernel, sizes),
        in_specs=[pl.BlockSpec(memory_space=pltpu.SMEM), vmem, vmem, vmem] + [any_space] * (4 + group_count),
        out_specs=vmem,
        out_shape=jax.ShapeDtypeStruct((sources, 1, group_rows + LANES), jnp.float32),
        scratch_shapes=[
            pltpu.VMEM((cent_dev, width), jnp.bfloat16),
            pltpu.VMEM((cent_dev + SUB, width), jnp.float32),
            pltpu.VMEM((pass_dev, packed, width), jnp.int32),
            pltpu.VMEM((group_count, group_rows, width), jnp.bfloat16),
            pltpu.VMEM((quads, width, LANES), jnp.bfloat16),
            pltpu.VMEM((width, group_rows), jnp.bfloat16),
            pltpu.VMEM((BLOCKS * SUB * FIELDS, width), jnp.float32),
            pltpu.VMEM((BLOCKS * SUB * FIELDS, width), jnp.bfloat16),
            pltpu.VMEM((tiles, items + SUB, LANES), jnp.float32),
            pltpu.VMEM((sources, LANES), jnp.int32),
            pltpu.SMEM((sources, LANES), jnp.int32),
            pltpu.SMEM((pass_dev * plen,), jnp.int32),
            pltpu.SMEM((pass_dev,), jnp.int32),
            pltpu.SMEM((work_size,), jnp.int32),
            pltpu.SMEM((work_size // ALIGN + items * tiles // quads,), jnp.int32),
            pltpu.SMEM((items + 1,), jnp.int32),
            pltpu.SMEM((items + 1,), jnp.int32),
            pltpu.SMEM((items + 1,), jnp.int32),
            pltpu.SemaphoreType.DMA((quads,)),
            pltpu.SemaphoreType.DMA((4,)),
            pltpu.SemaphoreType.DMA((group_count,)),
            pltpu.SemaphoreType.DMA((3,)),
        ],
        compiler_params=pltpu.CompilerParams(vmem_limit_bytes=56 * MIB),
        cost_estimate=pl.CostEstimate(
            flops=2 * (tokens * LANES + cent_dev * group_rows) * width, bytes_accessed=2 * cent_dev * width * 2, transcendentals=tokens
        ),
        name="owner_scores",
    )(
        me, cand_all, query_parts[0], levels, centroids, resid_words, token_codes.reshape(pass_dev * plen), lengths, *query_parts
    )


def finish_kernel(sizes, me_ref, back_ref, cand_ref, best_out, score_out):
    group_count, cent_count, _, query_len, capacity, pass_dev, _ = sizes
    group = jnp.bitwise_and(me_ref[0], group_count - 1)
    best_lanes = best_out.shape[0] * query_len
    best = back_ref[group, :, :best_lanes]
    for cent in range(1, cent_count):
        best = jnp.maximum(best, back_ref[cent * group_count + group, :, :best_lanes])
    for index in range(best_out.shape[0]):
        best_out[index : index + 1, :] = best[:, index * query_len : (index + 1) * query_len]
    back = back_ref[:, 0, best_lanes:]
    owners = jnp.right_shift(one_row(cand_ref[...]), pass_dev.bit_length() - 1).astype(jnp.float32)
    pairs = owners.shape[1]
    earlier = lax.broadcasted_iota(jnp.int32, (pairs, pairs), 0) < lax.broadcasted_iota(
        jnp.int32, (pairs, pairs), 1
    )
    same = transposed_by_eye(owners) == owners
    slots = jnp.sum(jnp.where(same & earlier, 1.0, 0.0), axis=0, keepdims=True)
    target = (owners * capacity + slots).astype(jnp.int32)
    owner = lax.broadcasted_iota(jnp.int32, (back.shape[0], pairs), 0)
    found = jnp.zeros(owner.shape, jnp.float32)
    for slot in range(capacity):
        found = found + jnp.where(owner * capacity + slot == target, back[:, slot : slot + 1], 0.0)
    scores = jnp.sum(found, axis=0, keepdims=True)
    width = score_out.shape[1]
    for index in range(score_out.shape[0]):
        score_out[index : index + 1, :] = scores[:, index * width : (index + 1) * width]


def finish(me, back, cand, group_rows, sizes):
    _, _, per_device, query_len, _, _, cand_count = sizes
    vmem = pl.BlockSpec(memory_space=pltpu.VMEM)
    return pl.pallas_call(
        functools.partial(finish_kernel, sizes),
        in_specs=[pl.BlockSpec(memory_space=pltpu.SMEM), vmem, vmem],
        out_specs=[vmem] * 2,
        out_shape=[
            jax.ShapeDtypeStruct((group_rows, query_len), jnp.float32),
            jax.ShapeDtypeStruct((per_device, cand_count), jnp.float32),
        ],
        name="finish",
    )(me, back, cand)


def shards(queries, centroids, candidates, token_codes, resid_words, lengths, levels):
    group_rows, query_len, width = queries.shape
    pass_dev = token_codes.shape[0]
    per_device, cand_count = candidates.shape[2:]
    pair_count = per_device * cand_count
    cent_count = lax.axis_size("cent")
    group_count = lax.axis_size("grp")
    devices = cent_count * group_count
    capacity = max(2, 2 * pair_count // devices)
    sizes = (group_count, cent_count, per_device, query_len, capacity, pass_dev, cand_count)
    cand = candidates.reshape(per_device, cand_count)
    query_rows = queries.reshape(group_rows * query_len, width)
    me = (lax.axis_index("cent") * group_count + lax.axis_index("grp")).astype(jnp.int32).reshape(1)
    cand_all = lax.all_to_all(
        ids_for_all(cand, devices), ("cent", "grp"), split_axis=0, concat_axis=0, tiled=True
    )
    query_parts = [query_rows]
    for apart in range(1, group_count):
        pairs = [(index, index ^ apart) for index in range(group_count)]
        query_parts.append(lax.ppermute(query_rows, "grp", pairs))
    reply = owner_scores(
        me, cand_all, query_parts, centroids, token_codes, resid_words, lengths, levels, sizes
    )
    back = lax.all_to_all(reply, ("cent", "grp"), split_axis=0, concat_axis=0, tiled=True)
    token_best, scores = finish(me, back, cand, group_rows, sizes)
    return (token_best, scores.reshape(1, 1, per_device, cand_count))


def solution(mesh):
    placed = (
        P("grp", None, None),
        P("cent", None),
        P("grp", "cent", None, None),
        P(("cent", "grp"), None),
        P(("cent", "grp"), None, None),
        P(("cent", "grp")),
        P(),
    )
    return jax.shard_map(
        shards,
        mesh=mesh,
        in_specs=placed,
        out_specs=(P("grp", None), P("grp", "cent", None, None)),
        check_vma=False,
    )
```

```python
import functools

import jax
import jax.numpy as jnp
from jax import lax
from jax.experimental import pallas as pl
from jax.experimental.pallas import tpu as pltpu
from jax.sharding import PartitionSpec as P

MASKED = -1000000000.0
LANES = 128
SUB = 8
FIELDS = 4
BLOCKS = 16
ALIGN = 8
TILE = 1024
PARTS = 16
WORD_PARTS = 4
MIB = 1 << 20


def transposed_by_eye(row):
    size = row.shape[1]
    down = lax.broadcasted_iota(jnp.int32, (size, size), 0)
    across = lax.broadcasted_iota(jnp.int32, (size, size), 1)
    return jnp.sum(jnp.where(down == across, row, 0.0), axis=1, keepdims=True)


def one_row(rows):
    return jnp.concatenate([rows[index : index + 1, :] for index in range(rows.shape[0])], axis=1)


def ids_kernel(cand_ref, ids_ref):
    ids_ref[...] = jnp.broadcast_to(one_row(cand_ref[...]), ids_ref.shape)


def ids_for_all(cand, devices):
    vmem = pl.BlockSpec(memory_space=pltpu.VMEM)
    return pl.pallas_call(
        ids_kernel,
        in_specs=[vmem],
        out_specs=vmem,
        out_shape=jax.ShapeDtypeStruct((devices, cand.size), jnp.int32),
        name="ids_for_all",
    )(cand)


def tables_kernel(cent_hbm, words_hbm, table, staged, words, table_sem, words_sem):
    rows = staged.shape[0] // PARTS
    word_rows = words.shape[0] // WORD_PARTS

    def table_copy(part):
        piece = pl.ds(pl.multiple_of(part * rows, rows), rows)
        return pltpu.make_async_copy(cent_hbm.at[piece, :], staged.at[piece, :], table_sem.at[part])

    def words_copy(part):
        piece = pl.ds(part * word_rows, word_rows)
        return pltpu.make_async_copy(words_hbm.at[piece], words.at[piece], words_sem.at[part])

    for part in range(PARTS):
        table_copy(part).start()
    for part in range(WORD_PARTS):
        words_copy(part).start()

    def widen(part, carry):
        table_copy(part).wait()
        piece = pl.ds(pl.multiple_of(part * rows, rows), rows)
        table[piece, :] = staged[piece, :].astype(jnp.float32)
        return carry

    lax.fori_loop(0, PARTS, widen, 0)
    for part in range(WORD_PARTS):
        words_copy(part).wait()


def tables(centroids, resid_words):
    cent_dev, width = centroids.shape
    vmem = pl.BlockSpec(memory_space=pltpu.VMEM)
    centroids = pltpu.with_memory_space_constraint(centroids, pltpu.HBM)
    resid_words = pltpu.with_memory_space_constraint(resid_words, pltpu.HBM)
    return pl.pallas_call(
        tables_kernel,
        in_specs=[pl.BlockSpec(memory_space=pltpu.HBM)] * 2,
        out_specs=[vmem] * 3,
        out_shape=[
            pltpu.VMEM((cent_dev + SUB, width), jnp.float32),
            pltpu.VMEM((cent_dev, width), jnp.bfloat16),
            pltpu.VMEM(resid_words.shape, jnp.int32),
        ],
        scratch_shapes=[pltpu.SemaphoreType.DMA((PARTS,)), pltpu.SemaphoreType.DMA((WORD_PARTS,))],
        compiler_params=pltpu.CompilerParams(vmem_limit_bytes=4 * MIB),
        cost_estimate=pl.CostEstimate(
            flops=0, bytes_accessed=2 * cent_dev * width + 4 * resid_words.size, transcendentals=0
        ),
        name="tables",
    )(centroids, resid_words)


def score_kernel(
    sizes,
    me_ref,
    cand_ref,
    own_ref,
    levels_ref,
    table,
    staged,
    words,
    codes_hbm,
    lens_hbm,
    *rest,
):
    group_count, cent_count, per_device, query_len, capacity, pass_dev, cand_count = sizes
    query_hbm = rest[:group_count]
    (
        out_ref, query_rows, query_t, own_t, dense, embed, maxima, ids_vmem, ids, codes, lens,
        work, work_quad, item_pass, item_len, item_lane, query_sem, small_sem,
    ) = rest[group_count:]
    sources = cand_ref.shape[0]
    pairs = per_device * cand_count
    items = sources * capacity
    tiles = words.shape[1] // SUB
    tile_tokens = SUB * FIELDS
    quad_sources = LANES // (per_device * query_len)
    quads = sources // quad_sources
    group_quads = cent_count // quad_sources
    per_bits = per_device.bit_length() - 1
    tile_bits = tiles.bit_length() - 1
    group = jnp.bitwise_and(me_ref[0], group_count - 1)

    def query_copy(apart):
        return pltpu.make_async_copy(
            query_hbm[apart], query_rows.at[jnp.bitwise_xor(group, apart)], query_sem.at[apart]
        )

    lens_copy = pltpu.make_async_copy(lens_hbm, lens, small_sem.at[0])
    codes_copy = pltpu.make_async_copy(codes_hbm, codes, small_sem.at[1])
    lens_copy.start()
    for apart in range(group_count):
        query_copy(apart).start()
    codes_copy.start()

    first = me_ref[0] * pass_dev
    local = cand_ref[...] - first
    mine = (local >= 0) & (local < pass_dev)
    earlier = lax.broadcasted_iota(jnp.int32, (pairs, pairs), 0) < lax.broadcasted_iota(
        jnp.int32, (pairs, pairs), 1
    )
    slots = jnp.dot(
        mine.astype(jnp.bfloat16), earlier.astype(jnp.bfloat16), preferred_element_type=jnp.float32
    )
    which = lax.broadcasted_iota(jnp.int32, local.shape, 1) >= cand_count
    tagged = (local * per_device + which.astype(jnp.int32) + 1).astype(jnp.float32)
    lane = lax.broadcasted_iota(jnp.int32, ids_vmem.shape, 1)
    found = jnp.zeros(ids_vmem.shape, jnp.float32)
    for slot in range(capacity):
        chosen = jnp.sum(jnp.where(mine & (slots == slot), tagged, 0.0), axis=1, keepdims=True)
        found = jnp.where(lane == slot, chosen, found)
    ids_vmem[...] = found.astype(jnp.int32)
    ids_copy = pltpu.make_async_copy(ids_vmem, ids, small_sem.at[2])
    ids_copy.start()

    maxima[...] = jnp.full(maxima.shape, MASKED, jnp.float32)
    own_t[...] = jnp.transpose(own_ref[...].astype(jnp.float32)).astype(jnp.bfloat16)
    lens_copy.wait()
    ids_copy.wait()
    for apart in range(group_count):
        query_copy(apart).wait()

    item_pass[items] = 0
    item_len[items] = 0
    item_lane[items] = -1
    spare = items * tiles

    def prepare(quad, count):
        block = query_rows[quad // group_quads, pl.ds(quad % group_quads * LANES, LANES), :]
        query_t[quad] = jnp.transpose(block.astype(jnp.float32)).astype(jnp.bfloat16)
        start = count
        for part in range(quad_sources):
            cent = quad % group_quads * quad_sources + part
            source = cent * group_count + quad // group_quads
            for slot in range(capacity):
                tag = ids[source, slot] - 1
                item = source * capacity + slot
                real = tag >= 0
                held = jnp.maximum(tag, 0)
                passage = jnp.right_shift(held, per_bits)
                length = lens[passage]
                item_pass[item] = passage
                item_len[item] = length
                item_lane[item] = part * per_device + jnp.bitwise_and(held, per_device - 1)
                for tile in range(tiles):
                    work[count + tile] = item * tiles + tile
                count = count + jnp.where(real, jnp.right_shift(length + tile_tokens - 1, tile_tokens.bit_length() - 1), 0)
        for index in range(ALIGN):
            work[count + index] = spare
        count = (count + ALIGN - 1) // ALIGN * ALIGN
        for index in range(quad_sources * capacity * tiles // ALIGN):
            work_quad[start // ALIGN + index] = quad
        return count

    total = lax.fori_loop(0, quads, prepare, 0)
    for index in range(2 * BLOCKS):
        work[total + index] = spare
    for index in range(2 * BLOCKS // ALIGN):
        work_quad[total // ALIGN + index] = 0
    chunks = jnp.maximum((total + BLOCKS - 1) // BLOCKS, 2)
    codes_copy.wait()

    sub = lax.broadcasted_iota(jnp.int32, (SUB, LANES), 0)
    position = jnp.concatenate([sub * FIELDS + field for field in range(FIELDS)], axis=0)
    lane_group = lax.broadcasted_iota(jnp.int32, (1, LANES), 1) // query_len
    level = [levels_ref[index : index + 1, :] for index in range(FIELDS)]

    def score(chunk):
        scores = []
        for part in range(BLOCKS // ALIGN):
            rows = embed[part * ALIGN * tile_tokens : (part + 1) * ALIGN * tile_tokens, :]
            quad = work_quad[chunk * (BLOCKS // ALIGN) + part]
            scores.append(jnp.dot(rows, query_t[quad], preferred_element_type=jnp.float32))
        for index in range(BLOCKS):
            entry = work[chunk * BLOCKS + index]
            item, tile = jnp.right_shift(entry, tile_bits), jnp.bitwise_and(entry, tiles - 1)
            inner = index % ALIGN
            block = scores[index // ALIGN][inner * tile_tokens : (inner + 1) * tile_tokens]
            kept = jnp.where(position < item_len[item] - tile * tile_tokens, block, MASKED)
            best = jnp.max(kept, axis=0, keepdims=True)
            maxima[tile, pl.ds(item, 1), :] = jnp.where(lane_group == item_lane[item], best, 0.0)

    def decode(chunk):
        for index in range(BLOCKS):
            entry = work[chunk * BLOCKS + index]
            item, tile = jnp.right_shift(entry, tile_bits), jnp.bitwise_and(entry, tiles - 1)
            passage = item_pass[item]
            start = passage * (tiles * tile_tokens) + tile * tile_tokens
            word = words[passage, pl.ds(pl.multiple_of(tile * SUB, SUB), SUB), :]
            for field in range(FIELDS):
                rows = jnp.zeros((SUB, LANES), jnp.float32)
                for row in range(SUB):
                    code = codes[start + (row * FIELDS + field)]
                    rows = jnp.where(sub == row, table[pl.ds(code, SUB, stride=0), :], rows)
                low = jnp.bitwise_and(word, 1 << (2 * field)) != 0
                high = jnp.bitwise_and(word, 2 << (2 * field)) != 0
                residual = jnp.where(
                    high, jnp.where(low, level[3], level[2]), jnp.where(low, level[1], level[0])
                )
                base = index * tile_tokens + field * SUB
                dense[base : base + SUB, :] = rows + residual

    def normalize():
        for index in range(BLOCKS):
            rows = slice(index * tile_tokens, (index + 1) * tile_tokens)
            block = dense[rows, :]
            inverse = lax.rsqrt(jnp.sum(block * block, axis=1, keepdims=True) + 1e-06)
            embed[rows, :] = (block * inverse).astype(jnp.bfloat16)

    tile_rows = min(staged.shape[0], TILE)
    best_tiles = staged.shape[0] // tile_rows

    def centroid_tile(index, best):
        block = staged[pl.ds(pl.multiple_of(index * tile_rows, tile_rows), tile_rows), :]
        scores = jnp.dot(block, own_t[...], preferred_element_type=jnp.float32)
        return jnp.maximum(best, jnp.max(scores.reshape(tile_rows // SUB, SUB, scores.shape[1]), axis=0))

    decode(0)
    normalize()
    decode(1)

    def step(chunk, carry):
        score(chunk - 2)
        normalize()
        decode(chunk)
        return carry

    def step_with_tile(chunk, best):
        step(chunk, 0)
        return centroid_tile(chunk - 2, best)

    token_best = jnp.full((SUB, own_t.shape[1]), -jnp.inf, jnp.float32)
    shared = jnp.minimum(chunks, best_tiles + 2)
    token_best = lax.fori_loop(2, shared, step_with_tile, token_best)
    lax.fori_loop(shared, chunks, step, 0)
    score(chunks - 2)
    normalize()
    score(chunks - 1)
    token_best = lax.fori_loop(shared - 2, best_tiles, centroid_tile, token_best)
    token_best = jnp.max(token_best, axis=0, keepdims=True)

    best = maxima[0, :items, :]
    for tile in range(1, tiles):
        best = jnp.maximum(best, maxima[tile, :items, :])
    sums = jnp.sum(best, axis=1, keepdims=True) / query_len
    item_down = lax.broadcasted_iota(jnp.int32, (items, LANES), 0)
    item_slot = lax.broadcasted_iota(jnp.int32, (items, LANES), 1)
    spread = jnp.where(item_down % capacity == item_slot, sums, 0.0)
    source_down = lax.broadcasted_iota(jnp.int32, (sources, items), 0)
    item_across = lax.broadcasted_iota(jnp.int32, (sources, items), 1)
    gather = (item_across // capacity == source_down).astype(jnp.float32)
    by_source = jnp.dot(
        gather, spread, precision=lax.Precision.HIGHEST, preferred_element_type=jnp.float32
    )
    best_lanes = token_best.shape[1]
    for source in range(sources):
        out_ref[source, :, :best_lanes] = token_best
        out_ref[source, :, best_lanes:] = by_source[source : source + 1, :]


def owner_scores(me, cand_all, query_parts, held, token_codes, lengths, levels, sizes):
    held = [pltpu.with_memory_space_constraint(array, pltpu.VMEM) for array in held]
    _, centroids, resid_words = held
    capacity = sizes[4]
    sources = cand_all.shape[0]
    group_count = len(query_parts)
    group_rows = query_parts[0].shape[0]
    cent_dev, width = centroids.shape
    pass_dev, plen = token_codes.shape
    packed = resid_words.shape[1]
    tiles = packed // SUB
    items = sources * capacity
    quads = group_count * group_rows // LANES
    work_size = items * tiles + quads * ALIGN + 2 * BLOCKS
    any_space = pl.BlockSpec(memory_space=pl.ANY)
    vmem = pl.BlockSpec(memory_space=pltpu.VMEM)
    tokens = items * plen
    return pl.pallas_call(
        functools.partial(score_kernel, sizes),
        in_specs=[pl.BlockSpec(memory_space=pltpu.SMEM), vmem, vmem, vmem, vmem, vmem, vmem] + [any_space] * (2 + group_count),
        out_specs=vmem,
        out_shape=jax.ShapeDtypeStruct((sources, 1, group_rows + LANES), jnp.float32),
        scratch_shapes=[
            pltpu.VMEM((group_count, group_rows, width), jnp.bfloat16),
            pltpu.VMEM((quads, width, LANES), jnp.bfloat16),
            pltpu.VMEM((width, group_rows), jnp.bfloat16),
            pltpu.VMEM((BLOCKS * SUB * FIELDS, width), jnp.float32),
            pltpu.VMEM((BLOCKS * SUB * FIELDS, width), jnp.bfloat16),
            pltpu.VMEM((tiles, items + SUB, LANES), jnp.float32),
            pltpu.VMEM((sources, LANES), jnp.int32),
            pltpu.SMEM((sources, LANES), jnp.int32),
            pltpu.SMEM((pass_dev * plen,), jnp.int32),
            pltpu.SMEM((pass_dev,), jnp.int32),
            pltpu.SMEM((work_size,), jnp.int32),
            pltpu.SMEM((work_size // ALIGN + items * tiles // quads,), jnp.int32),
            pltpu.SMEM((items + 1,), jnp.int32),
            pltpu.SMEM((items + 1,), jnp.int32),
            pltpu.SMEM((items + 1,), jnp.int32),
            pltpu.SemaphoreType.DMA((group_count,)),
            pltpu.SemaphoreType.DMA((3,)),
        ],
        compiler_params=pltpu.CompilerParams(vmem_limit_bytes=16 * MIB),
        cost_estimate=pl.CostEstimate(
            flops=2 * (tokens * LANES + cent_dev * group_rows) * width, bytes_accessed=2 * cent_dev * width * 2, transcendentals=tokens
        ),
        name="owner_scores",
    )(
        me, cand_all, query_parts[0], levels, *held, token_codes.reshape(pass_dev * plen), lengths, *query_parts
    )


def finish_kernel(sizes, me_ref, back_ref, cand_ref, best_out, score_out):
    group_count, cent_count, _, query_len, capacity, pass_dev, _ = sizes
    group = jnp.bitwise_and(me_ref[0], group_count - 1)
    best_lanes = best_out.shape[0] * query_len
    best = back_ref[group, :, :best_lanes]
    for cent in range(1, cent_count):
        best = jnp.maximum(best, back_ref[cent * group_count + group, :, :best_lanes])
    for index in range(best_out.shape[0]):
        best_out[index : index + 1, :] = best[:, index * query_len : (index + 1) * query_len]
    back = back_ref[:, 0, best_lanes:]
    owners = jnp.right_shift(one_row(cand_ref[...]), pass_dev.bit_length() - 1).astype(jnp.float32)
    pairs = owners.shape[1]
    earlier = lax.broadcasted_iota(jnp.int32, (pairs, pairs), 0) < lax.broadcasted_iota(
        jnp.int32, (pairs, pairs), 1
    )
    same = transposed_by_eye(owners) == owners
    slots = jnp.sum(jnp.where(same & earlier, 1.0, 0.0), axis=0, keepdims=True)
    target = (owners * capacity + slots).astype(jnp.int32)
    owner = lax.broadcasted_iota(jnp.int32, (back.shape[0], pairs), 0)
    found = jnp.zeros(owner.shape, jnp.float32)
    for slot in range(capacity):
        found = found + jnp.where(owner * capacity + slot == target, back[:, slot : slot + 1], 0.0)
    scores = jnp.sum(found, axis=0, keepdims=True)
    width = score_out.shape[1]
    for index in range(score_out.shape[0]):
        score_out[index : index + 1, :] = scores[:, index * width : (index + 1) * width]


def finish(me, back, cand, group_rows, sizes):
    _, _, per_device, query_len, _, _, cand_count = sizes
    vmem = pl.BlockSpec(memory_space=pltpu.VMEM)
    return pl.pallas_call(
        functools.partial(finish_kernel, sizes),
        in_specs=[pl.BlockSpec(memory_space=pltpu.SMEM), vmem, vmem],
        out_specs=[vmem] * 2,
        out_shape=[
            jax.ShapeDtypeStruct((group_rows, query_len), jnp.float32),
            jax.ShapeDtypeStruct((per_device, cand_count), jnp.float32),
        ],
        name="finish",
    )(me, back, cand)


def shards(queries, centroids, candidates, token_codes, resid_words, lengths, levels):
    group_rows, query_len, width = queries.shape
    pass_dev = token_codes.shape[0]
    per_device, cand_count = candidates.shape[2:]
    pair_count = per_device * cand_count
    cent_count = lax.axis_size("cent")
    group_count = lax.axis_size("grp")
    devices = cent_count * group_count
    capacity = max(2, 2 * pair_count // devices)
    sizes = (group_count, cent_count, per_device, query_len, capacity, pass_dev, cand_count)
    cand = candidates.reshape(per_device, cand_count)
    query_rows = queries.reshape(group_rows * query_len, width)
    me = (lax.axis_index("cent") * group_count + lax.axis_index("grp")).astype(jnp.int32).reshape(1)
    cand_all = lax.all_to_all(
        ids_for_all(cand, devices), ("cent", "grp"), split_axis=0, concat_axis=0, tiled=True
    )
    query_parts = [query_rows]
    for apart in range(1, group_count):
        pairs = [(index, index ^ apart) for index in range(group_count)]
        query_parts.append(lax.ppermute(query_rows, "grp", pairs))
    reply = owner_scores(
        me, cand_all, query_parts, tables(centroids, resid_words), token_codes, lengths, levels, sizes
    )
    back = lax.all_to_all(reply, ("cent", "grp"), split_axis=0, concat_axis=0, tiled=True)
    token_best, scores = finish(me, back, cand, group_rows, sizes)
    return (token_best, scores.reshape(1, 1, per_device, cand_count))


def solution(mesh):
    placed = (
        P("grp", None, None),
        P("cent", None),
        P("grp", "cent", None, None),
        P(("cent", "grp"), None),
        P(("cent", "grp"), None, None),
        P(("cent", "grp")),
        P(),
    )
    return jax.shard_map(
        shards,
        mesh=mesh,
        in_specs=placed,
        out_specs=(P("grp", None), P("grp", "cent", None, None)),
        check_vma=False,
    )
```

```python
import functools

import jax
import jax.numpy as jnp
from jax import lax
from jax.experimental import pallas as pl
from jax.experimental.pallas import tpu as pltpu
from jax.sharding import PartitionSpec as P

MASKED = -1000000000.0
LANES = 128
SUB = 8
FIELDS = 4
BLOCKS = 16
ALIGN = 8
TILE = 1024
MIB = 1 << 20


def transposed_by_eye(row):
    size = row.shape[1]
    down = lax.broadcasted_iota(jnp.int32, (size, size), 0)
    across = lax.broadcasted_iota(jnp.int32, (size, size), 1)
    return jnp.sum(jnp.where(down == across, row, 0.0), axis=1, keepdims=True)


def one_row(rows):
    return jnp.concatenate([rows[index : index + 1, :] for index in range(rows.shape[0])], axis=1)


def ids_kernel(cand_ref, ids_ref):
    ids_ref[...] = jnp.broadcast_to(one_row(cand_ref[...]), ids_ref.shape)


def ids_for_all(cand, devices):
    vmem = pl.BlockSpec(memory_space=pltpu.VMEM)
    return pl.pallas_call(
        ids_kernel,
        in_specs=[vmem],
        out_specs=vmem,
        out_shape=jax.ShapeDtypeStruct((devices, cand.size), jnp.int32),
        name="ids_for_all",
    )(cand)


def score_kernel(
    sizes,
    me_ref,
    cand_ref,
    own_ref,
    levels_ref,
    cent_hbm,
    words_hbm,
    codes_hbm,
    lens_hbm,
    *rest,
):
    group_count, cent_count, per_device, query_len, capacity, pass_dev, cand_count = sizes
    query_hbm = rest[:group_count]
    (
        out_ref, staged, table, words, query_rows, query_t, own_t, dense, embed, maxima, ids_vmem, ids, codes,
        word_stage, code_stage, slot_even, slot_odd, lens, work, work_quad, item_pass, item_len, item_lane, table_sem, words_sem, query_sem, small_sem, slot_sem,
    ) = rest[group_count:]
    code_slots = (slot_even, slot_odd)
    sources = cand_ref.shape[0]
    pairs = per_device * cand_count
    items = sources * capacity
    tiles = words.shape[1] // SUB
    tile_tokens = SUB * FIELDS
    quad_sources = LANES // (per_device * query_len)
    quads = sources // quad_sources
    group_quads = cent_count // quad_sources
    per_bits = per_device.bit_length() - 1
    tile_bits = tiles.bit_length() - 1
    part_rows = staged.shape[0] // quads
    word_parts = words_sem.shape[0]
    part_pass = pass_dev // word_parts

    def table_copy(part):
        rows = pl.ds(pl.multiple_of(part * part_rows, part_rows), part_rows)
        return pltpu.make_async_copy(cent_hbm.at[rows, :], staged.at[rows, :], table_sem.at[part])

    def words_copy(part):
        rows = pl.ds(part * part_pass, part_pass)
        return pltpu.make_async_copy(words_hbm.at[rows], words.at[rows], words_sem.at[part])

    def start_table(part, carry):
        table_copy(part).start()
        return carry

    group = jnp.bitwise_and(me_ref[0], group_count - 1)

    def query_copy(apart):
        return pltpu.make_async_copy(
            query_hbm[apart], query_rows.at[jnp.bitwise_xor(group, apart)], query_sem.at[apart]
        )

    lens_copy = pltpu.make_async_copy(lens_hbm, lens, small_sem.at[0])
    codes_copy = pltpu.make_async_copy(codes_hbm, codes, small_sem.at[1])
    lens_copy.start()
    for apart in range(group_count):
        query_copy(apart).start()
    lax.fori_loop(0, quads, start_table, 0)
    codes_copy.start()
    for part in range(word_parts):
        words_copy(part).start()

    first = me_ref[0] * pass_dev
    local = cand_ref[...] - first
    mine = (local >= 0) & (local < pass_dev)
    earlier = lax.broadcasted_iota(jnp.int32, (pairs, pairs), 0) < lax.broadcasted_iota(
        jnp.int32, (pairs, pairs), 1
    )
    slots = jnp.dot(
        mine.astype(jnp.bfloat16), earlier.astype(jnp.bfloat16), preferred_element_type=jnp.float32
    )
    which = lax.broadcasted_iota(jnp.int32, local.shape, 1) >= cand_count
    tagged = (local * per_device + which.astype(jnp.int32) + 1).astype(jnp.float32)
    lane = lax.broadcasted_iota(jnp.int32, ids_vmem.shape, 1)
    found = jnp.zeros(ids_vmem.shape, jnp.float32)
    for slot in range(capacity):
        chosen = jnp.sum(jnp.where(mine & (slots == slot), tagged, 0.0), axis=1, keepdims=True)
        found = jnp.where(lane == slot, chosen, found)
    ids_vmem[...] = found.astype(jnp.int32)
    ids_copy = pltpu.make_async_copy(ids_vmem, ids, small_sem.at[2])
    ids_copy.start()

    maxima[...] = jnp.full(maxima.shape, MASKED, jnp.float32)
    own_t[...] = jnp.transpose(own_ref[...].astype(jnp.float32)).astype(jnp.bfloat16)
    lens_copy.wait()
    ids_copy.wait()
    for apart in range(group_count):
        query_copy(apart).wait()

    item_pass[items] = 0
    item_len[items] = 0
    item_lane[items] = -1
    spare = items * tiles

    def prepare(quad, count):
        table_copy(quad).wait()
        rows = pl.ds(pl.multiple_of(quad * part_rows, part_rows), part_rows)
        table[rows, :] = staged[rows, :].astype(jnp.float32)
        block = query_rows[quad // group_quads, pl.ds(quad % group_quads * LANES, LANES), :]
        query_t[quad] = jnp.transpose(block.astype(jnp.float32)).astype(jnp.bfloat16)
        start = count
        found = []
        for part in range(quad_sources):
            cent = quad % group_quads * quad_sources + part
            source = cent * group_count + quad // group_quads
            found += [(part, source * capacity + slot, ids[source, slot] - 1) for slot in range(capacity)]
        found = [(part, item, tag, jnp.maximum(tag, 0)) for part, item, tag in found]
        lengths = [lens[jnp.right_shift(held, per_bits)] for _, _, _, held in found]
        for (part, item, tag, held), length in zip(found, lengths):
            item_pass[item] = jnp.right_shift(held, per_bits)
            item_len[item] = length
            item_lane[item] = part * per_device + jnp.bitwise_and(held, per_device - 1)
            for tile in range(tiles):
                work[count + tile] = item * tiles + tile
            blocks = jnp.right_shift(length + tile_tokens - 1, tile_tokens.bit_length() - 1)
            count = count + jnp.where(tag >= 0, blocks, 0)
        for index in range(ALIGN):
            work[count + index] = spare
        count = (count + ALIGN - 1) // ALIGN * ALIGN
        for index in range(quad_sources * capacity * tiles // ALIGN):
            work_quad[start // ALIGN + index] = quad
        return count

    total = lax.fori_loop(0, quads, prepare, 0)
    for index in range(4 * BLOCKS):
        work[total + index] = spare
    for index in range(4 * BLOCKS // ALIGN):
        work_quad[total // ALIGN + index] = 0
    pairs_of_chunks = jnp.maximum((total + 2 * BLOCKS - 1) // (2 * BLOCKS), 1)
    codes_copy.wait()
    for part in range(word_parts):
        words_copy(part).wait()

    sub = lax.broadcasted_iota(jnp.int32, (SUB, LANES), 0)
    position = jnp.concatenate([sub * FIELDS + field for field in range(FIELDS)], axis=0)
    row_blocks = LANES // tile_tokens
    lane_tile = lax.broadcasted_iota(jnp.int32, (1, LANES), 1) // tile_tokens
    lane_group = lax.broadcasted_iota(jnp.int32, (1, LANES), 1) // query_len
    level = [levels_ref[index : index + 1, :] for index in range(FIELDS)]

    def score(chunk):
        scores = []
        for part in range(BLOCKS // ALIGN):
            rows = embed[part * ALIGN * tile_tokens : (part + 1) * ALIGN * tile_tokens, :]
            quad = work_quad[chunk * (BLOCKS // ALIGN) + part]
            scores.append(jnp.dot(rows, query_t[quad], preferred_element_type=jnp.float32))
        for index in range(BLOCKS):
            entry = work[chunk * BLOCKS + index]
            item, tile = jnp.right_shift(entry, tile_bits), jnp.bitwise_and(entry, tiles - 1)
            inner = index % ALIGN
            block = scores[index // ALIGN][inner * tile_tokens : (inner + 1) * tile_tokens]
            kept = jnp.where(position < item_len[item] - tile * tile_tokens, block, MASKED)
            best = jnp.max(kept, axis=0, keepdims=True)
            maxima[tile, pl.ds(item, 1), :] = jnp.where(lane_group == item_lane[item], best, 0.0)

    def slot_copy(slot):
        return pltpu.make_async_copy(code_stage.at[slot], code_slots[slot], slot_sem.at[slot])

    def fetch(chunk, slot):
        for row in range(BLOCKS // row_blocks):
            together = jnp.zeros((1, LANES), jnp.int32)
            for index in range(row_blocks):
                block = row * row_blocks + index
                entry = work[chunk * BLOCKS + block]
                passage = item_pass[jnp.right_shift(entry, tile_bits)]
                tile = jnp.bitwise_and(entry, tiles - 1)
                shift = jnp.bitwise_and(index - tile, row_blocks - 1) * tile_tokens
                moved = pltpu.roll(codes[pl.ds(passage, 1), :], shift, 1)
                together = jnp.where(lane_tile == index, moved, together)
                rows = pl.ds(pl.multiple_of(tile * SUB, SUB), SUB)
                word_stage[slot, block * SUB : (block + 1) * SUB, :] = words[passage, rows, :]
            code_stage[slot, row : row + 1, :] = together
        slot_copy(slot).start()

    def decode(slot):
        for index in range(BLOCKS):
            word = word_stage[slot, index * SUB : (index + 1) * SUB, :]
            for field in range(FIELDS):
                rows = jnp.zeros((SUB, LANES), jnp.float32)
                for row in range(SUB):
                    place = index % row_blocks * tile_tokens + row * FIELDS + field
                    code = code_slots[slot][index // row_blocks, place]
                    rows = jnp.where(sub == row, table[pl.ds(code, SUB, stride=0), :], rows)
                low = jnp.bitwise_and(word, 1 << (2 * field)) != 0
                high = jnp.bitwise_and(word, 2 << (2 * field)) != 0
                residual = jnp.where(
                    high, jnp.where(low, level[3], level[2]), jnp.where(low, level[1], level[0])
                )
                base = index * tile_tokens + field * SUB
                dense[base : base + SUB, :] = rows + residual

    def normalize():
        for index in range(BLOCKS):
            rows = slice(index * tile_tokens, (index + 1) * tile_tokens)
            block = dense[rows, :]
            inverse = lax.rsqrt(jnp.sum(block * block, axis=1, keepdims=True) + 1e-06)
            embed[rows, :] = (block * inverse).astype(jnp.bfloat16)

    tile_rows = min(staged.shape[0], TILE)
    best_tiles = staged.shape[0] // tile_rows

    def centroid_tile(index, best):
        block = staged[pl.ds(pl.multiple_of(index * tile_rows, tile_rows), tile_rows), :]
        scores = jnp.dot(block, own_t[...], preferred_element_type=jnp.float32)
        return jnp.maximum(best, jnp.max(scores.reshape(tile_rows // SUB, SUB, scores.shape[1]), axis=0))

    fetch(0, 0)
    fetch(1, 1)
    slot_copy(0).wait()
    decode(0)
    fetch(2, 0)
    normalize()
    slot_copy(1).wait()
    decode(1)
    fetch(3, 1)

    def step(pair, carry):
        for slot in range(2):
            chunk = 2 * pair + slot
            slot_copy(slot).wait()
            score(chunk - 2)
            normalize()
            decode(slot)
            fetch(chunk + 2, slot)
        return carry

    def step_with_tile(pair, best):
        for slot in range(2):
            chunk = 2 * pair + slot
            slot_copy(slot).wait()
            score(chunk - 2)
            normalize()
            decode(slot)
            best = centroid_tile(chunk - 2, best)
            fetch(chunk + 2, slot)
        return best

    token_best = jnp.full((SUB, own_t.shape[1]), -jnp.inf, jnp.float32)
    shared = jnp.minimum(pairs_of_chunks, best_tiles // 2 + 1)
    token_best = lax.fori_loop(1, shared, step_with_tile, token_best)
    lax.fori_loop(shared, pairs_of_chunks, step, 0)
    score(2 * pairs_of_chunks - 2)
    normalize()
    score(2 * pairs_of_chunks - 1)
    for slot in range(2):
        slot_copy(slot).wait()
    token_best = lax.fori_loop(2 * (shared - 1), best_tiles, centroid_tile, token_best)
    token_best = jnp.max(token_best, axis=0, keepdims=True)

    best = maxima[0, :items, :]
    for tile in range(1, tiles):
        best = jnp.maximum(best, maxima[tile, :items, :])
    sums = jnp.sum(best, axis=1, keepdims=True) / query_len
    item_down = lax.broadcasted_iota(jnp.int32, (items, LANES), 0)
    item_slot = lax.broadcasted_iota(jnp.int32, (items, LANES), 1)
    spread = jnp.where(item_down % capacity == item_slot, sums, 0.0)
    source_down = lax.broadcasted_iota(jnp.int32, (sources, items), 0)
    item_across = lax.broadcasted_iota(jnp.int32, (sources, items), 1)
    gather = (item_across // capacity == source_down).astype(jnp.float32)
    by_source = jnp.dot(
        gather, spread, precision=lax.Precision.HIGHEST, preferred_element_type=jnp.float32
    )
    best_lanes = token_best.shape[1]
    for source in range(sources):
        out_ref[source, :, :best_lanes] = token_best
        out_ref[source, :, best_lanes:] = by_source[source : source + 1, :]


def owner_scores(me, cand_all, query_parts, centroids, token_codes, resid_words, lengths, levels, sizes):
    capacity = sizes[4]
    sources = cand_all.shape[0]
    group_count = len(query_parts)
    group_rows = query_parts[0].shape[0]
    cent_dev, width = centroids.shape
    pass_dev, plen = token_codes.shape
    packed = resid_words.shape[1]
    tiles = packed // SUB
    items = sources * capacity
    quads = group_count * group_rows // LANES
    work_size = items * tiles + quads * ALIGN + 4 * BLOCKS
    any_space = pl.BlockSpec(memory_space=pl.ANY)
    vmem = pl.BlockSpec(memory_space=pltpu.VMEM)
    tokens = items * plen
    return pl.pallas_call(
        functools.partial(score_kernel, sizes),
        in_specs=[pl.BlockSpec(memory_space=pltpu.SMEM), vmem, vmem, vmem] + [any_space] * (4 + group_count),
        out_specs=vmem,
        out_shape=jax.ShapeDtypeStruct((sources, 1, group_rows + LANES), jnp.float32),
        scratch_shapes=[
            pltpu.VMEM((cent_dev, width), jnp.bfloat16),
            pltpu.VMEM((cent_dev + SUB, width), jnp.float32),
            pltpu.VMEM((pass_dev, packed, width), jnp.int32),
            pltpu.VMEM((group_count, group_rows, width), jnp.bfloat16),
            pltpu.VMEM((quads, width, LANES), jnp.bfloat16),
            pltpu.VMEM((width, group_rows), jnp.bfloat16),
            pltpu.VMEM((BLOCKS * SUB * FIELDS, width), jnp.float32),
            pltpu.VMEM((BLOCKS * SUB * FIELDS, width), jnp.bfloat16),
            pltpu.VMEM((tiles, items + SUB, LANES), jnp.float32),
            pltpu.VMEM((sources, LANES), jnp.int32),
            pltpu.SMEM((sources, LANES), jnp.int32),
            pltpu.VMEM((pass_dev, plen), jnp.int32),
            pltpu.VMEM((2, BLOCKS * SUB, LANES), jnp.int32),
            pltpu.VMEM((2, BLOCKS * SUB * FIELDS // LANES, LANES), jnp.int32),
            pltpu.SMEM((BLOCKS * SUB * FIELDS // LANES, LANES), jnp.int32),
            pltpu.SMEM((BLOCKS * SUB * FIELDS // LANES, LANES), jnp.int32),
            pltpu.SMEM((pass_dev,), jnp.int32),
            pltpu.SMEM((work_size,), jnp.int32),
            pltpu.SMEM((work_size // ALIGN + items * tiles // quads,), jnp.int32),
            pltpu.SMEM((items + 1,), jnp.int32),
            pltpu.SMEM((items + 1,), jnp.int32),
            pltpu.SMEM((items + 1,), jnp.int32),
            pltpu.SemaphoreType.DMA((quads,)),
            pltpu.SemaphoreType.DMA((4,)),
            pltpu.SemaphoreType.DMA((group_count,)),
            pltpu.SemaphoreType.DMA((3,)),
            pltpu.SemaphoreType.DMA((2,)),
        ],
        compiler_params=pltpu.CompilerParams(vmem_limit_bytes=56 * MIB),
        cost_estimate=pl.CostEstimate(
            flops=2 * (tokens * LANES + cent_dev * group_rows) * width, bytes_accessed=2 * cent_dev * width * 2, transcendentals=tokens
        ),
        name="owner_scores",
    )(
        me, cand_all, query_parts[0], levels, centroids, resid_words, token_codes, lengths, *query_parts
    )


def finish_kernel(sizes, me_ref, back_ref, cand_ref, best_out, score_out):
    group_count, cent_count, _, query_len, capacity, pass_dev, _ = sizes
    group = jnp.bitwise_and(me_ref[0], group_count - 1)
    best_lanes = best_out.shape[0] * query_len
    best = back_ref[group, :, :best_lanes]
    for cent in range(1, cent_count):
        best = jnp.maximum(best, back_ref[cent * group_count + group, :, :best_lanes])
    for index in range(best_out.shape[0]):
        best_out[index : index + 1, :] = best[:, index * query_len : (index + 1) * query_len]
    back = back_ref[:, 0, best_lanes:]
    owners = jnp.right_shift(one_row(cand_ref[...]), pass_dev.bit_length() - 1).astype(jnp.float32)
    pairs = owners.shape[1]
    earlier = lax.broadcasted_iota(jnp.int32, (pairs, pairs), 0) < lax.broadcasted_iota(
        jnp.int32, (pairs, pairs), 1
    )
    same = transposed_by_eye(owners) == owners
    slots = jnp.sum(jnp.where(same & earlier, 1.0, 0.0), axis=0, keepdims=True)
    target = (owners * capacity + slots).astype(jnp.int32)
    owner = lax.broadcasted_iota(jnp.int32, (back.shape[0], pairs), 0)
    found = jnp.zeros(owner.shape, jnp.float32)
    for slot in range(capacity):
        found = found + jnp.where(owner * capacity + slot == target, back[:, slot : slot + 1], 0.0)
    scores = jnp.sum(found, axis=0, keepdims=True)
    width = score_out.shape[1]
    for index in range(score_out.shape[0]):
        score_out[index : index + 1, :] = scores[:, index * width : (index + 1) * width]


def finish(me, back, cand, group_rows, sizes):
    _, _, per_device, query_len, _, _, cand_count = sizes
    vmem = pl.BlockSpec(memory_space=pltpu.VMEM)
    return pl.pallas_call(
        functools.partial(finish_kernel, sizes),
        in_specs=[pl.BlockSpec(memory_space=pltpu.SMEM), vmem, vmem],
        out_specs=[vmem] * 2,
        out_shape=[
            jax.ShapeDtypeStruct((group_rows, query_len), jnp.float32),
            jax.ShapeDtypeStruct((per_device, cand_count), jnp.float32),
        ],
        name="finish",
    )(me, back, cand)


def shards(queries, centroids, candidates, token_codes, resid_words, lengths, levels):
    group_rows, query_len, width = queries.shape
    pass_dev = token_codes.shape[0]
    per_device, cand_count = candidates.shape[2:]
    pair_count = per_device * cand_count
    cent_count = lax.axis_size("cent")
    group_count = lax.axis_size("grp")
    devices = cent_count * group_count
    capacity = max(2, 2 * pair_count // devices)
    sizes = (group_count, cent_count, per_device, query_len, capacity, pass_dev, cand_count)
    cand = candidates.reshape(per_device, cand_count)
    query_rows = queries.reshape(group_rows * query_len, width)
    me = (lax.axis_index("cent") * group_count + lax.axis_index("grp")).astype(jnp.int32).reshape(1)
    cand_all = lax.all_to_all(
        ids_for_all(cand, devices), ("cent", "grp"), split_axis=0, concat_axis=0, tiled=True
    )
    query_parts = [query_rows]
    for apart in range(1, group_count):
        pairs = [(index, index ^ apart) for index in range(group_count)]
        query_parts.append(lax.ppermute(query_rows, "grp", pairs))
    reply = owner_scores(
        me, cand_all, query_parts, centroids, token_codes, resid_words, lengths, levels, sizes
    )
    back = lax.all_to_all(reply, ("cent", "grp"), split_axis=0, concat_axis=0, tiled=True)
    token_best, scores = finish(me, back, cand, group_rows, sizes)
    return (token_best, scores.reshape(1, 1, per_device, cand_count))


def solution(mesh):
    placed = (
        P("grp", None, None),
        P("cent", None),
        P("grp", "cent", None, None),
        P(("cent", "grp"), None),
        P(("cent", "grp"), None, None),
        P(("cent", "grp")),
        P(),
    )
    return jax.shard_map(
        shards,
        mesh=mesh,
        in_specs=placed,
        out_specs=(P("grp", None), P("grp", "cent", None, None)),
        check_vma=False,
    )
```

```python
import functools

import jax
import jax.numpy as jnp
from jax import lax
from jax.experimental import pallas as pl
from jax.experimental.pallas import tpu as pltpu
from jax.sharding import PartitionSpec as P

MASKED = -1000000000.0
LANES = 128
SUB = 8
FIELDS = 4
BLOCKS = 16
ALIGN = 8
MIB = 1 << 20


def transposed_by_eye(row):
    size = row.shape[1]
    down = lax.broadcasted_iota(jnp.int32, (size, size), 0)
    across = lax.broadcasted_iota(jnp.int32, (size, size), 1)
    return jnp.sum(jnp.where(down == across, row, 0.0), axis=1, keepdims=True)


def one_row(rows):
    return jnp.concatenate([rows[index : index + 1, :] for index in range(rows.shape[0])], axis=1)


def slots_kernel(pass_dev, capacity, cand_ref, slots_ref, target_ref):
    per_device = cand_ref.shape[0]
    ids = one_row(cand_ref[...])
    pairs = ids.shape[1]
    owners = jnp.right_shift(ids, pass_dev.bit_length() - 1)
    earlier = lax.broadcasted_iota(jnp.int32, (pairs, pairs), 0) < lax.broadcasted_iota(
        jnp.int32, (pairs, pairs), 1
    )
    named = owners.astype(jnp.float32)
    same = transposed_by_eye(named) == named
    slots = jnp.sum(jnp.where(same & earlier, 1.0, 0.0), axis=0, keepdims=True).astype(jnp.int32)
    target_ref[...] = owners * capacity + slots
    query = lax.broadcasted_iota(jnp.int32, ids.shape, 1) // (pairs // per_device)
    tagged = (jnp.bitwise_and(ids, pass_dev - 1) * per_device + query + 1).astype(jnp.float32)
    down = lax.broadcasted_iota(jnp.int32, (slots_ref.shape[0], pairs), 0)
    lane = lax.broadcasted_iota(jnp.int32, slots_ref.shape, 1)
    found = jnp.zeros(slots_ref.shape, jnp.float32)
    for slot in range(capacity):
        chosen = jnp.where((down == owners) & (slots == slot), tagged, 0.0)
        found = jnp.where(lane == slot, jnp.sum(chosen, axis=1, keepdims=True), found)
    slots_ref[...] = found.astype(jnp.int32)


def slots_by_owner(cand, devices, pass_dev, capacity):
    vmem = pl.BlockSpec(memory_space=pltpu.VMEM)
    return pl.pallas_call(
        functools.partial(slots_kernel, pass_dev, capacity),
        in_specs=[vmem],
        out_specs=[vmem] * 2,
        out_shape=[
            jax.ShapeDtypeStruct((devices, capacity), jnp.int32),
            jax.ShapeDtypeStruct((1, cand.size), jnp.int32),
        ],
        name="slots_by_owner",
    )(cand)


def score_kernel(
    sizes,
    me_ref,
    ids,
    own_ref,
    levels_ref,
    cent_hbm,
    words_hbm,
    codes_hbm,
    lens_hbm,
    *rest,
):
    group_count, cent_count, per_device, query_len, capacity, pass_dev, cand_count = sizes
    query_hbm = rest[:group_count]
    (
        out_ref, staged, table, words, query_rows, query_t, own_t, dense, embed, maxima, codes,
        word_stage, code_stage, slot_even, slot_odd, lens, work, work_quad, item_pass, item_len, item_lane, table_sem, words_sem, query_sem, small_sem, slot_sem,
    ) = rest[group_count:]
    code_slots = (slot_even, slot_odd)
    sources = ids.shape[0]
    items = sources * capacity
    tiles = words.shape[1] // SUB
    tile_tokens = SUB * FIELDS
    quad_sources = LANES // (per_device * query_len)
    quads = sources // quad_sources
    group_quads = cent_count // quad_sources
    per_bits = per_device.bit_length() - 1
    tile_bits = tiles.bit_length() - 1
    part_rows = staged.shape[0] // quads
    word_parts = words_sem.shape[0]
    part_pass = pass_dev // word_parts

    def table_copy(part):
        rows = pl.ds(pl.multiple_of(part * part_rows, part_rows), part_rows)
        return pltpu.make_async_copy(cent_hbm.at[rows, :], staged.at[rows, :], table_sem.at[part])

    def words_copy(part):
        rows = pl.ds(part * part_pass, part_pass)
        return pltpu.make_async_copy(words_hbm.at[rows], words.at[rows], words_sem.at[part])

    def start_table(part, carry):
        table_copy(part).start()
        return carry

    group = jnp.bitwise_and(me_ref[0], group_count - 1)

    def query_copy(apart):
        return pltpu.make_async_copy(
            query_hbm[apart], query_rows.at[jnp.bitwise_xor(group, apart)], query_sem.at[apart]
        )

    lens_copy = pltpu.make_async_copy(lens_hbm, lens, small_sem.at[0])
    codes_copy = pltpu.make_async_copy(codes_hbm, codes, small_sem.at[1])
    lens_copy.start()
    for apart in range(group_count):
        query_copy(apart).start()
    lax.fori_loop(0, quads, start_table, 0)
    codes_copy.start()
    for part in range(word_parts):
        words_copy(part).start()

    maxima[...] = jnp.full(maxima.shape, MASKED, jnp.float32)
    own_t[...] = jnp.transpose(own_ref[...].astype(jnp.float32)).astype(jnp.bfloat16)
    lens_copy.wait()
    for apart in range(group_count):
        query_copy(apart).wait()

    item_pass[items] = 0
    item_len[items] = 0
    item_lane[items] = -1
    spare = items * tiles

    def prepare(quad, carry):
        count, best = carry
        table_copy(quad).wait()
        rows = pl.ds(pl.multiple_of(quad * part_rows, part_rows), part_rows)
        scores = jnp.dot(staged[rows, :], own_t[...], preferred_element_type=jnp.float32)
        best = jnp.maximum(best, jnp.max(scores.reshape(part_rows // SUB, SUB, scores.shape[1]), axis=0))
        table[rows, :] = staged[rows, :].astype(jnp.float32)
        block = query_rows[quad // group_quads, pl.ds(quad % group_quads * LANES, LANES), :]
        query_t[quad] = jnp.transpose(block.astype(jnp.float32)).astype(jnp.bfloat16)
        start = count
        found = []
        for part in range(quad_sources):
            cent = quad % group_quads * quad_sources + part
            source = cent * group_count + quad // group_quads
            found += [(part, source * capacity + slot, ids[source, slot] - 1) for slot in range(capacity)]
        found = [(part, item, tag, jnp.maximum(tag, 0)) for part, item, tag in found]
        lengths = [lens[jnp.right_shift(held, per_bits)] for _, _, _, held in found]
        for (part, item, tag, held), length in zip(found, lengths):
            item_pass[item] = jnp.right_shift(held, per_bits)
            item_len[item] = length
            item_lane[item] = part * per_device + jnp.bitwise_and(held, per_device - 1)
            for tile in range(tiles):
                work[count + tile] = item * tiles + tile
            blocks = jnp.right_shift(length + tile_tokens - 1, tile_tokens.bit_length() - 1)
            count = count + jnp.where(tag >= 0, blocks, 0)
        for index in range(ALIGN):
            work[count + index] = spare
        count = (count + ALIGN - 1) // ALIGN * ALIGN
        for index in range(quad_sources * capacity * tiles // ALIGN):
            work_quad[start // ALIGN + index] = quad
        return count, best

    lowest = jnp.full((SUB, own_t.shape[1]), -jnp.inf, jnp.float32)
    total, token_best = lax.fori_loop(0, quads, prepare, (0, lowest))
    token_best = jnp.max(token_best, axis=0, keepdims=True)
    for index in range(4 * BLOCKS):
        work[total + index] = spare
    for index in range(4 * BLOCKS // ALIGN):
        work_quad[total // ALIGN + index] = 0
    pairs_of_chunks = jnp.maximum((total + 2 * BLOCKS - 1) // (2 * BLOCKS), 1)
    codes_copy.wait()
    for part in range(word_parts):
        words_copy(part).wait()

    sub = lax.broadcasted_iota(jnp.int32, (SUB, LANES), 0)
    position = jnp.concatenate([sub * FIELDS + field for field in range(FIELDS)], axis=0)
    row_blocks = LANES // tile_tokens
    lane_tile = lax.broadcasted_iota(jnp.int32, (1, LANES), 1) // tile_tokens
    lane_group = lax.broadcasted_iota(jnp.int32, (1, LANES), 1) // query_len
    level = [levels_ref[index : index + 1, :] for index in range(FIELDS)]

    def score(chunk):
        scores = []
        for part in range(BLOCKS // ALIGN):
            rows = embed[part * ALIGN * tile_tokens : (part + 1) * ALIGN * tile_tokens, :]
            quad = work_quad[chunk * (BLOCKS // ALIGN) + part]
            scores.append(jnp.dot(rows, query_t[quad], preferred_element_type=jnp.float32))
        for index in range(BLOCKS):
            entry = work[chunk * BLOCKS + index]
            item, tile = jnp.right_shift(entry, tile_bits), jnp.bitwise_and(entry, tiles - 1)
            inner = index % ALIGN
            block = scores[index // ALIGN][inner * tile_tokens : (inner + 1) * tile_tokens]
            kept = jnp.where(position < item_len[item] - tile * tile_tokens, block, MASKED)
            best = jnp.max(kept, axis=0, keepdims=True)
            maxima[tile, pl.ds(item, 1), :] = jnp.where(lane_group == item_lane[item], best, 0.0)

    def slot_copy(slot):
        return pltpu.make_async_copy(code_stage.at[slot], code_slots[slot], slot_sem.at[slot])

    def fetch(chunk, slot):
        for row in range(BLOCKS // row_blocks):
            together = jnp.zeros((1, LANES), jnp.int32)
            for index in range(row_blocks):
                block = row * row_blocks + index
                entry = work[chunk * BLOCKS + block]
                passage = item_pass[jnp.right_shift(entry, tile_bits)]
                tile = jnp.bitwise_and(entry, tiles - 1)
                shift = jnp.bitwise_and(index - tile, row_blocks - 1) * tile_tokens
                moved = pltpu.roll(codes[pl.ds(passage, 1), :], shift, 1)
                together = jnp.where(lane_tile == index, moved, together)
                rows = pl.ds(pl.multiple_of(tile * SUB, SUB), SUB)
                word_stage[slot, block * SUB : (block + 1) * SUB, :] = words[passage, rows, :]
            code_stage[slot, row : row + 1, :] = together

    def decode(slot):
        for index in range(BLOCKS):
            word = word_stage[slot, index * SUB : (index + 1) * SUB, :]
            for field in range(FIELDS):
                rows = jnp.zeros((SUB, LANES), jnp.float32)
                for row in range(SUB):
                    place = index % row_blocks * tile_tokens + row * FIELDS + field
                    code = code_slots[slot][index // row_blocks, place]
                    rows = jnp.where(sub == row, table[pl.ds(code, SUB, stride=0), :], rows)
                low = jnp.bitwise_and(word, 1 << (2 * field)) != 0
                high = jnp.bitwise_and(word, 2 << (2 * field)) != 0
                residual = jnp.where(
                    high, jnp.where(low, level[3], level[2]), jnp.where(low, level[1], level[0])
                )
                base = index * tile_tokens + field * SUB
                dense[base : base + SUB, :] = rows + residual

    def normalize():
        for index in range(BLOCKS):
            rows = slice(index * tile_tokens, (index + 1) * tile_tokens)
            block = dense[rows, :]
            inverse = lax.rsqrt(jnp.sum(block * block, axis=1, keepdims=True) + 1e-06)
            embed[rows, :] = (block * inverse).astype(jnp.bfloat16)

    fetch(0, 0)
    slot_copy(0).start()
    fetch(1, 1)
    slot_copy(0).wait()
    slot_copy(1).start()
    decode(0)
    fetch(2, 0)
    normalize()
    slot_copy(1).wait()
    slot_copy(0).start()
    decode(1)
    fetch(3, 1)

    def step(pair, carry):
        for slot in range(2):
            chunk = 2 * pair + slot
            slot_copy(slot).wait()
            slot_copy(1 - slot).start()
            score(chunk - 2)
            normalize()
            decode(slot)
            fetch(chunk + 2, slot)
        return carry

    lax.fori_loop(1, pairs_of_chunks, step, 0)
    slot_copy(0).wait()
    score(2 * pairs_of_chunks - 2)
    normalize()
    score(2 * pairs_of_chunks - 1)

    best = maxima[0, :items, :]
    for tile in range(1, tiles):
        best = jnp.maximum(best, maxima[tile, :items, :])
    sums = jnp.sum(best, axis=1, keepdims=True) / query_len
    item_down = lax.broadcasted_iota(jnp.int32, (items, LANES), 0)
    item_slot = lax.broadcasted_iota(jnp.int32, (items, LANES), 1)
    spread = jnp.where(item_down % capacity == item_slot, sums, 0.0)
    source_down = lax.broadcasted_iota(jnp.int32, (sources, items), 0)
    item_across = lax.broadcasted_iota(jnp.int32, (sources, items), 1)
    gather = (item_across // capacity == source_down).astype(jnp.float32)
    by_source = jnp.dot(
        gather, spread, precision=lax.Precision.HIGHEST, preferred_element_type=jnp.float32
    )
    best_lanes = token_best.shape[1]
    for source in range(sources):
        out_ref[source, :, :best_lanes] = token_best
        out_ref[source, :, best_lanes:] = by_source[source : source + 1, :]


def owner_scores(me, slots, query_parts, centroids, token_codes, resid_words, lengths, levels, sizes):
    capacity = sizes[4]
    sources = slots.shape[0]
    group_count = len(query_parts)
    group_rows = query_parts[0].shape[0]
    cent_dev, width = centroids.shape
    pass_dev, plen = token_codes.shape
    packed = resid_words.shape[1]
    tiles = packed // SUB
    items = sources * capacity
    quads = group_count * group_rows // LANES
    work_size = items * tiles + quads * ALIGN + 4 * BLOCKS
    any_space = pl.BlockSpec(memory_space=pl.ANY)
    vmem = pl.BlockSpec(memory_space=pltpu.VMEM)
    tokens = items * plen
    return pl.pallas_call(
        functools.partial(score_kernel, sizes),
        in_specs=[pl.BlockSpec(memory_space=pltpu.SMEM)] * 2 + [vmem, vmem] + [any_space] * (4 + group_count),
        out_specs=vmem,
        out_shape=jax.ShapeDtypeStruct((sources, 1, group_rows + LANES), jnp.float32),
        scratch_shapes=[
            pltpu.VMEM((cent_dev, width), jnp.bfloat16),
            pltpu.VMEM((cent_dev + SUB, width), jnp.float32),
            pltpu.VMEM((pass_dev, packed, width), jnp.int32),
            pltpu.VMEM((group_count, group_rows, width), jnp.bfloat16),
            pltpu.VMEM((quads, width, LANES), jnp.bfloat16),
            pltpu.VMEM((width, group_rows), jnp.bfloat16),
            pltpu.VMEM((BLOCKS * SUB * FIELDS, width), jnp.float32),
            pltpu.VMEM((BLOCKS * SUB * FIELDS, width), jnp.bfloat16),
            pltpu.VMEM((tiles, items + SUB, LANES), jnp.float32),
            pltpu.VMEM((pass_dev, plen), jnp.int32),
            pltpu.VMEM((2, BLOCKS * SUB, LANES), jnp.int32),
            pltpu.VMEM((2, BLOCKS * SUB * FIELDS // LANES, LANES), jnp.int32),
            pltpu.SMEM((BLOCKS * SUB * FIELDS // LANES, LANES), jnp.int32),
            pltpu.SMEM((BLOCKS * SUB * FIELDS // LANES, LANES), jnp.int32),
            pltpu.SMEM((pass_dev,), jnp.int32),
            pltpu.SMEM((work_size,), jnp.int32),
            pltpu.SMEM((work_size // ALIGN + items * tiles // quads,), jnp.int32),
            pltpu.SMEM((items + 1,), jnp.int32),
            pltpu.SMEM((items + 1,), jnp.int32),
            pltpu.SMEM((items + 1,), jnp.int32),
            pltpu.SemaphoreType.DMA((quads,)),
            pltpu.SemaphoreType.DMA((4,)),
            pltpu.SemaphoreType.DMA((group_count,)),
            pltpu.SemaphoreType.DMA((2,)),
            pltpu.SemaphoreType.DMA((2,)),
        ],
        compiler_params=pltpu.CompilerParams(vmem_limit_bytes=56 * MIB),
        cost_estimate=pl.CostEstimate(
            flops=2 * (tokens * LANES + cent_dev * group_rows) * width, bytes_accessed=2 * cent_dev * width * 2, transcendentals=tokens
        ),
        name="owner_scores",
    )(
        me, slots, query_parts[0], levels, centroids, resid_words, token_codes, lengths, *query_parts
    )


def finish_kernel(sizes, me_ref, back_ref, target_ref, best_out, score_out):
    group_count, cent_count, _, query_len, capacity, _, _ = sizes
    group = jnp.bitwise_and(me_ref[0], group_count - 1)
    best_lanes = best_out.shape[0] * query_len
    best = back_ref[group, :, :best_lanes]
    for cent in range(1, cent_count):
        best = jnp.maximum(best, back_ref[cent * group_count + group, :, :best_lanes])
    for index in range(best_out.shape[0]):
        best_out[index : index + 1, :] = best[:, index * query_len : (index + 1) * query_len]
    back = back_ref[:, 0, best_lanes:]
    target = target_ref[...]
    owner = lax.broadcasted_iota(jnp.int32, (back.shape[0], target.shape[1]), 0)
    found = jnp.zeros(owner.shape, jnp.float32)
    for slot in range(capacity):
        found = found + jnp.where(owner * capacity + slot == target, back[:, slot : slot + 1], 0.0)
    scores = jnp.sum(found, axis=0, keepdims=True)
    width = score_out.shape[1]
    for index in range(score_out.shape[0]):
        score_out[index : index + 1, :] = scores[:, index * width : (index + 1) * width]


def finish(me, back, target, group_rows, sizes):
    _, _, per_device, query_len, _, _, cand_count = sizes
    vmem = pl.BlockSpec(memory_space=pltpu.VMEM)
    return pl.pallas_call(
        functools.partial(finish_kernel, sizes),
        in_specs=[pl.BlockSpec(memory_space=pltpu.SMEM), vmem, vmem],
        out_specs=[vmem] * 2,
        out_shape=[
            jax.ShapeDtypeStruct((group_rows, query_len), jnp.float32),
            jax.ShapeDtypeStruct((per_device, cand_count), jnp.float32),
        ],
        name="finish",
    )(me, back, target)


def shards(queries, centroids, candidates, token_codes, resid_words, lengths, levels):
    group_rows, query_len, width = queries.shape
    pass_dev = token_codes.shape[0]
    per_device, cand_count = candidates.shape[2:]
    pair_count = per_device * cand_count
    cent_count = lax.axis_size("cent")
    group_count = lax.axis_size("grp")
    devices = cent_count * group_count
    capacity = max(2, 2 * pair_count // devices)
    sizes = (group_count, cent_count, per_device, query_len, capacity, pass_dev, cand_count)
    cand = candidates.reshape(per_device, cand_count)
    query_rows = queries.reshape(group_rows * query_len, width)
    me = (lax.axis_index("cent") * group_count + lax.axis_index("grp")).astype(jnp.int32).reshape(1)
    slots, target = slots_by_owner(cand, devices, pass_dev, capacity)
    slots = lax.all_to_all(slots, ("cent", "grp"), split_axis=0, concat_axis=0, tiled=True)
    query_parts = [query_rows]
    for apart in range(1, group_count):
        pairs = [(index, index ^ apart) for index in range(group_count)]
        query_parts.append(lax.ppermute(query_rows, "grp", pairs))
    reply = owner_scores(
        me, slots, query_parts, centroids, token_codes, resid_words, lengths, levels, sizes
    )
    back = lax.all_to_all(reply, ("cent", "grp"), split_axis=0, concat_axis=0, tiled=True)
    token_best, scores = finish(me, back, target, group_rows, sizes)
    return (token_best, scores.reshape(1, 1, per_device, cand_count))


def solution(mesh):
    placed = (
        P("grp", None, None),
        P("cent", None),
        P("grp", "cent", None, None),
        P(("cent", "grp"), None),
        P(("cent", "grp"), None, None),
        P(("cent", "grp")),
        P(),
    )
    return jax.shard_map(
        shards,
        mesh=mesh,
        in_specs=placed,
        out_specs=(P("grp", None), P("grp", "cent", None, None)),
        check_vma=False,
    )
```

```python
import functools

import jax
import jax.numpy as jnp
from jax import lax
from jax.experimental import pallas as pl
from jax.experimental.pallas import tpu as pltpu
from jax.sharding import PartitionSpec as P

MASKED = -1000000000.0
LANES = 128
SUB = 8
FIELDS = 4
BLOCKS = 16
ALIGN = 8
SLOTS = 4
MIB = 1 << 20


def transposed_by_eye(row):
    size = row.shape[1]
    down = lax.broadcasted_iota(jnp.int32, (size, size), 0)
    across = lax.broadcasted_iota(jnp.int32, (size, size), 1)
    return jnp.sum(jnp.where(down == across, row, 0.0), axis=1, keepdims=True)


def one_row(rows):
    return jnp.concatenate([rows[index : index + 1, :] for index in range(rows.shape[0])], axis=1)


def slots_kernel(pass_dev, capacity, cand_ref, slots_ref, target_ref):
    per_device = cand_ref.shape[0]
    ids = one_row(cand_ref[...])
    pairs = ids.shape[1]
    owners = jnp.right_shift(ids, pass_dev.bit_length() - 1)
    earlier = lax.broadcasted_iota(jnp.int32, (pairs, pairs), 0) < lax.broadcasted_iota(
        jnp.int32, (pairs, pairs), 1
    )
    named = owners.astype(jnp.float32)
    same = transposed_by_eye(named) == named
    slots = jnp.sum(jnp.where(same & earlier, 1.0, 0.0), axis=0, keepdims=True).astype(jnp.int32)
    target_ref[...] = owners * capacity + slots
    query = lax.broadcasted_iota(jnp.int32, ids.shape, 1) // (pairs // per_device)
    tagged = (jnp.bitwise_and(ids, pass_dev - 1) * per_device + query + 1).astype(jnp.float32)
    down = lax.broadcasted_iota(jnp.int32, (slots_ref.shape[0], pairs), 0)
    lane = lax.broadcasted_iota(jnp.int32, slots_ref.shape, 1)
    found = jnp.zeros(slots_ref.shape, jnp.float32)
    for slot in range(capacity):
        chosen = jnp.where((down == owners) & (slots == slot), tagged, 0.0)
        found = jnp.where(lane == slot, jnp.sum(chosen, axis=1, keepdims=True), found)
    slots_ref[...] = found.astype(jnp.int32)


def slots_by_owner(cand, devices, pass_dev, capacity):
    vmem = pl.BlockSpec(memory_space=pltpu.VMEM)
    return pl.pallas_call(
        functools.partial(slots_kernel, pass_dev, capacity),
        in_specs=[vmem],
        out_specs=[vmem] * 2,
        out_shape=[
            jax.ShapeDtypeStruct((devices, capacity), jnp.int32),
            jax.ShapeDtypeStruct((1, cand.size), jnp.int32),
        ],
        name="slots_by_owner",
    )(cand)


def score_kernel(
    sizes,
    me_ref,
    ids,
    own_ref,
    levels_ref,
    cent_hbm,
    words_hbm,
    codes_hbm,
    lens_hbm,
    *rest,
):
    group_count, cent_count, per_device, query_len, capacity, pass_dev, cand_count = sizes
    query_hbm = rest[:group_count]
    (out_ref, staged, table, words, query_rows, query_t, own_t, dense, embed, maxima, codes, word_stage,
     code_stage, *more) = rest[group_count:]
    code_slots, more = more[:SLOTS], more[SLOTS:]
    (lens, work, work_quad, item_pass, item_len, item_lane, table_sem, words_sem, query_sem, small_sem,
     slot_sem) = more
    sources = ids.shape[0]
    items = sources * capacity
    tiles = words.shape[1] // SUB
    tile_tokens = SUB * FIELDS
    quad_sources = LANES // (per_device * query_len)
    quads = sources // quad_sources
    group_quads = cent_count // quad_sources
    per_bits = per_device.bit_length() - 1
    tile_bits = tiles.bit_length() - 1
    part_rows = staged.shape[0] // quads
    word_parts = words_sem.shape[0]
    part_pass = pass_dev // word_parts

    def table_copy(part):
        rows = pl.ds(pl.multiple_of(part * part_rows, part_rows), part_rows)
        return pltpu.make_async_copy(cent_hbm.at[rows, :], staged.at[rows, :], table_sem.at[part])

    def words_copy(part):
        rows = pl.ds(part * part_pass, part_pass)
        return pltpu.make_async_copy(words_hbm.at[rows], words.at[rows], words_sem.at[part])

    def start_table(part, carry):
        table_copy(part).start()
        return carry

    group = jnp.bitwise_and(me_ref[0], group_count - 1)

    def query_copy(apart):
        return pltpu.make_async_copy(
            query_hbm[apart], query_rows.at[jnp.bitwise_xor(group, apart)], query_sem.at[apart]
        )

    lens_copy = pltpu.make_async_copy(lens_hbm, lens, small_sem.at[0])
    codes_copy = pltpu.make_async_copy(codes_hbm, codes, small_sem.at[1])
    lens_copy.start()
    for apart in range(group_count):
        query_copy(apart).start()
    lax.fori_loop(0, quads, start_table, 0)
    codes_copy.start()
    for part in range(word_parts):
        words_copy(part).start()

    maxima[...] = jnp.full(maxima.shape, MASKED, jnp.float32)
    own_t[...] = jnp.transpose(own_ref[...].astype(jnp.float32)).astype(jnp.bfloat16)
    lens_copy.wait()
    for apart in range(group_count):
        query_copy(apart).wait()

    item_pass[items] = 0
    item_len[items] = 0
    item_lane[items] = -1
    spare = items * tiles

    def prepare(quad, carry):
        count, best = carry
        table_copy(quad).wait()
        rows = pl.ds(pl.multiple_of(quad * part_rows, part_rows), part_rows)
        scores = jnp.dot(staged[rows, :], own_t[...], preferred_element_type=jnp.float32)
        best = jnp.maximum(best, jnp.max(scores.reshape(part_rows // SUB, SUB, scores.shape[1]), axis=0))
        table[rows, :] = staged[rows, :].astype(jnp.float32)
        block = query_rows[quad // group_quads, pl.ds(quad % group_quads * LANES, LANES), :]
        query_t[quad] = jnp.transpose(block.astype(jnp.float32)).astype(jnp.bfloat16)
        start = count
        found = []
        for part in range(quad_sources):
            cent = quad % group_quads * quad_sources + part
            source = cent * group_count + quad // group_quads
            found += [(part, source * capacity + slot, ids[source, slot] - 1) for slot in range(capacity)]
        found = [(part, item, tag, jnp.maximum(tag, 0)) for part, item, tag in found]
        lengths = [lens[jnp.right_shift(held, per_bits)] for _, _, _, held in found]
        for (part, item, tag, held), length in zip(found, lengths):
            item_pass[item] = jnp.right_shift(held, per_bits)
            item_len[item] = length
            item_lane[item] = part * per_device + jnp.bitwise_and(held, per_device - 1)
            for tile in range(tiles):
                work[count + tile] = item * tiles + tile
            blocks = jnp.right_shift(length + tile_tokens - 1, tile_tokens.bit_length() - 1)
            count = count + jnp.where(tag >= 0, blocks, 0)
        for index in range(ALIGN):
            work[count + index] = spare
        count = (count + ALIGN - 1) // ALIGN * ALIGN
        for index in range(quad_sources * capacity * tiles // ALIGN):
            work_quad[start // ALIGN + index] = quad
        return count, best

    lowest = jnp.full((SUB, own_t.shape[1]), -jnp.inf, jnp.float32)
    total, token_best = lax.fori_loop(0, quads, prepare, (0, lowest))
    token_best = jnp.max(token_best, axis=0, keepdims=True)
    for index in range((SLOTS + 1) * BLOCKS):
        work[total + index] = spare
    for index in range(2 * BLOCKS // ALIGN):
        work_quad[total // ALIGN + index] = 0
    chunks = jnp.maximum((total + BLOCKS - 1) // BLOCKS, 2)
    codes_copy.wait()
    for part in range(word_parts):
        words_copy(part).wait()

    sub = lax.broadcasted_iota(jnp.int32, (SUB, LANES), 0)
    position = jnp.concatenate([sub * FIELDS + field for field in range(FIELDS)], axis=0)
    row_blocks = LANES // tile_tokens
    lane_tile = lax.broadcasted_iota(jnp.int32, (1, LANES), 1) // tile_tokens
    lane_group = lax.broadcasted_iota(jnp.int32, (1, LANES), 1) // query_len
    level = [levels_ref[index : index + 1, :] for index in range(FIELDS)]

    def score(chunk):
        scores = []
        for part in range(BLOCKS // ALIGN):
            rows = embed[part * ALIGN * tile_tokens : (part + 1) * ALIGN * tile_tokens, :]
            quad = work_quad[chunk * (BLOCKS // ALIGN) + part]
            scores.append(jnp.dot(rows, query_t[quad], preferred_element_type=jnp.float32))
        for index in range(BLOCKS):
            entry = work[chunk * BLOCKS + index]
            item, tile = jnp.right_shift(entry, tile_bits), jnp.bitwise_and(entry, tiles - 1)
            inner = index % ALIGN
            block = scores[index // ALIGN][inner * tile_tokens : (inner + 1) * tile_tokens]
            kept = jnp.where(position < item_len[item] - tile * tile_tokens, block, MASKED)
            best = jnp.max(kept, axis=0, keepdims=True)
            maxima[tile, pl.ds(item, 1), :] = jnp.where(lane_group == item_lane[item], best, 0.0)

    def slot_copy(slot):
        return pltpu.make_async_copy(code_stage.at[slot], code_slots[slot], slot_sem.at[slot])

    def fetch(chunk, slot):
        for row in range(BLOCKS // row_blocks):
            together = jnp.zeros((1, LANES), jnp.int32)
            for index in range(row_blocks):
                block = row * row_blocks + index
                entry = work[chunk * BLOCKS + block]
                passage = item_pass[jnp.right_shift(entry, tile_bits)]
                tile = jnp.bitwise_and(entry, tiles - 1)
                shift = jnp.bitwise_and(index - tile, row_blocks - 1) * tile_tokens
                moved = pltpu.roll(codes[pl.ds(passage, 1), :], shift, 1)
                together = jnp.where(lane_tile == index, moved, together)
                rows = pl.ds(pl.multiple_of(tile * SUB, SUB), SUB)
                word_stage[slot, block * SUB : (block + 1) * SUB, :] = words[passage, rows, :]
            code_stage[slot, row : row + 1, :] = together

    def decode(slot):
        for index in range(BLOCKS):
            word = word_stage[slot, index * SUB : (index + 1) * SUB, :]
            for field in range(FIELDS):
                rows = jnp.zeros((SUB, LANES), jnp.float32)
                for row in range(SUB):
                    place = index % row_blocks * tile_tokens + row * FIELDS + field
                    code = code_slots[slot][index // row_blocks, place]
                    rows = jnp.where(sub == row, table[pl.ds(code, SUB, stride=0), :], rows)
                low = jnp.bitwise_and(word, 1 << (2 * field)) != 0
                high = jnp.bitwise_and(word, 2 << (2 * field)) != 0
                residual = jnp.where(
                    high, jnp.where(low, level[3], level[2]), jnp.where(low, level[1], level[0])
                )
                base = index * tile_tokens + field * SUB
                dense[base : base + SUB, :] = rows + residual

    def normalize():
        for index in range(BLOCKS):
            rows = slice(index * tile_tokens, (index + 1) * tile_tokens)
            block = dense[rows, :]
            inverse = lax.rsqrt(jnp.sum(block * block, axis=1, keepdims=True) + 1e-06)
            embed[rows, :] = (block * inverse).astype(jnp.bfloat16)

    dense[...] = jnp.zeros(dense.shape, dense.dtype)
    embed[...] = jnp.zeros(embed.shape, embed.dtype)
    for slot in range(SLOTS):
        fetch(slot, slot)
        if slot < SLOTS - 1:
            slot_copy(slot).start()

    def step(group, carry):
        for slot in range(SLOTS):
            chunk = SLOTS * group + slot
            slot_copy(slot).wait()
            slot_copy((slot + SLOTS - 1) % SLOTS).start()

            @pl.when(chunk < chunks)
            def _(chunk=chunk, slot=slot):
                score(jnp.maximum(chunk - 2, 0))
                normalize()
                decode(slot)
                fetch(chunk + SLOTS, slot)

        return carry

    lax.fori_loop(0, (chunks + SLOTS - 1) // SLOTS, step, 0)
    for slot in range(SLOTS - 1):
        slot_copy(slot).wait()
    score(chunks - 2)
    normalize()
    score(chunks - 1)

    best = maxima[0, :items, :]
    for tile in range(1, tiles):
        best = jnp.maximum(best, maxima[tile, :items, :])
    sums = jnp.sum(best, axis=1, keepdims=True) / query_len
    item_down = lax.broadcasted_iota(jnp.int32, (items, LANES), 0)
    item_slot = lax.broadcasted_iota(jnp.int32, (items, LANES), 1)
    spread = jnp.where(item_down % capacity == item_slot, sums, 0.0)
    source_down = lax.broadcasted_iota(jnp.int32, (sources, items), 0)
    item_across = lax.broadcasted_iota(jnp.int32, (sources, items), 1)
    gather = (item_across // capacity == source_down).astype(jnp.float32)
    by_source = jnp.dot(
        gather, spread, precision=lax.Precision.HIGHEST, preferred_element_type=jnp.float32
    )
    best_lanes = token_best.shape[1]
    for source in range(sources):
        out_ref[source, :, :best_lanes] = token_best
        out_ref[source, :, best_lanes:] = by_source[source : source + 1, :]


def owner_scores(me, slots, query_parts, centroids, token_codes, resid_words, lengths, levels, sizes):
    capacity = sizes[4]
    sources = slots.shape[0]
    group_count = len(query_parts)
    group_rows = query_parts[0].shape[0]
    cent_dev, width = centroids.shape
    pass_dev, plen = token_codes.shape
    packed = resid_words.shape[1]
    tiles = packed // SUB
    items = sources * capacity
    quads = group_count * group_rows // LANES
    work_size = items * tiles + quads * ALIGN + (SLOTS + 1) * BLOCKS
    any_space = pl.BlockSpec(memory_space=pl.ANY)
    vmem = pl.BlockSpec(memory_space=pltpu.VMEM)
    tokens = items * plen
    return pl.pallas_call(
        functools.partial(score_kernel, sizes),
        in_specs=[pl.BlockSpec(memory_space=pltpu.SMEM)] * 2 + [vmem, vmem] + [any_space] * (4 + group_count),
        out_specs=vmem,
        out_shape=jax.ShapeDtypeStruct((sources, 1, group_rows + LANES), jnp.float32),
        scratch_shapes=[
            pltpu.VMEM((cent_dev, width), jnp.bfloat16),
            pltpu.VMEM((cent_dev + SUB, width), jnp.float32),
            pltpu.VMEM((pass_dev, packed, width), jnp.int32),
            pltpu.VMEM((group_count, group_rows, width), jnp.bfloat16),
            pltpu.VMEM((quads, width, LANES), jnp.bfloat16),
            pltpu.VMEM((width, group_rows), jnp.bfloat16),
            pltpu.VMEM((BLOCKS * SUB * FIELDS, width), jnp.float32),
            pltpu.VMEM((BLOCKS * SUB * FIELDS, width), jnp.bfloat16),
            pltpu.VMEM((tiles, items + SUB, LANES), jnp.float32),
            pltpu.VMEM((pass_dev, plen), jnp.int32),
            pltpu.VMEM((SLOTS, BLOCKS * SUB, LANES), jnp.int32),
            pltpu.VMEM((SLOTS, BLOCKS * SUB * FIELDS // LANES, LANES), jnp.int32),
            *[pltpu.SMEM((BLOCKS * SUB * FIELDS // LANES, LANES), jnp.int32)] * SLOTS,
            pltpu.SMEM((pass_dev,), jnp.int32),
            pltpu.SMEM((work_size,), jnp.int32),
            pltpu.SMEM((work_size // ALIGN + items * tiles // quads,), jnp.int32),
            pltpu.SMEM((items + 1,), jnp.int32),
            pltpu.SMEM((items + 1,), jnp.int32),
            pltpu.SMEM((items + 1,), jnp.int32),
            pltpu.SemaphoreType.DMA((quads,)),
            pltpu.SemaphoreType.DMA((4,)),
            pltpu.SemaphoreType.DMA((group_count,)),
            pltpu.SemaphoreType.DMA((2,)),
            pltpu.SemaphoreType.DMA((SLOTS,)),
        ],
        compiler_params=pltpu.CompilerParams(vmem_limit_bytes=56 * MIB),
        cost_estimate=pl.CostEstimate(
            flops=2 * (tokens * LANES + cent_dev * group_rows) * width, bytes_accessed=2 * cent_dev * width * 2, transcendentals=tokens
        ),
        name="owner_scores",
    )(
        me, slots, query_parts[0], levels, centroids, resid_words, token_codes, lengths, *query_parts
    )


def finish_kernel(sizes, me_ref, back_ref, target_ref, best_out, score_out):
    group_count, cent_count, _, query_len, capacity, _, _ = sizes
    group = jnp.bitwise_and(me_ref[0], group_count - 1)
    best_lanes = best_out.shape[0] * query_len
    best = back_ref[group, :, :best_lanes]
    for cent in range(1, cent_count):
        best = jnp.maximum(best, back_ref[cent * group_count + group, :, :best_lanes])
    for index in range(best_out.shape[0]):
        best_out[index : index + 1, :] = best[:, index * query_len : (index + 1) * query_len]
    back = back_ref[:, 0, best_lanes:]
    target = target_ref[...]
    owner = lax.broadcasted_iota(jnp.int32, (back.shape[0], target.shape[1]), 0)
    found = jnp.zeros(owner.shape, jnp.float32)
    for slot in range(capacity):
        found = found + jnp.where(owner * capacity + slot == target, back[:, slot : slot + 1], 0.0)
    scores = jnp.sum(found, axis=0, keepdims=True)
    width = score_out.shape[1]
    for index in range(score_out.shape[0]):
        score_out[index : index + 1, :] = scores[:, index * width : (index + 1) * width]


def finish(me, back, target, group_rows, sizes):
    _, _, per_device, query_len, _, _, cand_count = sizes
    vmem = pl.BlockSpec(memory_space=pltpu.VMEM)
    return pl.pallas_call(
        functools.partial(finish_kernel, sizes),
        in_specs=[pl.BlockSpec(memory_space=pltpu.SMEM), vmem, vmem],
        out_specs=[vmem] * 2,
        out_shape=[
            jax.ShapeDtypeStruct((group_rows, query_len), jnp.float32),
            jax.ShapeDtypeStruct((per_device, cand_count), jnp.float32),
        ],
        name="finish",
    )(me, back, target)


def shards(queries, centroids, candidates, token_codes, resid_words, lengths, levels):
    group_rows, query_len, width = queries.shape
    pass_dev = token_codes.shape[0]
    per_device, cand_count = candidates.shape[2:]
    pair_count = per_device * cand_count
    cent_count = lax.axis_size("cent")
    group_count = lax.axis_size("grp")
    devices = cent_count * group_count
    capacity = max(2, 2 * pair_count // devices)
    sizes = (group_count, cent_count, per_device, query_len, capacity, pass_dev, cand_count)
    cand = candidates.reshape(per_device, cand_count)
    query_rows = queries.reshape(group_rows * query_len, width)
    me = (lax.axis_index("cent") * group_count + lax.axis_index("grp")).astype(jnp.int32).reshape(1)
    slots, target = slots_by_owner(cand, devices, pass_dev, capacity)
    slots = lax.all_to_all(slots, ("cent", "grp"), split_axis=0, concat_axis=0, tiled=True)
    query_parts = [query_rows]
    for apart in range(1, group_count):
        pairs = [(index, index ^ apart) for index in range(group_count)]
        query_parts.append(lax.ppermute(query_rows, "grp", pairs))
    reply = owner_scores(
        me, slots, query_parts, centroids, token_codes, resid_words, lengths, levels, sizes
    )
    back = lax.all_to_all(reply, ("cent", "grp"), split_axis=0, concat_axis=0, tiled=True)
    token_best, scores = finish(me, back, target, group_rows, sizes)
    return (token_best, scores.reshape(1, 1, per_device, cand_count))


def solution(mesh):
    placed = (
        P("grp", None, None),
        P("cent", None),
        P("grp", "cent", None, None),
        P(("cent", "grp"), None),
        P(("cent", "grp"), None, None),
        P(("cent", "grp")),
        P(),
    )
    return jax.shard_map(
        shards,
        mesh=mesh,
        in_specs=placed,
        out_specs=(P("grp", None), P("grp", "cent", None, None)),
        check_vma=False,
    )
```

```python
import functools

import jax
import jax.numpy as jnp
from jax import lax
from jax.experimental import pallas as pl
from jax.experimental.pallas import tpu as pltpu
from jax.sharding import PartitionSpec as P

MASKED = -1000000000.0
LANES = 128
SUB = 8
FIELDS = 4
BLOCKS = 16
ALIGN = 8
SLOTS = 4
PARTS = 8
MIB = 1 << 20


def transposed_by_eye(row):
    size = row.shape[1]
    down = lax.broadcasted_iota(jnp.int32, (size, size), 0)
    across = lax.broadcasted_iota(jnp.int32, (size, size), 1)
    return jnp.sum(jnp.where(down == across, row, 0.0), axis=1, keepdims=True)


def one_row(rows):
    return jnp.concatenate([rows[index : index + 1, :] for index in range(rows.shape[0])], axis=1)


def slots_kernel(pass_dev, capacity, cand_ref, slots_ref, target_ref):
    per_device = cand_ref.shape[0]
    ids = one_row(cand_ref[...])
    pairs = ids.shape[1]
    owners = jnp.right_shift(ids, pass_dev.bit_length() - 1)
    earlier = lax.broadcasted_iota(jnp.int32, (pairs, pairs), 0) < lax.broadcasted_iota(
        jnp.int32, (pairs, pairs), 1
    )
    named = owners.astype(jnp.float32)
    same = transposed_by_eye(named) == named
    slots = jnp.sum(jnp.where(same & earlier, 1.0, 0.0), axis=0, keepdims=True).astype(jnp.int32)
    target_ref[...] = owners * capacity + slots
    query = lax.broadcasted_iota(jnp.int32, ids.shape, 1) // (pairs // per_device)
    tagged = (jnp.bitwise_and(ids, pass_dev - 1) * per_device + query + 1).astype(jnp.float32)
    down = lax.broadcasted_iota(jnp.int32, (slots_ref.shape[0], pairs), 0)
    lane = lax.broadcasted_iota(jnp.int32, slots_ref.shape, 1)
    found = jnp.zeros(slots_ref.shape, jnp.float32)
    for slot in range(capacity):
        chosen = jnp.where((down == owners) & (slots == slot), tagged, 0.0)
        found = jnp.where(lane == slot, jnp.sum(chosen, axis=1, keepdims=True), found)
    slots_ref[...] = found.astype(jnp.int32)


def slots_by_owner(cand, devices, pass_dev, capacity):
    vmem = pl.BlockSpec(memory_space=pltpu.VMEM)
    return pl.pallas_call(
        functools.partial(slots_kernel, pass_dev, capacity),
        in_specs=[vmem],
        out_specs=[vmem] * 2,
        out_shape=[
            jax.ShapeDtypeStruct((devices, capacity), jnp.int32),
            jax.ShapeDtypeStruct((1, cand.size), jnp.int32),
        ],
        name="slots_by_owner",
    )(cand)


def score_kernel(
    sizes,
    me_ref,
    ids,
    own_ref,
    levels_ref,
    cent_hbm,
    words_hbm,
    codes_hbm,
    lens_hbm,
    *rest,
):
    group_count, cent_count, per_device, query_len, capacity, pass_dev, cand_count = sizes
    query_hbm = rest[:group_count]
    (out_ref, staged, table, words, query_rows, query_t, own_t, dense, embed, maxima, codes, word_stage,
     code_stage, *more) = rest[group_count:]
    code_slots, more = more[:SLOTS], more[SLOTS:]
    (lens, work, work_quad, item_pass, item_len, item_lane, table_sem, words_sem, query_sem, small_sem,
     slot_sem) = more
    sources = ids.shape[0]
    items = sources * capacity
    tiles = words.shape[1] // SUB
    tile_tokens = SUB * FIELDS
    quad_sources = LANES // (per_device * query_len)
    quads = sources // quad_sources
    group_quads = cent_count // quad_sources
    per_bits = per_device.bit_length() - 1
    tile_bits = tiles.bit_length() - 1
    parts = min(quads, PARTS)
    part_rows = staged.shape[0] // parts
    part_quads = quads // parts
    word_parts = words_sem.shape[0]
    part_pass = pass_dev // word_parts

    def table_copy(part):
        rows = pl.ds(pl.multiple_of(part * part_rows, part_rows), part_rows)
        return pltpu.make_async_copy(cent_hbm.at[rows, :], staged.at[rows, :], table_sem.at[part])

    def words_copy(part):
        rows = pl.ds(part * part_pass, part_pass)
        return pltpu.make_async_copy(words_hbm.at[rows], words.at[rows], words_sem.at[part])

    def start_table(part, carry):
        table_copy(part).start()
        return carry

    group = jnp.bitwise_and(me_ref[0], group_count - 1)

    def query_copy(apart):
        return pltpu.make_async_copy(
            query_hbm[apart], query_rows.at[jnp.bitwise_xor(group, apart)], query_sem.at[apart]
        )

    lens_copy = pltpu.make_async_copy(lens_hbm, lens, small_sem.at[0])
    codes_copy = pltpu.make_async_copy(codes_hbm, codes, small_sem.at[1])
    lens_copy.start()
    for apart in range(group_count):
        query_copy(apart).start()
    lax.fori_loop(0, parts, start_table, 0)
    codes_copy.start()
    for part in range(word_parts):
        words_copy(part).start()

    maxima[...] = jnp.full(maxima.shape, MASKED, jnp.float32)
    own_t[...] = jnp.transpose(own_ref[...].astype(jnp.float32)).astype(jnp.bfloat16)
    lens_copy.wait()
    for apart in range(group_count):
        query_copy(apart).wait()

    item_pass[items] = 0
    item_len[items] = 0
    item_lane[items] = -1
    spare = items * tiles

    def fill(quad, count):
        block = query_rows[quad // group_quads, pl.ds(quad % group_quads * LANES, LANES), :]
        query_t[quad] = jnp.transpose(block.astype(jnp.float32)).astype(jnp.bfloat16)
        start = count
        found = []
        for part in range(quad_sources):
            cent = quad % group_quads * quad_sources + part
            source = cent * group_count + quad // group_quads
            found += [(part, source * capacity + slot, ids[source, slot] - 1) for slot in range(capacity)]
        found = [(part, item, tag, jnp.maximum(tag, 0)) for part, item, tag in found]
        lengths = [lens[jnp.right_shift(held, per_bits)] for _, _, _, held in found]
        for (part, item, tag, held), length in zip(found, lengths):
            item_pass[item] = jnp.right_shift(held, per_bits)
            item_len[item] = length
            item_lane[item] = part * per_device + jnp.bitwise_and(held, per_device - 1)
            for tile in range(tiles):
                work[count + tile] = item * tiles + tile
            blocks = jnp.right_shift(length + tile_tokens - 1, tile_tokens.bit_length() - 1)
            count = count + jnp.where(tag >= 0, blocks, 0)
        for index in range(ALIGN):
            work[count + index] = spare
        count = (count + ALIGN - 1) // ALIGN * ALIGN
        for index in range(quad_sources * capacity * tiles // ALIGN):
            work_quad[start // ALIGN + index] = quad
        return count

    def prepare(part, carry):
        count, best = carry
        table_copy(part).wait()
        rows = pl.ds(pl.multiple_of(part * part_rows, part_rows), part_rows)
        scores = jnp.dot(staged[rows, :], own_t[...], preferred_element_type=jnp.float32)
        best = jnp.maximum(best, jnp.max(scores.reshape(part_rows // SUB, SUB, scores.shape[1]), axis=0))
        table[rows, :] = staged[rows, :].astype(jnp.float32)
        for index in range(part_quads):
            count = fill(part * part_quads + index, count)
        return count, best

    lowest = jnp.full((SUB, own_t.shape[1]), -jnp.inf, jnp.float32)
    total, token_best = lax.fori_loop(0, parts, prepare, (0, lowest))
    token_best = jnp.max(token_best, axis=0, keepdims=True)
    for index in range((SLOTS + 1) * BLOCKS):
        work[total + index] = spare
    for index in range(2 * BLOCKS // ALIGN):
        work_quad[total // ALIGN + index] = 0
    chunks = jnp.maximum((total + BLOCKS - 1) // BLOCKS, 2)
    codes_copy.wait()
    for part in range(word_parts):
        words_copy(part).wait()

    sub = lax.broadcasted_iota(jnp.int32, (SUB, LANES), 0)
    position = jnp.concatenate([sub * FIELDS + field for field in range(FIELDS)], axis=0)
    row_blocks = LANES // tile_tokens
    lane_tile = lax.broadcasted_iota(jnp.int32, (1, LANES), 1) // tile_tokens
    lane_group = lax.broadcasted_iota(jnp.int32, (1, LANES), 1) // query_len
    level = [levels_ref[index : index + 1, :] for index in range(FIELDS)]

    def score(chunk):
        scores = []
        for part in range(BLOCKS // ALIGN):
            rows = embed[part * ALIGN * tile_tokens : (part + 1) * ALIGN * tile_tokens, :]
            quad = work_quad[chunk * (BLOCKS // ALIGN) + part]
            scores.append(jnp.dot(rows, query_t[quad], preferred_element_type=jnp.float32))
        for index in range(BLOCKS):
            entry = work[chunk * BLOCKS + index]
            item, tile = jnp.right_shift(entry, tile_bits), jnp.bitwise_and(entry, tiles - 1)
            inner = index % ALIGN
            block = scores[index // ALIGN][inner * tile_tokens : (inner + 1) * tile_tokens]
            kept = jnp.where(position < item_len[item] - tile * tile_tokens, block, MASKED)
            best = jnp.max(kept, axis=0, keepdims=True)
            maxima[tile, pl.ds(item, 1), :] = jnp.where(lane_group == item_lane[item], best, 0.0)

    def slot_copy(slot):
        return pltpu.make_async_copy(code_stage.at[slot], code_slots[slot], slot_sem.at[slot])

    def fetch(chunk, slot):
        for row in range(BLOCKS // row_blocks):
            together = jnp.zeros((1, LANES), jnp.int32)
            for index in range(row_blocks):
                block = row * row_blocks + index
                entry = work[chunk * BLOCKS + block]
                passage = item_pass[jnp.right_shift(entry, tile_bits)]
                tile = jnp.bitwise_and(entry, tiles - 1)
                shift = jnp.bitwise_and(index - tile, row_blocks - 1) * tile_tokens
                moved = pltpu.roll(codes[pl.ds(passage, 1), :], shift, 1)
                together = jnp.where(lane_tile == index, moved, together)
                rows = pl.ds(pl.multiple_of(tile * SUB, SUB), SUB)
                word_stage[slot, block * SUB : (block + 1) * SUB, :] = words[passage, rows, :]
            code_stage[slot, row : row + 1, :] = together

    def decode(slot):
        for index in range(BLOCKS):
            word = word_stage[slot, index * SUB : (index + 1) * SUB, :]
            for field in range(FIELDS):
                rows = jnp.zeros((SUB, LANES), jnp.float32)
                for row in range(SUB):
                    place = index % row_blocks * tile_tokens + row * FIELDS + field
                    code = code_slots[slot][index // row_blocks, place]
                    rows = jnp.where(sub == row, table[pl.ds(code, SUB, stride=0), :], rows)
                low = jnp.bitwise_and(word, 1 << (2 * field)) != 0
                high = jnp.bitwise_and(word, 2 << (2 * field)) != 0
                residual = jnp.where(
                    high, jnp.where(low, level[3], level[2]), jnp.where(low, level[1], level[0])
                )
                base = index * tile_tokens + field * SUB
                dense[base : base + SUB, :] = rows + residual

    def normalize():
        for index in range(BLOCKS):
            rows = slice(index * tile_tokens, (index + 1) * tile_tokens)
            block = dense[rows, :]
            inverse = lax.rsqrt(jnp.sum(block * block, axis=1, keepdims=True) + 1e-06)
            embed[rows, :] = (block * inverse).astype(jnp.bfloat16)

    dense[...] = jnp.zeros(dense.shape, dense.dtype)
    embed[...] = jnp.zeros(embed.shape, embed.dtype)
    for slot in range(SLOTS):
        fetch(slot, slot)
        if slot < 2:
            slot_copy(slot).start()
        elif slot < SLOTS - 1:
            pl.when(slot < chunks)(slot_copy(slot).start)

    def step(group, carry):
        for slot in range(SLOTS):
            chunk = SLOTS * group + slot
            pl.when(chunk + SLOTS - 1 < chunks)(slot_copy((slot + SLOTS - 1) % SLOTS).start)

            @pl.when(chunk < chunks)
            def _(chunk=chunk, slot=slot):
                slot_copy(slot).wait()
                score(jnp.maximum(chunk - 2, 0))
                normalize()
                decode(slot)
                fetch(chunk + SLOTS, slot)

        return carry

    lax.fori_loop(0, (chunks + SLOTS - 1) // SLOTS, step, 0)
    score(chunks - 2)
    normalize()
    score(chunks - 1)

    best = maxima[0, :items, :]
    for tile in range(1, tiles):
        best = jnp.maximum(best, maxima[tile, :items, :])
    sums = jnp.sum(best, axis=1, keepdims=True) / query_len
    item_down = lax.broadcasted_iota(jnp.int32, (items, LANES), 0)
    item_slot = lax.broadcasted_iota(jnp.int32, (items, LANES), 1)
    spread = jnp.where(item_down % capacity == item_slot, sums, 0.0)
    source_down = lax.broadcasted_iota(jnp.int32, (sources, items), 0)
    item_across = lax.broadcasted_iota(jnp.int32, (sources, items), 1)
    gather = (item_across // capacity == source_down).astype(jnp.float32)
    by_source = jnp.dot(
        gather, spread, precision=lax.Precision.HIGHEST, preferred_element_type=jnp.float32
    )
    best_lanes = token_best.shape[1]
    for source in range(sources):
        out_ref[source, :, :best_lanes] = token_best
        out_ref[source, :, best_lanes:] = by_source[source : source + 1, :]


def owner_scores(me, slots, query_parts, centroids, token_codes, resid_words, lengths, levels, sizes):
    capacity = sizes[4]
    sources = slots.shape[0]
    group_count = len(query_parts)
    group_rows = query_parts[0].shape[0]
    cent_dev, width = centroids.shape
    pass_dev, plen = token_codes.shape
    packed = resid_words.shape[1]
    tiles = packed // SUB
    items = sources * capacity
    quads = group_count * group_rows // LANES
    work_size = items * tiles + quads * ALIGN + (SLOTS + 1) * BLOCKS
    any_space = pl.BlockSpec(memory_space=pl.ANY)
    in_hbm = pl.BlockSpec(memory_space=pltpu.HBM)
    pinned = [
        pltpu.with_memory_space_constraint(array, pltpu.HBM)
        for array in (centroids, resid_words, token_codes, lengths)
    ]
    vmem = pl.BlockSpec(memory_space=pltpu.VMEM)
    tokens = items * plen
    return pl.pallas_call(
        functools.partial(score_kernel, sizes),
        in_specs=[pl.BlockSpec(memory_space=pltpu.SMEM)] * 2 + [vmem, vmem] + [in_hbm] * 4 + [any_space] * group_count,
        out_specs=vmem,
        out_shape=jax.ShapeDtypeStruct((sources, 1, group_rows + LANES), jnp.float32),
        scratch_shapes=[
            pltpu.VMEM((cent_dev, width), jnp.bfloat16),
            pltpu.VMEM((cent_dev + SUB, width), jnp.float32),
            pltpu.VMEM((pass_dev, packed, width), jnp.int32),
            pltpu.VMEM((group_count, group_rows, width), jnp.bfloat16),
            pltpu.VMEM((quads, width, LANES), jnp.bfloat16),
            pltpu.VMEM((width, group_rows), jnp.bfloat16),
            pltpu.VMEM((BLOCKS * SUB * FIELDS, width), jnp.float32),
            pltpu.VMEM((BLOCKS * SUB * FIELDS, width), jnp.bfloat16),
            pltpu.VMEM((tiles, items + SUB, LANES), jnp.float32),
            pltpu.VMEM((pass_dev, plen), jnp.int32),
            pltpu.VMEM((SLOTS, BLOCKS * SUB, LANES), jnp.int32),
            pltpu.VMEM((SLOTS, BLOCKS * SUB * FIELDS // LANES, LANES), jnp.int32),
            *[pltpu.SMEM((BLOCKS * SUB * FIELDS // LANES, LANES), jnp.int32)] * SLOTS,
            pltpu.SMEM((pass_dev,), jnp.int32),
            pltpu.SMEM((work_size,), jnp.int32),
            pltpu.SMEM((work_size // ALIGN + items * tiles // quads,), jnp.int32),
            pltpu.SMEM((items + 1,), jnp.int32),
            pltpu.SMEM((items + 1,), jnp.int32),
            pltpu.SMEM((items + 1,), jnp.int32),
            pltpu.SemaphoreType.DMA((min(quads, PARTS),)),
            pltpu.SemaphoreType.DMA((4,)),
            pltpu.SemaphoreType.DMA((group_count,)),
            pltpu.SemaphoreType.DMA((2,)),
            pltpu.SemaphoreType.DMA((SLOTS,)),
        ],
        compiler_params=pltpu.CompilerParams(vmem_limit_bytes=44 * MIB),
        cost_estimate=pl.CostEstimate(
            flops=2 * (tokens * LANES + cent_dev * group_rows) * width, bytes_accessed=2 * cent_dev * width * 2, transcendentals=tokens
        ),
        name="owner_scores",
    )(
        me, slots, query_parts[0], levels, *pinned, *query_parts
    )


def finish_kernel(sizes, me_ref, back_ref, target_ref, best_out, score_out):
    group_count, cent_count, _, query_len, capacity, _, _ = sizes
    group = jnp.bitwise_and(me_ref[0], group_count - 1)
    best_lanes = best_out.shape[0] * query_len
    best = back_ref[group, :, :best_lanes]
    for cent in range(1, cent_count):
        best = jnp.maximum(best, back_ref[cent * group_count + group, :, :best_lanes])
    for index in range(best_out.shape[0]):
        best_out[index : index + 1, :] = best[:, index * query_len : (index + 1) * query_len]
    back = back_ref[:, 0, best_lanes:]
    target = target_ref[...]
    owner = lax.broadcasted_iota(jnp.int32, (back.shape[0], target.shape[1]), 0)
    found = jnp.zeros(owner.shape, jnp.float32)
    for slot in range(capacity):
        found = found + jnp.where(owner * capacity + slot == target, back[:, slot : slot + 1], 0.0)
    scores = jnp.sum(found, axis=0, keepdims=True)
    width = score_out.shape[1]
    for index in range(score_out.shape[0]):
        score_out[index : index + 1, :] = scores[:, index * width : (index + 1) * width]


def finish(me, back, target, group_rows, sizes):
    _, _, per_device, query_len, _, _, cand_count = sizes
    vmem = pl.BlockSpec(memory_space=pltpu.VMEM)
    return pl.pallas_call(
        functools.partial(finish_kernel, sizes),
        in_specs=[pl.BlockSpec(memory_space=pltpu.SMEM), vmem, vmem],
        out_specs=[vmem] * 2,
        out_shape=[
            jax.ShapeDtypeStruct((group_rows, query_len), jnp.float32),
            jax.ShapeDtypeStruct((per_device, cand_count), jnp.float32),
        ],
        name="finish",
    )(me, back, target)


def shards(queries, centroids, candidates, token_codes, resid_words, lengths, levels):
    group_rows, query_len, width = queries.shape
    pass_dev = token_codes.shape[0]
    per_device, cand_count = candidates.shape[2:]
    pair_count = per_device * cand_count
    cent_count = lax.axis_size("cent")
    group_count = lax.axis_size("grp")
    devices = cent_count * group_count
    capacity = max(2, 2 * pair_count // devices)
    sizes = (group_count, cent_count, per_device, query_len, capacity, pass_dev, cand_count)
    cand = candidates.reshape(per_device, cand_count)
    query_rows = queries.reshape(group_rows * query_len, width)
    me = (lax.axis_index("cent") * group_count + lax.axis_index("grp")).astype(jnp.int32).reshape(1)
    slots, target = slots_by_owner(cand, devices, pass_dev, capacity)
    slots = lax.all_to_all(slots, ("cent", "grp"), split_axis=0, concat_axis=0, tiled=True)
    query_parts = [query_rows]
    for apart in range(1, group_count):
        pairs = [(index, index ^ apart) for index in range(group_count)]
        query_parts.append(lax.ppermute(query_rows, "grp", pairs))
    reply = owner_scores(
        me, slots, query_parts, centroids, token_codes, resid_words, lengths, levels, sizes
    )
    back = lax.all_to_all(reply, ("cent", "grp"), split_axis=0, concat_axis=0, tiled=True)
    token_best, scores = finish(me, back, target, group_rows, sizes)
    return (token_best, scores.reshape(1, 1, per_device, cand_count))


def solution(mesh):
    placed = (
        P("grp", None, None),
        P("cent", None),
        P("grp", "cent", None, None),
        P(("cent", "grp"), None),
        P(("cent", "grp"), None, None),
        P(("cent", "grp")),
        P(),
    )
    return jax.shard_map(
        shards,
        mesh=mesh,
        in_specs=placed,
        out_specs=(P("grp", None), P("grp", "cent", None, None)),
        check_vma=False,
    )
```

```python
import functools

import jax
import jax.numpy as jnp
from jax import lax
from jax.experimental import pallas as pl
from jax.experimental.pallas import tpu as pltpu
from jax.sharding import PartitionSpec as P

MASKED = -1000000000.0
LANES = 128
SUB = 8
FIELDS = 4
BLOCKS = 16
ALIGN = 4
SLOTS = 4
PARTS = 8
MIB = 1 << 20


def transposed_by_eye(row):
    size = row.shape[1]
    down = lax.broadcasted_iota(jnp.int32, (size, size), 0)
    across = lax.broadcasted_iota(jnp.int32, (size, size), 1)
    return jnp.sum(jnp.where(down == across, row, 0.0), axis=1, keepdims=True)


def one_row(rows):
    return jnp.concatenate([rows[index : index + 1, :] for index in range(rows.shape[0])], axis=1)


def slots_kernel(pass_dev, capacity, cand_ref, slots_ref, target_ref):
    per_device = cand_ref.shape[0]
    ids = one_row(cand_ref[...])
    pairs = ids.shape[1]
    owners = jnp.right_shift(ids, pass_dev.bit_length() - 1)
    earlier = lax.broadcasted_iota(jnp.int32, (pairs, pairs), 0) < lax.broadcasted_iota(
        jnp.int32, (pairs, pairs), 1
    )
    named = owners.astype(jnp.float32)
    same = transposed_by_eye(named) == named
    slots = jnp.sum(jnp.where(same & earlier, 1.0, 0.0), axis=0, keepdims=True).astype(jnp.int32)
    target_ref[...] = owners * capacity + slots
    query = lax.broadcasted_iota(jnp.int32, ids.shape, 1) // (pairs // per_device)
    tagged = (jnp.bitwise_and(ids, pass_dev - 1) * per_device + query + 1).astype(jnp.float32)
    down = lax.broadcasted_iota(jnp.int32, (slots_ref.shape[0], pairs), 0)
    lane = lax.broadcasted_iota(jnp.int32, slots_ref.shape, 1)
    found = jnp.zeros(slots_ref.shape, jnp.float32)
    for slot in range(capacity):
        chosen = jnp.where((down == owners) & (slots == slot), tagged, 0.0)
        found = jnp.where(lane == slot, jnp.sum(chosen, axis=1, keepdims=True), found)
    slots_ref[...] = found.astype(jnp.int32)


def slots_by_owner(cand, devices, pass_dev, capacity):
    vmem = pl.BlockSpec(memory_space=pltpu.VMEM)
    return pl.pallas_call(
        functools.partial(slots_kernel, pass_dev, capacity),
        in_specs=[vmem],
        out_specs=[vmem] * 2,
        out_shape=[
            jax.ShapeDtypeStruct((devices, capacity), jnp.int32),
            jax.ShapeDtypeStruct((1, cand.size), jnp.int32),
        ],
        name="slots_by_owner",
    )(cand)


def score_kernel(
    sizes,
    me_ref,
    ids,
    levels_hbm,
    cent_hbm,
    words_hbm,
    codes_hbm,
    lens_hbm,
    *rest,
):
    group_count, cent_count, per_device, query_len, capacity, pass_dev, cand_count = sizes
    query_hbm = rest[:group_count]
    (out_ref, staged, table, words, query_rows, query_t, own_t, dense, embed, maxima, codes, word_stage,
     code_stage, *more) = rest[group_count:]
    code_slots, more = more[:SLOTS], more[SLOTS:]
    (levels_ref, lens, work, work_quad, item_pass, item_len, item_lane, table_sem, words_sem, query_sem, small_sem,
     slot_sem) = more
    sources = ids.shape[0]
    items = sources * capacity
    tiles = words.shape[1] // SUB
    tile_tokens = SUB * FIELDS
    quad_sources = LANES // (per_device * query_len)
    quads = sources // quad_sources
    group_quads = cent_count // quad_sources
    per_bits = per_device.bit_length() - 1
    tile_bits = tiles.bit_length() - 1
    parts = min(quads, PARTS)
    part_rows = staged.shape[0] // parts
    part_quads = quads // parts
    word_parts = words_sem.shape[0]
    part_pass = pass_dev // word_parts

    def table_copy(part):
        rows = pl.ds(pl.multiple_of(part * part_rows, part_rows), part_rows)
        return pltpu.make_async_copy(cent_hbm.at[rows, :], staged.at[rows, :], table_sem.at[part])

    def words_copy(part):
        rows = pl.ds(part * part_pass, part_pass)
        return pltpu.make_async_copy(words_hbm.at[rows], words.at[rows], words_sem.at[part])

    def start_table(part, carry):
        table_copy(part).start()
        return carry

    group = jnp.bitwise_and(me_ref[0], group_count - 1)

    def query_copy(apart):
        return pltpu.make_async_copy(
            query_hbm[apart], query_rows.at[jnp.bitwise_xor(group, apart)], query_sem.at[apart]
        )

    lens_copy = pltpu.make_async_copy(lens_hbm, lens, small_sem.at[0])
    codes_copy = pltpu.make_async_copy(codes_hbm, codes, small_sem.at[1])
    levels_copy = pltpu.make_async_copy(levels_hbm, levels_ref, small_sem.at[2])
    lens_copy.start()
    levels_copy.start()
    for apart in range(group_count):
        query_copy(apart).start()
    lax.fori_loop(0, parts, start_table, 0)
    codes_copy.start()
    for part in range(word_parts):
        words_copy(part).start()

    maxima[...] = jnp.full(maxima.shape, MASKED, jnp.float32)
    query_copy(0).wait()
    own_t[...] = jnp.transpose(query_rows[group].astype(jnp.float32)).astype(jnp.bfloat16)
    lens_copy.wait()
    for apart in range(1, group_count):
        query_copy(apart).wait()

    item_pass[items] = 0
    item_len[items] = 0
    item_lane[items] = -1
    spare = items * tiles

    def fill(quad, count):
        block = query_rows[quad // group_quads, pl.ds(quad % group_quads * LANES, LANES), :]
        query_t[quad] = jnp.transpose(block.astype(jnp.float32)).astype(jnp.bfloat16)
        start = count
        found = []
        for part in range(quad_sources):
            cent = quad % group_quads * quad_sources + part
            source = cent * group_count + quad // group_quads
            found += [(part, source * capacity + slot, ids[source, slot] - 1) for slot in range(capacity)]
        found = [(part, item, tag, jnp.maximum(tag, 0)) for part, item, tag in found]
        lengths = [lens[jnp.right_shift(held, per_bits)] for _, _, _, held in found]
        for (part, item, tag, held), length in zip(found, lengths):
            item_pass[item] = jnp.right_shift(held, per_bits)
            item_len[item] = length
            item_lane[item] = part * per_device + jnp.bitwise_and(held, per_device - 1)
            for tile in range(tiles):
                work[count + tile] = item * tiles + tile
            blocks = jnp.right_shift(length + tile_tokens - 1, tile_tokens.bit_length() - 1)
            count = count + jnp.where(tag >= 0, blocks, 0)
        for index in range(ALIGN):
            work[count + index] = spare
        count = (count + ALIGN - 1) // ALIGN * ALIGN
        for index in range(quad_sources * capacity * tiles // ALIGN):
            work_quad[start // ALIGN + index] = quad
        return count

    def prepare(part, carry):
        count, best = carry
        table_copy(part).wait()
        rows = pl.ds(pl.multiple_of(part * part_rows, part_rows), part_rows)
        scores = jnp.dot(staged[rows, :], own_t[...], preferred_element_type=jnp.float32)
        best = jnp.maximum(best, jnp.max(scores.reshape(part_rows // SUB, SUB, scores.shape[1]), axis=0))
        table[rows, :] = staged[rows, :].astype(jnp.float32)
        for index in range(part_quads):
            count = fill(part * part_quads + index, count)
        return count, best

    lowest = jnp.full((SUB, own_t.shape[1]), -jnp.inf, jnp.float32)
    total, token_best = lax.fori_loop(0, parts, prepare, (0, lowest))
    token_best = jnp.max(token_best, axis=0, keepdims=True)
    for index in range((SLOTS + 1) * BLOCKS):
        work[total + index] = spare
    for index in range(2 * BLOCKS // ALIGN):
        work_quad[total // ALIGN + index] = 0
    chunks = jnp.maximum((total + BLOCKS - 1) // BLOCKS, 2)
    codes_copy.wait()
    levels_copy.wait()
    for part in range(word_parts):
        words_copy(part).wait()

    sub = lax.broadcasted_iota(jnp.int32, (SUB, LANES), 0)
    position = jnp.concatenate([sub * FIELDS + field for field in range(FIELDS)], axis=0)
    row_blocks = LANES // tile_tokens
    lane_tile = lax.broadcasted_iota(jnp.int32, (1, LANES), 1) // tile_tokens
    lane_group = lax.broadcasted_iota(jnp.int32, (1, LANES), 1) // query_len
    level = [levels_ref[index : index + 1, :] for index in range(FIELDS)]

    def score(chunk):
        scores = []
        for part in range(BLOCKS // ALIGN):
            rows = embed[part * ALIGN * tile_tokens : (part + 1) * ALIGN * tile_tokens, :]
            quad = work_quad[chunk * (BLOCKS // ALIGN) + part]
            scores.append(jnp.dot(rows, query_t[quad], preferred_element_type=jnp.float32))
        for index in range(BLOCKS):
            entry = work[chunk * BLOCKS + index]
            item, tile = jnp.right_shift(entry, tile_bits), jnp.bitwise_and(entry, tiles - 1)
            inner = index % ALIGN
            block = scores[index // ALIGN][inner * tile_tokens : (inner + 1) * tile_tokens]
            kept = jnp.where(position < item_len[item] - tile * tile_tokens, block, MASKED)
            best = jnp.max(kept, axis=0, keepdims=True)
            maxima[tile, pl.ds(item, 1), :] = jnp.where(lane_group == item_lane[item], best, 0.0)

    def slot_copy(slot):
        return pltpu.make_async_copy(code_stage.at[slot], code_slots[slot], slot_sem.at[slot])

    def fetch_codes(chunk, slot):
        places = []
        for row in range(BLOCKS // row_blocks):
            together = jnp.zeros((1, LANES), jnp.int32)
            for index in range(row_blocks):
                entry = work[chunk * BLOCKS + row * row_blocks + index]
                passage = item_pass[jnp.right_shift(entry, tile_bits)]
                tile = jnp.bitwise_and(entry, tiles - 1)
                shift = jnp.bitwise_and(index - tile, row_blocks - 1) * tile_tokens
                moved = pltpu.roll(codes[pl.ds(passage, 1), :], shift, 1)
                together = jnp.where(lane_tile == index, moved, together)
                places.append((passage, tile))
            code_stage[slot, row : row + 1, :] = together
        return places

    def fetch_words(places, slot):
        for block, (passage, tile) in enumerate(places):
            rows = pl.ds(pl.multiple_of(tile * SUB, SUB), SUB)
            word_stage[slot, block * SUB : (block + 1) * SUB, :] = words[passage, rows, :]

    def decode(slot):
        for index in range(BLOCKS):
            word = word_stage[slot, index * SUB : (index + 1) * SUB, :]
            for field in range(FIELDS):
                rows = jnp.zeros((SUB, LANES), jnp.float32)
                for row in range(SUB):
                    place = index % row_blocks * tile_tokens + row * FIELDS + field
                    code = code_slots[slot][index // row_blocks, place]
                    rows = jnp.where(sub == row, table[pl.ds(code, SUB, stride=0), :], rows)
                low = jnp.bitwise_and(word, 1 << (2 * field)) != 0
                high = jnp.bitwise_and(word, 2 << (2 * field)) != 0
                residual = jnp.where(
                    high, jnp.where(low, level[3], level[2]), jnp.where(low, level[1], level[0])
                )
                base = index * tile_tokens + field * SUB
                dense[base : base + SUB, :] = rows + residual

    def normalize():
        for index in range(BLOCKS):
            rows = slice(index * tile_tokens, (index + 1) * tile_tokens)
            block = dense[rows, :]
            inverse = lax.rsqrt(jnp.sum(block * block, axis=1, keepdims=True) + 1e-06)
            embed[rows, :] = (block * inverse).astype(jnp.bfloat16)

    dense[...] = jnp.zeros(dense.shape, dense.dtype)
    embed[...] = jnp.zeros(embed.shape, embed.dtype)
    for slot in range(SLOTS):
        fetch_words(fetch_codes(slot, slot), slot)
        if slot < 2:
            slot_copy(slot).start()
        elif slot < SLOTS - 1:
            pl.when(slot < chunks)(slot_copy(slot).start)

    def step(group, carry):
        for slot in range(SLOTS):
            chunk = SLOTS * group + slot
            pl.when(chunk + SLOTS - 1 < chunks)(slot_copy((slot + SLOTS - 1) % SLOTS).start)

            @pl.when(chunk < chunks)
            def _(chunk=chunk, slot=slot):
                slot_copy(slot).wait()
                score(jnp.maximum(chunk - 2, 0))
                normalize()
                places = fetch_codes(chunk + SLOTS, slot)
                decode(slot)
                fetch_words(places, slot)

        return carry

    lax.fori_loop(0, (chunks + SLOTS - 1) // SLOTS, step, 0)
    score(chunks - 2)
    normalize()
    score(chunks - 1)

    best = maxima[0, :items, :]
    for tile in range(1, tiles):
        best = jnp.maximum(best, maxima[tile, :items, :])
    sums = jnp.sum(best, axis=1, keepdims=True) / query_len
    item_down = lax.broadcasted_iota(jnp.int32, (items, LANES), 0)
    item_slot = lax.broadcasted_iota(jnp.int32, (items, LANES), 1)
    spread = jnp.where(item_down % capacity == item_slot, sums, 0.0)
    source_down = lax.broadcasted_iota(jnp.int32, (sources, items), 0)
    item_across = lax.broadcasted_iota(jnp.int32, (sources, items), 1)
    gather = (item_across // capacity == source_down).astype(jnp.float32)
    by_source = jnp.dot(
        gather, spread, precision=lax.Precision.HIGHEST, preferred_element_type=jnp.float32
    )
    best_lanes = token_best.shape[1]
    for source in range(sources):
        out_ref[source, :, :best_lanes] = token_best
        out_ref[source, :, best_lanes:] = by_source[source : source + 1, :]


def owner_scores(me, slots, query_parts, centroids, token_codes, resid_words, lengths, levels, sizes):
    capacity = sizes[4]
    sources = slots.shape[0]
    group_count = len(query_parts)
    group_rows = query_parts[0].shape[0]
    cent_dev, width = centroids.shape
    pass_dev, plen = token_codes.shape
    packed = resid_words.shape[1]
    tiles = packed // SUB
    items = sources * capacity
    quads = group_count * group_rows // LANES
    work_size = items * tiles + quads * ALIGN + (SLOTS + 1) * BLOCKS
    any_space = pl.BlockSpec(memory_space=pl.ANY)
    in_hbm = pl.BlockSpec(memory_space=pltpu.HBM)
    pinned = [
        pltpu.with_memory_space_constraint(array, pltpu.HBM)
        for array in (levels, centroids, resid_words, token_codes, lengths, query_parts[0])
    ]
    vmem = pl.BlockSpec(memory_space=pltpu.VMEM)
    tokens = items * plen
    return pl.pallas_call(
        functools.partial(score_kernel, sizes),
        in_specs=[pl.BlockSpec(memory_space=pltpu.SMEM)] * 2 + [in_hbm] * 6 + [any_space] * (group_count - 1),
        out_specs=vmem,
        out_shape=jax.ShapeDtypeStruct((sources, 1, group_rows + LANES), jnp.float32),
        scratch_shapes=[
            pltpu.VMEM((cent_dev, width), jnp.bfloat16),
            pltpu.VMEM((cent_dev + SUB, width), jnp.float32),
            pltpu.VMEM((pass_dev, packed, width), jnp.int32),
            pltpu.VMEM((group_count, group_rows, width), jnp.bfloat16),
            pltpu.VMEM((quads, width, LANES), jnp.bfloat16),
            pltpu.VMEM((width, group_rows), jnp.bfloat16),
            pltpu.VMEM((BLOCKS * SUB * FIELDS, width), jnp.float32),
            pltpu.VMEM((BLOCKS * SUB * FIELDS, width), jnp.bfloat16),
            pltpu.VMEM((tiles, items + SUB, LANES), jnp.float32),
            pltpu.VMEM((pass_dev, plen), jnp.int32),
            pltpu.VMEM((SLOTS, BLOCKS * SUB, LANES), jnp.int32),
            pltpu.VMEM((SLOTS, BLOCKS * SUB * FIELDS // LANES, LANES), jnp.int32),
            *[pltpu.SMEM((BLOCKS * SUB * FIELDS // LANES, LANES), jnp.int32)] * SLOTS,
            pltpu.VMEM(levels.shape, jnp.float32),
            pltpu.SMEM((pass_dev,), jnp.int32),
            pltpu.SMEM((work_size,), jnp.int32),
            pltpu.SMEM((work_size // ALIGN + items * tiles // quads,), jnp.int32),
            pltpu.SMEM((items + 1,), jnp.int32),
            pltpu.SMEM((items + 1,), jnp.int32),
            pltpu.SMEM((items + 1,), jnp.int32),
            pltpu.SemaphoreType.DMA((min(quads, PARTS),)),
            pltpu.SemaphoreType.DMA((4,)),
            pltpu.SemaphoreType.DMA((group_count,)),
            pltpu.SemaphoreType.DMA((3,)),
            pltpu.SemaphoreType.DMA((SLOTS,)),
        ],
        compiler_params=pltpu.CompilerParams(vmem_limit_bytes=44 * MIB),
        cost_estimate=pl.CostEstimate(
            flops=2 * (tokens * LANES + cent_dev * group_rows) * width, bytes_accessed=2 * cent_dev * width * 2, transcendentals=tokens
        ),
        name="owner_scores",
    )(
        me, slots, *pinned, *query_parts[1:]
    )


def finish_kernel(sizes, me_ref, back_ref, target_ref, best_out, score_out):
    group_count, cent_count, _, query_len, capacity, _, _ = sizes
    group = jnp.bitwise_and(me_ref[0], group_count - 1)
    best_lanes = best_out.shape[0] * query_len
    best = back_ref[group, :, :best_lanes]
    for cent in range(1, cent_count):
        best = jnp.maximum(best, back_ref[cent * group_count + group, :, :best_lanes])
    for index in range(best_out.shape[0]):
        best_out[index : index + 1, :] = best[:, index * query_len : (index + 1) * query_len]
    back = back_ref[:, 0, best_lanes:]
    target = target_ref[...]
    owner = lax.broadcasted_iota(jnp.int32, (back.shape[0], target.shape[1]), 0)
    found = jnp.zeros(owner.shape, jnp.float32)
    for slot in range(capacity):
        found = found + jnp.where(owner * capacity + slot == target, back[:, slot : slot + 1], 0.0)
    scores = jnp.sum(found, axis=0, keepdims=True)
    width = score_out.shape[1]
    for index in range(score_out.shape[0]):
        score_out[index : index + 1, :] = scores[:, index * width : (index + 1) * width]


def finish(me, back, target, group_rows, sizes):
    _, _, per_device, query_len, _, _, cand_count = sizes
    vmem = pl.BlockSpec(memory_space=pltpu.VMEM)
    return pl.pallas_call(
        functools.partial(finish_kernel, sizes),
        in_specs=[pl.BlockSpec(memory_space=pltpu.SMEM), vmem, vmem],
        out_specs=[vmem] * 2,
        out_shape=[
            jax.ShapeDtypeStruct((group_rows, query_len), jnp.float32),
            jax.ShapeDtypeStruct((per_device, cand_count), jnp.float32),
        ],
        name="finish",
    )(me, back, target)


def shards(queries, centroids, candidates, token_codes, resid_words, lengths, levels):
    group_rows, query_len, width = queries.shape
    pass_dev = token_codes.shape[0]
    per_device, cand_count = candidates.shape[2:]
    pair_count = per_device * cand_count
    cent_count = lax.axis_size("cent")
    group_count = lax.axis_size("grp")
    devices = cent_count * group_count
    capacity = max(2, 2 * pair_count // devices)
    sizes = (group_count, cent_count, per_device, query_len, capacity, pass_dev, cand_count)
    cand = candidates.reshape(per_device, cand_count)
    query_rows = queries.reshape(group_rows * query_len, width)
    me = (lax.axis_index("cent") * group_count + lax.axis_index("grp")).astype(jnp.int32).reshape(1)
    slots, target = slots_by_owner(cand, devices, pass_dev, capacity)
    slots = lax.all_to_all(slots, ("cent", "grp"), split_axis=0, concat_axis=0, tiled=True)
    query_parts = [query_rows]
    for apart in range(1, group_count):
        pairs = [(index, index ^ apart) for index in range(group_count)]
        query_parts.append(lax.ppermute(query_rows, "grp", pairs))
    reply = owner_scores(
        me, slots, query_parts, centroids, token_codes, resid_words, lengths, levels, sizes
    )
    back = lax.all_to_all(reply, ("cent", "grp"), split_axis=0, concat_axis=0, tiled=True)
    token_best, scores = finish(me, back, target, group_rows, sizes)
    return (token_best, scores.reshape(1, 1, per_device, cand_count))


def solution(mesh):
    placed = (
        P("grp", None, None),
        P("cent", None),
        P("grp", "cent", None, None),
        P(("cent", "grp"), None),
        P(("cent", "grp"), None, None),
        P(("cent", "grp")),
        P(),
    )
    return jax.shard_map(
        shards,
        mesh=mesh,
        in_specs=placed,
        out_specs=(P("grp", None), P("grp", "cent", None, None)),
        check_vma=False,
    )
```

```python
import functools

import jax
import jax.numpy as jnp
from jax import lax
from jax.experimental import pallas as pl
from jax.experimental.pallas import tpu as pltpu
from jax.sharding import PartitionSpec as P

MASKED = -1000000000.0
LANES = 128
SUB = 8
FIELDS = 4
BLOCKS = 16
ALIGN = 4
SLOTS = 4
PARTS = 8
MIB = 1 << 20


def transposed_by_eye(row):
    size = row.shape[1]
    down = lax.broadcasted_iota(jnp.int32, (size, size), 0)
    across = lax.broadcasted_iota(jnp.int32, (size, size), 1)
    return jnp.sum(jnp.where(down == across, row, 0.0), axis=1, keepdims=True)


def one_row(rows):
    return jnp.concatenate([rows[index : index + 1, :] for index in range(rows.shape[0])], axis=1)


def slots_kernel(pass_dev, capacity, cand_ref, slots_ref, target_ref):
    per_device = cand_ref.shape[0]
    ids = one_row(cand_ref[...])
    pairs = ids.shape[1]
    owners = jnp.right_shift(ids, pass_dev.bit_length() - 1)
    earlier = lax.broadcasted_iota(jnp.int32, (pairs, pairs), 0) < lax.broadcasted_iota(
        jnp.int32, (pairs, pairs), 1
    )
    named = owners.astype(jnp.float32)
    same = transposed_by_eye(named) == named
    slots = jnp.sum(jnp.where(same & earlier, 1.0, 0.0), axis=0, keepdims=True).astype(jnp.int32)
    target_ref[...] = owners * capacity + slots
    query = lax.broadcasted_iota(jnp.int32, ids.shape, 1) // (pairs // per_device)
    tagged = (jnp.bitwise_and(ids, pass_dev - 1) * per_device + query + 1).astype(jnp.float32)
    down = lax.broadcasted_iota(jnp.int32, (slots_ref.shape[0], pairs), 0)
    lane = lax.broadcasted_iota(jnp.int32, slots_ref.shape, 1)
    found = jnp.zeros(slots_ref.shape, jnp.float32)
    for slot in range(capacity):
        chosen = jnp.where((down == owners) & (slots == slot), tagged, 0.0)
        found = jnp.where(lane == slot, jnp.sum(chosen, axis=1, keepdims=True), found)
    slots_ref[...] = found.astype(jnp.int32)


def slots_by_owner(cand, devices, pass_dev, capacity):
    vmem = pl.BlockSpec(memory_space=pltpu.VMEM)
    return pl.pallas_call(
        functools.partial(slots_kernel, pass_dev, capacity),
        in_specs=[vmem],
        out_specs=[vmem] * 2,
        out_shape=[
            jax.ShapeDtypeStruct((devices, capacity), jnp.int32),
            jax.ShapeDtypeStruct((1, cand.size), jnp.int32),
        ],
        name="slots_by_owner",
    )(cand)


def score_kernel(
    sizes,
    me_ref,
    ids,
    levels_hbm,
    cent_hbm,
    words_hbm,
    codes_hbm,
    lens_hbm,
    *rest,
):
    group_count, cent_count, per_device, query_len, capacity, pass_dev, cand_count = sizes
    query_hbm = rest[:group_count]
    (out_ref, staged, table, words, query_rows, query_t, own_t, dense, embed, maxima, codes, word_stage,
     code_stage, *more) = rest[group_count:]
    code_slots, more = more[:SLOTS], more[SLOTS:]
    (levels_ref, lens, work, work_quad, table_sem, words_sem, query_sem, small_sem,
     slot_sem) = more
    sources = ids.shape[0]
    items = sources * capacity
    tiles = words.shape[0] // (pass_dev * SUB)
    tile_tokens = SUB * FIELDS
    quad_sources = LANES // (per_device * query_len)
    quads = sources // quad_sources
    group_quads = cent_count // quad_sources
    per_bits = per_device.bit_length() - 1
    tile_bits = tiles.bit_length() - 1
    row_at = (pass_dev * tiles - 1).bit_length()
    lane_at = row_at + (items * tiles).bit_length()
    last_at = lane_at + (quad_sources * per_device - 1).bit_length()
    assert last_at + (tiles * tile_tokens - 1).bit_length() < 32
    next_tile = 1 + (1 << row_at) - (tile_tokens << last_at)
    parts = min(quads, PARTS)
    part_rows = staged.shape[0] // parts
    part_quads = quads // parts
    word_parts = words_sem.shape[0]
    part_words = words.shape[0] // word_parts

    def table_copy(part):
        rows = pl.ds(pl.multiple_of(part * part_rows, part_rows), part_rows)
        return pltpu.make_async_copy(cent_hbm.at[rows, :], staged.at[rows, :], table_sem.at[part])

    def words_copy(part):
        rows = pl.ds(part * part_words, part_words)
        return pltpu.make_async_copy(words_hbm.at[rows, :], words.at[rows, :], words_sem.at[part])

    def start_table(part, carry):
        table_copy(part).start()
        return carry

    group = jnp.bitwise_and(me_ref[0], group_count - 1)

    def query_copy(apart):
        return pltpu.make_async_copy(
            query_hbm[apart], query_rows.at[jnp.bitwise_xor(group, apart)], query_sem.at[apart]
        )

    lens_copy = pltpu.make_async_copy(lens_hbm, lens, small_sem.at[0])
    codes_copy = pltpu.make_async_copy(codes_hbm, codes, small_sem.at[1])
    levels_copy = pltpu.make_async_copy(levels_hbm, levels_ref, small_sem.at[2])
    lens_copy.start()
    levels_copy.start()
    for apart in range(group_count):
        query_copy(apart).start()
    lax.fori_loop(0, parts, start_table, 0)
    codes_copy.start()
    for part in range(word_parts):
        words_copy(part).start()

    maxima[...] = jnp.full(maxima.shape, MASKED, jnp.float32)
    query_copy(0).wait()
    own_t[...] = jnp.transpose(query_rows[group].astype(jnp.float32)).astype(jnp.bfloat16)
    lens_copy.wait()
    for apart in range(1, group_count):
        query_copy(apart).wait()

    spare = ((items * tiles) << row_at) - (1 << last_at)

    def fill(quad, count):
        block = query_rows[quad // group_quads, pl.ds(quad % group_quads * LANES, LANES), :]
        query_t[quad] = jnp.transpose(block.astype(jnp.float32)).astype(jnp.bfloat16)
        start = count
        found = []
        for part in range(quad_sources):
            cent = quad % group_quads * quad_sources + part
            source = cent * group_count + quad // group_quads
            rows = jnp.left_shift(source * (capacity * tiles), row_at)
            for slot in range(capacity):
                tag = ids[source, slot] - 1
                lane = part * per_device + jnp.bitwise_and(tag, per_device - 1)
                entry = rows + jnp.left_shift(lane, lane_at) + ((slot * tiles) << row_at)
                found.append((tag, jnp.right_shift(jnp.maximum(tag, 0), per_bits), entry))
        lengths = [lens[passage] for _, passage, _ in found]
        for (tag, passage, entry), length in zip(found, lengths):
            entry = entry + jnp.left_shift(passage, tile_bits) + jnp.left_shift(length - 1, last_at)
            for tile in range(tiles):
                work[count + tile] = entry + tile * next_tile
            blocks = jnp.right_shift(length + tile_tokens - 1, tile_tokens.bit_length() - 1)
            count = count + jnp.where(tag >= 0, blocks, 0)
        for index in range(ALIGN):
            work[count + index] = spare
        count = (count + ALIGN - 1) // ALIGN * ALIGN
        for index in range(quad_sources * capacity * tiles // ALIGN):
            work_quad[start // ALIGN + index] = quad
        return count

    def prepare(part, carry):
        count, best = carry
        table_copy(part).wait()
        rows = pl.ds(pl.multiple_of(part * part_rows, part_rows), part_rows)
        scores = jnp.dot(staged[rows, :], own_t[...], preferred_element_type=jnp.float32)
        best = jnp.maximum(best, jnp.max(scores.reshape(part_rows // SUB, SUB, scores.shape[1]), axis=0))
        table[rows, :] = staged[rows, :].astype(jnp.float32)
        for index in range(part_quads):
            count = fill(part * part_quads + index, count)
        return count, best

    lowest = jnp.full((SUB, own_t.shape[1]), -jnp.inf, jnp.float32)
    total, token_best = lax.fori_loop(0, parts, prepare, (0, lowest))
    token_best = jnp.max(token_best, axis=0, keepdims=True)
    for index in range((SLOTS + 1) * BLOCKS):
        work[total + index] = spare
    for index in range(2 * BLOCKS // ALIGN):
        work_quad[total // ALIGN + index] = 0
    chunks = jnp.maximum((total + BLOCKS - 1) // BLOCKS, 2)
    codes_copy.wait()
    levels_copy.wait()
    for part in range(word_parts):
        words_copy(part).wait()

    sub = lax.broadcasted_iota(jnp.int32, (SUB, LANES), 0)
    position = jnp.concatenate([sub * FIELDS + field for field in range(FIELDS)], axis=0)
    row_blocks = LANES // tile_tokens
    lane_tile = lax.broadcasted_iota(jnp.int32, (1, LANES), 1) // tile_tokens
    lane_group = lax.broadcasted_iota(jnp.int32, (1, LANES), 1) // query_len
    level = [levels_ref[index : index + 1, :] for index in range(FIELDS)]

    def score(chunk):
        scores = []
        for part in range(BLOCKS // ALIGN):
            rows = embed[part * ALIGN * tile_tokens : (part + 1) * ALIGN * tile_tokens, :]
            quad = work_quad[chunk * (BLOCKS // ALIGN) + part]
            scores.append(jnp.dot(rows, query_t[quad], preferred_element_type=jnp.float32))
        for index in range(BLOCKS):
            entry = work[chunk * BLOCKS + index]
            inner = index % ALIGN
            block = scores[index // ALIGN][inner * tile_tokens : (inner + 1) * tile_tokens]
            kept = jnp.where(position <= jnp.right_shift(entry, last_at), block, MASKED)
            best = jnp.max(kept, axis=0, keepdims=True)
            row = jnp.bitwise_and(jnp.right_shift(entry, row_at), (1 << (lane_at - row_at)) - 1)
            lane = jnp.bitwise_and(jnp.right_shift(entry, lane_at), (1 << (last_at - lane_at)) - 1)
            maxima[pl.ds(row, 1), :] = jnp.where(lane_group == lane, best, 0.0)

    def slot_copy(slot):
        return pltpu.make_async_copy(code_stage.at[slot], code_slots[slot], slot_sem.at[slot])

    def fetch_codes(chunk, slot):
        places = []
        for row in range(BLOCKS // row_blocks):
            together = jnp.zeros((1, LANES), jnp.int32)
            for index in range(row_blocks):
                entry = work[chunk * BLOCKS + row * row_blocks + index]
                place = jnp.bitwise_and(entry, (1 << row_at) - 1)
                passage = jnp.right_shift(place, tile_bits)
                shift = jnp.bitwise_and(index - place, row_blocks - 1) * tile_tokens
                moved = pltpu.roll(codes[pl.ds(passage, 1), :], shift, 1)
                together = jnp.where(lane_tile == index, moved, together)
                places.append(place)
            code_stage[slot, row : row + 1, :] = together
        return places

    def fetch_words(places, slot):
        for block, place in enumerate(places):
            rows = pl.ds(pl.multiple_of(place * SUB, SUB), SUB)
            word_stage[slot, block * SUB : (block + 1) * SUB, :] = words[rows, :]

    def decode(slot):
        for index in range(BLOCKS):
            word = word_stage[slot, index * SUB : (index + 1) * SUB, :]
            for field in range(FIELDS):
                rows = jnp.zeros((SUB, LANES), jnp.float32)
                for row in range(SUB):
                    place = index % row_blocks * tile_tokens + row * FIELDS + field
                    code = code_slots[slot][index // row_blocks, place]
                    rows = jnp.where(sub == row, table[pl.ds(code, SUB, stride=0), :], rows)
                low = jnp.bitwise_and(word, 1 << (2 * field)) != 0
                high = jnp.bitwise_and(word, 2 << (2 * field)) != 0
                residual = jnp.where(
                    high, jnp.where(low, level[3], level[2]), jnp.where(low, level[1], level[0])
                )
                base = index * tile_tokens + field * SUB
                dense[base : base + SUB, :] = rows + residual

    def normalize():
        for index in range(BLOCKS):
            rows = slice(index * tile_tokens, (index + 1) * tile_tokens)
            block = dense[rows, :]
            inverse = lax.rsqrt(jnp.sum(block * block, axis=1, keepdims=True) + 1e-06)
            embed[rows, :] = (block * inverse).astype(jnp.bfloat16)

    dense[...] = jnp.zeros(dense.shape, dense.dtype)
    embed[...] = jnp.zeros(embed.shape, embed.dtype)
    for slot in range(SLOTS):
        fetch_words(fetch_codes(slot, slot), slot)
        if slot < 2:
            slot_copy(slot).start()
        elif slot < SLOTS - 1:
            pl.when(slot < chunks)(slot_copy(slot).start)

    def step(group, carry):
        for slot in range(SLOTS):
            chunk = SLOTS * group + slot
            pl.when(chunk + SLOTS - 1 < chunks)(slot_copy((slot + SLOTS - 1) % SLOTS).start)

            @pl.when(chunk < chunks)
            def _(chunk=chunk, slot=slot):
                slot_copy(slot).wait()
                score(jnp.maximum(chunk - 2, 0))
                normalize()
                places = fetch_codes(chunk + SLOTS, slot)
                decode(slot)
                fetch_words(places, slot)

        return carry

    lax.fori_loop(0, (chunks + SLOTS - 1) // SLOTS, step, 0)
    score(chunks - 2)
    normalize()
    score(chunks - 1)

    best = maxima[pl.ds(0, items, stride=tiles), :]
    for tile in range(1, tiles):
        best = jnp.maximum(best, maxima[pl.ds(tile, items, stride=tiles), :])
    sums = jnp.sum(best, axis=1, keepdims=True) / query_len
    item_down = lax.broadcasted_iota(jnp.int32, (items, LANES), 0)
    item_slot = lax.broadcasted_iota(jnp.int32, (items, LANES), 1)
    spread = jnp.where(item_down % capacity == item_slot, sums, 0.0)
    source_down = lax.broadcasted_iota(jnp.int32, (sources, items), 0)
    item_across = lax.broadcasted_iota(jnp.int32, (sources, items), 1)
    gather = (item_across // capacity == source_down).astype(jnp.float32)
    by_source = jnp.dot(
        gather, spread, precision=lax.Precision.HIGHEST, preferred_element_type=jnp.float32
    )
    best_lanes = token_best.shape[1]
    for source in range(sources):
        out_ref[source, :, :best_lanes] = token_best
        out_ref[source, :, best_lanes:] = by_source[source : source + 1, :]


def owner_scores(me, slots, query_parts, centroids, token_codes, resid_words, lengths, levels, sizes):
    capacity = sizes[4]
    sources = slots.shape[0]
    group_count = len(query_parts)
    group_rows = query_parts[0].shape[0]
    cent_dev, width = centroids.shape
    pass_dev, plen = token_codes.shape
    packed = resid_words.shape[1]
    tiles = packed // SUB
    items = sources * capacity
    quads = group_count * group_rows // LANES
    work_size = items * tiles + quads * ALIGN + (SLOTS + 1) * BLOCKS
    any_space = pl.BlockSpec(memory_space=pl.ANY)
    in_hbm = pl.BlockSpec(memory_space=pltpu.HBM)
    pinned = [
        pltpu.with_memory_space_constraint(array, pltpu.HBM)
        for array in (levels, centroids, resid_words.reshape(pass_dev * packed, width), token_codes, lengths, query_parts[0])
    ]
    vmem = pl.BlockSpec(memory_space=pltpu.VMEM)
    tokens = items * plen
    return pl.pallas_call(
        functools.partial(score_kernel, sizes),
        in_specs=[pl.BlockSpec(memory_space=pltpu.SMEM)] * 2 + [in_hbm] * 6 + [any_space] * (group_count - 1),
        out_specs=vmem,
        out_shape=jax.ShapeDtypeStruct((sources, 1, group_rows + LANES), jnp.float32),
        scratch_shapes=[
            pltpu.VMEM((cent_dev, width), jnp.bfloat16),
            pltpu.VMEM((cent_dev + SUB, width), jnp.float32),
            pltpu.VMEM((pass_dev * packed, width), jnp.int32),
            pltpu.VMEM((group_count, group_rows, width), jnp.bfloat16),
            pltpu.VMEM((quads, width, LANES), jnp.bfloat16),
            pltpu.VMEM((width, group_rows), jnp.bfloat16),
            pltpu.VMEM((BLOCKS * SUB * FIELDS, width), jnp.float32),
            pltpu.VMEM((BLOCKS * SUB * FIELDS, width), jnp.bfloat16),
            pltpu.VMEM((items * tiles + SUB, LANES), jnp.float32),
            pltpu.VMEM((pass_dev, plen), jnp.int32),
            pltpu.VMEM((SLOTS, BLOCKS * SUB, LANES), jnp.int32),
            pltpu.VMEM((SLOTS, BLOCKS * SUB * FIELDS // LANES, LANES), jnp.int32),
            *[pltpu.SMEM((BLOCKS * SUB * FIELDS // LANES, LANES), jnp.int32)] * SLOTS,
            pltpu.VMEM(levels.shape, jnp.float32),
            pltpu.SMEM((pass_dev,), jnp.int32),
            pltpu.SMEM((work_size,), jnp.int32),
            pltpu.SMEM((work_size // ALIGN + items * tiles // quads,), jnp.int32),
            pltpu.SemaphoreType.DMA((min(quads, PARTS),)),
            pltpu.SemaphoreType.DMA((4,)),
            pltpu.SemaphoreType.DMA((group_count,)),
            pltpu.SemaphoreType.DMA((3,)),
            pltpu.SemaphoreType.DMA((SLOTS,)),
        ],
        compiler_params=pltpu.CompilerParams(vmem_limit_bytes=44 * MIB),
        cost_estimate=pl.CostEstimate(
            flops=2 * (tokens * LANES + cent_dev * group_rows) * width, bytes_accessed=2 * cent_dev * width * 2, transcendentals=tokens
        ),
        name="owner_scores",
    )(
        me, slots, *pinned, *query_parts[1:]
    )


def finish_kernel(sizes, me_ref, back_ref, target_ref, best_out, score_out):
    group_count, cent_count, _, query_len, capacity, _, _ = sizes
    group = jnp.bitwise_and(me_ref[0], group_count - 1)
    best_lanes = best_out.shape[0] * query_len
    best = back_ref[group, :, :best_lanes]
    for cent in range(1, cent_count):
        best = jnp.maximum(best, back_ref[cent * group_count + group, :, :best_lanes])
    for index in range(best_out.shape[0]):
        best_out[index : index + 1, :] = best[:, index * query_len : (index + 1) * query_len]
    back = back_ref[:, 0, best_lanes:]
    target = target_ref[...]
    owner = lax.broadcasted_iota(jnp.int32, (back.shape[0], target.shape[1]), 0)
    found = jnp.zeros(owner.shape, jnp.float32)
    for slot in range(capacity):
        found = found + jnp.where(owner * capacity + slot == target, back[:, slot : slot + 1], 0.0)
    scores = jnp.sum(found, axis=0, keepdims=True)
    width = score_out.shape[1]
    for index in range(score_out.shape[0]):
        score_out[index : index + 1, :] = scores[:, index * width : (index + 1) * width]


def finish(me, back, target, group_rows, sizes):
    _, _, per_device, query_len, _, _, cand_count = sizes
    vmem = pl.BlockSpec(memory_space=pltpu.VMEM)
    return pl.pallas_call(
        functools.partial(finish_kernel, sizes),
        in_specs=[pl.BlockSpec(memory_space=pltpu.SMEM), vmem, vmem],
        out_specs=[vmem] * 2,
        out_shape=[
            jax.ShapeDtypeStruct((group_rows, query_len), jnp.float32),
            jax.ShapeDtypeStruct((per_device, cand_count), jnp.float32),
        ],
        name="finish",
    )(me, back, target)


def shards(queries, centroids, candidates, token_codes, resid_words, lengths, levels):
    group_rows, query_len, width = queries.shape
    pass_dev = token_codes.shape[0]
    per_device, cand_count = candidates.shape[2:]
    pair_count = per_device * cand_count
    cent_count = lax.axis_size("cent")
    group_count = lax.axis_size("grp")
    devices = cent_count * group_count
    capacity = max(2, 2 * pair_count // devices)
    sizes = (group_count, cent_count, per_device, query_len, capacity, pass_dev, cand_count)
    cand = candidates.reshape(per_device, cand_count)
    query_rows = queries.reshape(group_rows * query_len, width)
    me = (lax.axis_index("cent") * group_count + lax.axis_index("grp")).astype(jnp.int32).reshape(1)
    slots, target = slots_by_owner(cand, devices, pass_dev, capacity)
    slots = lax.all_to_all(slots, ("cent", "grp"), split_axis=0, concat_axis=0, tiled=True)
    query_parts = [query_rows]
    for apart in range(1, group_count):
        pairs = [(index, index ^ apart) for index in range(group_count)]
        query_parts.append(lax.ppermute(query_rows, "grp", pairs))
    reply = owner_scores(
        me, slots, query_parts, centroids, token_codes, resid_words, lengths, levels, sizes
    )
    back = lax.all_to_all(reply, ("cent", "grp"), split_axis=0, concat_axis=0, tiled=True)
    token_best, scores = finish(me, back, target, group_rows, sizes)
    return (token_best, scores.reshape(1, 1, per_device, cand_count))


def solution(mesh):
    placed = (
        P("grp", None, None),
        P("cent", None),
        P("grp", "cent", None, None),
        P(("cent", "grp"), None),
        P(("cent", "grp"), None, None),
        P(("cent", "grp")),
        P(),
    )
    return jax.shard_map(
        shards,
        mesh=mesh,
        in_specs=placed,
        out_specs=(P("grp", None), P("grp", "cent", None, None)),
        check_vma=False,
    )
```

```python
import functools

import jax
import jax.numpy as jnp
from jax import lax
from jax.experimental import pallas as pl
from jax.experimental.pallas import tpu as pltpu
from jax.sharding import PartitionSpec as P

MASKED = -1000000000.0
LANES = 128
SUB = 8
FIELDS = 4
BLOCKS = 24
ALIGN = 4
SLOTS = 3
PARTS = 8
MIB = 1 << 20


def transposed_by_eye(row):
    size = row.shape[1]
    down = lax.broadcasted_iota(jnp.int32, (size, size), 0)
    across = lax.broadcasted_iota(jnp.int32, (size, size), 1)
    return jnp.sum(jnp.where(down == across, row, 0.0), axis=1, keepdims=True)


def one_row(rows):
    return jnp.concatenate([rows[index : index + 1, :] for index in range(rows.shape[0])], axis=1)


def slots_kernel(pass_dev, capacity, cand_ref, slots_ref, target_ref):
    per_device = cand_ref.shape[0]
    ids = one_row(cand_ref[...])
    pairs = ids.shape[1]
    owners = jnp.right_shift(ids, pass_dev.bit_length() - 1)
    earlier = lax.broadcasted_iota(jnp.int32, (pairs, pairs), 0) < lax.broadcasted_iota(
        jnp.int32, (pairs, pairs), 1
    )
    named = owners.astype(jnp.float32)
    same = transposed_by_eye(named) == named
    slots = jnp.sum(jnp.where(same & earlier, 1.0, 0.0), axis=0, keepdims=True).astype(jnp.int32)
    target_ref[...] = owners * capacity + slots
    query = lax.broadcasted_iota(jnp.int32, ids.shape, 1) // (pairs // per_device)
    tagged = (jnp.bitwise_and(ids, pass_dev - 1) * per_device + query + 1).astype(jnp.float32)
    down = lax.broadcasted_iota(jnp.int32, (slots_ref.shape[0], pairs), 0)
    lane = lax.broadcasted_iota(jnp.int32, slots_ref.shape, 1)
    found = jnp.zeros(slots_ref.shape, jnp.float32)
    for slot in range(capacity):
        chosen = jnp.where((down == owners) & (slots == slot), tagged, 0.0)
        found = jnp.where(lane == slot, jnp.sum(chosen, axis=1, keepdims=True), found)
    slots_ref[...] = found.astype(jnp.int32)


def slots_by_owner(cand, devices, pass_dev, capacity):
    vmem = pl.BlockSpec(memory_space=pltpu.VMEM)
    return pl.pallas_call(
        functools.partial(slots_kernel, pass_dev, capacity),
        in_specs=[vmem],
        out_specs=[vmem] * 2,
        out_shape=[
            jax.ShapeDtypeStruct((devices, capacity), jnp.int32),
            jax.ShapeDtypeStruct((1, cand.size), jnp.int32),
        ],
        name="slots_by_owner",
    )(cand)


def score_kernel(
    sizes,
    me_ref,
    ids,
    levels_hbm,
    cent_hbm,
    words_hbm,
    codes_hbm,
    lens_hbm,
    *rest,
):
    group_count, cent_count, per_device, query_len, capacity, pass_dev, cand_count = sizes
    query_hbm = rest[:group_count]
    (out_ref, staged, table, words, query_rows, query_t, own_t, dense, embed, maxima, codes, word_stage,
     code_stage, *more) = rest[group_count:]
    code_slots, more = more[:SLOTS], more[SLOTS:]
    (levels_ref, lens, work, work_quad, table_sem, words_sem, query_sem, small_sem,
     slot_sem) = more
    sources = ids.shape[0]
    items = sources * capacity
    tiles = words.shape[0] // (pass_dev * SUB)
    tile_tokens = SUB * FIELDS
    quad_sources = LANES // (per_device * query_len)
    quads = sources // quad_sources
    group_quads = cent_count // quad_sources
    per_bits = per_device.bit_length() - 1
    tile_bits = tiles.bit_length() - 1
    row_at = (pass_dev * tiles - 1).bit_length()
    lane_at = row_at + (items * tiles).bit_length()
    last_at = lane_at + (quad_sources * per_device - 1).bit_length()
    assert last_at + (tiles * tile_tokens - 1).bit_length() < 32
    next_tile = 1 + (1 << row_at) - (tile_tokens << last_at)
    parts = min(quads, PARTS)
    part_rows = staged.shape[0] // parts
    part_quads = quads // parts
    word_parts = words_sem.shape[0]
    part_words = words.shape[0] // word_parts

    def table_copy(part):
        rows = pl.ds(pl.multiple_of(part * part_rows, part_rows), part_rows)
        return pltpu.make_async_copy(cent_hbm.at[rows, :], staged.at[rows, :], table_sem.at[part])

    def words_copy(part):
        rows = pl.ds(part * part_words, part_words)
        return pltpu.make_async_copy(words_hbm.at[rows, :], words.at[rows, :], words_sem.at[part])

    def start_table(part, carry):
        table_copy(part).start()
        return carry

    group = jnp.bitwise_and(me_ref[0], group_count - 1)

    def query_copy(apart):
        return pltpu.make_async_copy(
            query_hbm[apart], query_rows.at[jnp.bitwise_xor(group, apart)], query_sem.at[apart]
        )

    lens_copy = pltpu.make_async_copy(lens_hbm, lens, small_sem.at[0])
    codes_copy = pltpu.make_async_copy(codes_hbm, codes, small_sem.at[1])
    levels_copy = pltpu.make_async_copy(levels_hbm, levels_ref, small_sem.at[2])
    lens_copy.start()
    levels_copy.start()
    for apart in range(group_count):
        query_copy(apart).start()
    lax.fori_loop(0, parts, start_table, 0)
    codes_copy.start()
    for part in range(word_parts):
        words_copy(part).start()

    maxima[...] = jnp.full(maxima.shape, MASKED, jnp.float32)
    query_copy(0).wait()
    own_t[...] = jnp.transpose(query_rows[group].astype(jnp.float32)).astype(jnp.bfloat16)
    lens_copy.wait()
    for apart in range(1, group_count):
        query_copy(apart).wait()

    spare = ((items * tiles) << row_at) - (1 << last_at)

    def fill(quad, count):
        block = query_rows[quad // group_quads, pl.ds(quad % group_quads * LANES, LANES), :]
        query_t[quad] = jnp.transpose(block.astype(jnp.float32)).astype(jnp.bfloat16)
        start = count
        found = []
        for part in range(quad_sources):
            cent = quad % group_quads * quad_sources + part
            source = cent * group_count + quad // group_quads
            rows = jnp.left_shift(source * (capacity * tiles), row_at)
            for slot in range(capacity):
                tag = ids[source, slot] - 1
                lane = part * per_device + jnp.bitwise_and(tag, per_device - 1)
                entry = rows + jnp.left_shift(lane, lane_at) + ((slot * tiles) << row_at)
                found.append((tag, jnp.right_shift(jnp.maximum(tag, 0), per_bits), entry))
        lengths = [lens[passage] for _, passage, _ in found]
        for (tag, passage, entry), length in zip(found, lengths):
            entry = entry + jnp.left_shift(passage, tile_bits) + jnp.left_shift(length - 1, last_at)
            for tile in range(tiles):
                work[count + tile] = entry + tile * next_tile
            blocks = jnp.right_shift(length + tile_tokens - 1, tile_tokens.bit_length() - 1)
            count = count + jnp.where(tag >= 0, blocks, 0)
        for index in range(ALIGN):
            work[count + index] = spare
        count = (count + ALIGN - 1) // ALIGN * ALIGN
        for index in range(quad_sources * capacity * tiles // ALIGN):
            work_quad[start // ALIGN + index] = quad
        return count

    def prepare(part, carry):
        count, best = carry
        table_copy(part).wait()
        rows = pl.ds(pl.multiple_of(part * part_rows, part_rows), part_rows)
        scores = jnp.dot(staged[rows, :], own_t[...], preferred_element_type=jnp.float32)
        best = jnp.maximum(best, jnp.max(scores.reshape(part_rows // SUB, SUB, scores.shape[1]), axis=0))
        table[rows, :] = staged[rows, :].astype(jnp.float32)
        for index in range(part_quads):
            count = fill(part * part_quads + index, count)
        return count, best

    lowest = jnp.full((SUB, own_t.shape[1]), -jnp.inf, jnp.float32)
    total, token_best = lax.fori_loop(0, parts, prepare, (0, lowest))
    token_best = jnp.max(token_best, axis=0, keepdims=True)
    for index in range((SLOTS + 1) * BLOCKS):
        work[total + index] = spare
    for index in range(2 * BLOCKS // ALIGN):
        work_quad[total // ALIGN + index] = 0
    chunks = jnp.maximum((total + BLOCKS - 1) // BLOCKS, 2)
    codes_copy.wait()
    levels_copy.wait()
    for part in range(word_parts):
        words_copy(part).wait()

    sub = lax.broadcasted_iota(jnp.int32, (SUB, LANES), 0)
    position = jnp.concatenate([sub * FIELDS + field for field in range(FIELDS)], axis=0)
    row_blocks = LANES // tile_tokens
    lane_tile = lax.broadcasted_iota(jnp.int32, (1, LANES), 1) // tile_tokens
    lane_group = lax.broadcasted_iota(jnp.int32, (1, LANES), 1) // query_len
    level = [levels_ref[index : index + 1, :] for index in range(FIELDS)]

    def score(chunk):
        scores = []
        for part in range(BLOCKS // ALIGN):
            rows = embed[part * ALIGN * tile_tokens : (part + 1) * ALIGN * tile_tokens, :]
            quad = work_quad[chunk * (BLOCKS // ALIGN) + part]
            scores.append(jnp.dot(rows, query_t[quad], preferred_element_type=jnp.float32))
        for index in range(BLOCKS):
            entry = work[chunk * BLOCKS + index]
            inner = index % ALIGN
            block = scores[index // ALIGN][inner * tile_tokens : (inner + 1) * tile_tokens]
            kept = jnp.where(position <= jnp.right_shift(entry, last_at), block, MASKED)
            best = jnp.max(kept, axis=0, keepdims=True)
            row = jnp.bitwise_and(jnp.right_shift(entry, row_at), (1 << (lane_at - row_at)) - 1)
            lane = jnp.bitwise_and(jnp.right_shift(entry, lane_at), (1 << (last_at - lane_at)) - 1)
            maxima[pl.ds(row, 1), :] = jnp.where(lane_group == lane, best, 0.0)

    def slot_copy(slot):
        return pltpu.make_async_copy(code_stage.at[slot], code_slots[slot], slot_sem.at[slot])

    def fetch_codes(chunk, slot):
        places = []
        for row in range(BLOCKS // row_blocks):
            together = jnp.zeros((1, LANES), jnp.int32)
            for index in range(row_blocks):
                entry = work[chunk * BLOCKS + row * row_blocks + index]
                place = jnp.bitwise_and(entry, (1 << row_at) - 1)
                passage = jnp.right_shift(place, tile_bits)
                shift = jnp.bitwise_and(index - place, row_blocks - 1) * tile_tokens
                moved = pltpu.roll(codes[pl.ds(passage, 1), :], shift, 1)
                together = jnp.where(lane_tile == index, moved, together)
                places.append(place)
            code_stage[slot, row : row + 1, :] = together
        return places

    def fetch_words(places, slot):
        for block, place in enumerate(places):
            rows = pl.ds(pl.multiple_of(place * SUB, SUB), SUB)
            word_stage[slot, block * SUB : (block + 1) * SUB, :] = words[rows, :]

    def decode(slot):
        for index in range(BLOCKS):
            word = word_stage[slot, index * SUB : (index + 1) * SUB, :]
            for field in range(FIELDS):
                rows = jnp.zeros((SUB, LANES), jnp.float32)
                for row in range(SUB):
                    place = index % row_blocks * tile_tokens + row * FIELDS + field
                    code = code_slots[slot][index // row_blocks, place]
                    rows = jnp.where(sub == row, table[pl.ds(code, SUB, stride=0), :], rows)
                low = jnp.bitwise_and(word, 1 << (2 * field)) != 0
                high = jnp.bitwise_and(word, 2 << (2 * field)) != 0
                residual = jnp.where(
                    high, jnp.where(low, level[3], level[2]), jnp.where(low, level[1], level[0])
                )
                base = index * tile_tokens + field * SUB
                dense[base : base + SUB, :] = rows + residual

    def normalize():
        for index in range(BLOCKS):
            rows = slice(index * tile_tokens, (index + 1) * tile_tokens)
            block = dense[rows, :]
            inverse = lax.rsqrt(jnp.sum(block * block, axis=1, keepdims=True) + 1e-06)
            embed[rows, :] = (block * inverse).astype(jnp.bfloat16)

    dense[...] = jnp.zeros(dense.shape, dense.dtype)
    embed[...] = jnp.zeros(embed.shape, embed.dtype)
    for slot in range(SLOTS):
        fetch_words(fetch_codes(slot, slot), slot)
        if slot < 2:
            slot_copy(slot).start()
        elif slot < SLOTS - 1:
            pl.when(slot < chunks)(slot_copy(slot).start)

    def step(group, carry):
        for slot in range(SLOTS):
            chunk = SLOTS * group + slot
            pl.when(chunk + SLOTS - 1 < chunks)(slot_copy((slot + SLOTS - 1) % SLOTS).start)

            @pl.when(chunk < chunks)
            def _(chunk=chunk, slot=slot):
                slot_copy(slot).wait()
                score(jnp.maximum(chunk - 2, 0))
                normalize()
                places = fetch_codes(chunk + SLOTS, slot)
                decode(slot)
                fetch_words(places, slot)

        return carry

    lax.fori_loop(0, (chunks + SLOTS - 1) // SLOTS, step, 0)
    score(chunks - 2)
    normalize()
    score(chunks - 1)

    best = maxima[pl.ds(0, items, stride=tiles), :]
    for tile in range(1, tiles):
        best = jnp.maximum(best, maxima[pl.ds(tile, items, stride=tiles), :])
    sums = jnp.sum(best, axis=1, keepdims=True) / query_len
    item_down = lax.broadcasted_iota(jnp.int32, (items, LANES), 0)
    item_slot = lax.broadcasted_iota(jnp.int32, (items, LANES), 1)
    spread = jnp.where(item_down % capacity == item_slot, sums, 0.0)
    source_down = lax.broadcasted_iota(jnp.int32, (sources, items), 0)
    item_across = lax.broadcasted_iota(jnp.int32, (sources, items), 1)
    gather = (item_across // capacity == source_down).astype(jnp.float32)
    by_source = jnp.dot(
        gather, spread, precision=lax.Precision.HIGHEST, preferred_element_type=jnp.float32
    )
    best_lanes = token_best.shape[1]
    for source in range(sources):
        out_ref[source, :, :best_lanes] = token_best
        out_ref[source, :, best_lanes:] = by_source[source : source + 1, :]


def owner_scores(me, slots, query_parts, centroids, token_codes, resid_words, lengths, levels, sizes):
    capacity = sizes[4]
    sources = slots.shape[0]
    group_count = len(query_parts)
    group_rows = query_parts[0].shape[0]
    cent_dev, width = centroids.shape
    pass_dev, plen = token_codes.shape
    packed = resid_words.shape[1]
    tiles = packed // SUB
    items = sources * capacity
    quads = group_count * group_rows // LANES
    work_size = items * tiles + quads * ALIGN + (SLOTS + 1) * BLOCKS
    any_space = pl.BlockSpec(memory_space=pl.ANY)
    in_hbm = pl.BlockSpec(memory_space=pltpu.HBM)
    pinned = [
        pltpu.with_memory_space_constraint(array, pltpu.HBM)
        for array in (levels, centroids, resid_words.reshape(pass_dev * packed, width), token_codes, lengths, query_parts[0])
    ]
    vmem = pl.BlockSpec(memory_space=pltpu.VMEM)
    tokens = items * plen
    return pl.pallas_call(
        functools.partial(score_kernel, sizes),
        in_specs=[pl.BlockSpec(memory_space=pltpu.SMEM)] * 2 + [in_hbm] * 6 + [any_space] * (group_count - 1),
        out_specs=vmem,
        out_shape=jax.ShapeDtypeStruct((sources, 1, group_rows + LANES), jnp.float32),
        scratch_shapes=[
            pltpu.VMEM((cent_dev, width), jnp.bfloat16),
            pltpu.VMEM((cent_dev + SUB, width), jnp.float32),
            pltpu.VMEM((pass_dev * packed, width), jnp.int32),
            pltpu.VMEM((group_count, group_rows, width), jnp.bfloat16),
            pltpu.VMEM((quads, width, LANES), jnp.bfloat16),
            pltpu.VMEM((width, group_rows), jnp.bfloat16),
            pltpu.VMEM((BLOCKS * SUB * FIELDS, width), jnp.float32),
            pltpu.VMEM((BLOCKS * SUB * FIELDS, width), jnp.bfloat16),
            pltpu.VMEM((items * tiles + SUB, LANES), jnp.float32),
            pltpu.VMEM((pass_dev, plen), jnp.int32),
            pltpu.VMEM((SLOTS, BLOCKS * SUB, LANES), jnp.int32),
            pltpu.VMEM((SLOTS, BLOCKS * SUB * FIELDS // LANES, LANES), jnp.int32),
            *[pltpu.SMEM((BLOCKS * SUB * FIELDS // LANES, LANES), jnp.int32)] * SLOTS,
            pltpu.VMEM(levels.shape, jnp.float32),
            pltpu.SMEM((pass_dev,), jnp.int32),
            pltpu.SMEM((work_size,), jnp.int32),
            pltpu.SMEM((work_size // ALIGN + items * tiles // quads,), jnp.int32),
            pltpu.SemaphoreType.DMA((min(quads, PARTS),)),
            pltpu.SemaphoreType.DMA((4,)),
            pltpu.SemaphoreType.DMA((group_count,)),
            pltpu.SemaphoreType.DMA((3,)),
            pltpu.SemaphoreType.DMA((SLOTS,)),
        ],
        compiler_params=pltpu.CompilerParams(vmem_limit_bytes=44 * MIB),
        cost_estimate=pl.CostEstimate(
            flops=2 * (tokens * LANES + cent_dev * group_rows) * width, bytes_accessed=2 * cent_dev * width * 2, transcendentals=tokens
        ),
        name="owner_scores",
    )(
        me, slots, *pinned, *query_parts[1:]
    )


def finish_kernel(sizes, me_ref, back_ref, target_ref, best_out, score_out):
    group_count, cent_count, _, query_len, capacity, _, _ = sizes
    group = jnp.bitwise_and(me_ref[0], group_count - 1)
    best_lanes = best_out.shape[0] * query_len
    best = back_ref[group, :, :best_lanes]
    for cent in range(1, cent_count):
        best = jnp.maximum(best, back_ref[cent * group_count + group, :, :best_lanes])
    for index in range(best_out.shape[0]):
        best_out[index : index + 1, :] = best[:, index * query_len : (index + 1) * query_len]
    back = back_ref[:, 0, best_lanes:]
    target = target_ref[...]
    owner = lax.broadcasted_iota(jnp.int32, (back.shape[0], target.shape[1]), 0)
    found = jnp.zeros(owner.shape, jnp.float32)
    for slot in range(capacity):
        found = found + jnp.where(owner * capacity + slot == target, back[:, slot : slot + 1], 0.0)
    scores = jnp.sum(found, axis=0, keepdims=True)
    width = score_out.shape[1]
    for index in range(score_out.shape[0]):
        score_out[index : index + 1, :] = scores[:, index * width : (index + 1) * width]


def finish(me, back, target, group_rows, sizes):
    _, _, per_device, query_len, _, _, cand_count = sizes
    vmem = pl.BlockSpec(memory_space=pltpu.VMEM)
    return pl.pallas_call(
        functools.partial(finish_kernel, sizes),
        in_specs=[pl.BlockSpec(memory_space=pltpu.SMEM), vmem, vmem],
        out_specs=[vmem] * 2,
        out_shape=[
            jax.ShapeDtypeStruct((group_rows, query_len), jnp.float32),
            jax.ShapeDtypeStruct((per_device, cand_count), jnp.float32),
        ],
        name="finish",
    )(me, back, target)


def shards(queries, centroids, candidates, token_codes, resid_words, lengths, levels):
    group_rows, query_len, width = queries.shape
    pass_dev = token_codes.shape[0]
    per_device, cand_count = candidates.shape[2:]
    pair_count = per_device * cand_count
    cent_count = lax.axis_size("cent")
    group_count = lax.axis_size("grp")
    devices = cent_count * group_count
    capacity = max(2, 2 * pair_count // devices)
    sizes = (group_count, cent_count, per_device, query_len, capacity, pass_dev, cand_count)
    cand = candidates.reshape(per_device, cand_count)
    query_rows = queries.reshape(group_rows * query_len, width)
    me = (lax.axis_index("cent") * group_count + lax.axis_index("grp")).astype(jnp.int32).reshape(1)
    slots, target = slots_by_owner(cand, devices, pass_dev, capacity)
    slots = lax.all_to_all(slots, ("cent", "grp"), split_axis=0, concat_axis=0, tiled=True)
    query_parts = [query_rows]
    for apart in range(1, group_count):
        away, block = (1, query_parts[apart - 1]) if apart % 2 else (apart, query_rows)
        pairs = [(index, index ^ away) for index in range(group_count)]
        query_parts.append(lax.ppermute(block, "grp", pairs))
    reply = owner_scores(
        me, slots, query_parts, centroids, token_codes, resid_words, lengths, levels, sizes
    )
    back = lax.all_to_all(reply, ("cent", "grp"), split_axis=0, concat_axis=0, tiled=True)
    token_best, scores = finish(me, back, target, group_rows, sizes)
    return (token_best, scores.reshape(1, 1, per_device, cand_count))


def solution(mesh):
    placed = (
        P("grp", None, None),
        P("cent", None),
        P("grp", "cent", None, None),
        P(("cent", "grp"), None),
        P(("cent", "grp"), None, None),
        P(("cent", "grp")),
        P(),
    )
    return jax.shard_map(
        shards,
        mesh=mesh,
        in_specs=placed,
        out_specs=(P("grp", None), P("grp", "cent", None, None)),
        check_vma=False,
    )
```

```python
import functools

import jax
import jax.numpy as jnp
from jax import lax
from jax.experimental import pallas as pl
from jax.experimental.pallas import tpu as pltpu
from jax.sharding import PartitionSpec as P

MASKED = -1000000000.0
LANES = 128
SUB = 8
FIELDS = 4
BLOCKS = 16
ALIGN = 4
SLOTS = 4
PARTS = 8
MIB = 1 << 20


def transposed_by_eye(row):
    size = row.shape[1]
    down = lax.broadcasted_iota(jnp.int32, (size, size), 0)
    across = lax.broadcasted_iota(jnp.int32, (size, size), 1)
    return jnp.sum(jnp.where(down == across, row, 0.0), axis=1, keepdims=True)


def one_row(rows):
    return jnp.concatenate([rows[index : index + 1, :] for index in range(rows.shape[0])], axis=1)


def slots_kernel(pass_dev, capacity, cand_ref, slots_ref, target_ref):
    per_device = cand_ref.shape[0]
    ids = one_row(cand_ref[...])
    pairs = ids.shape[1]
    owners = jnp.right_shift(ids, pass_dev.bit_length() - 1)
    earlier = lax.broadcasted_iota(jnp.int32, (pairs, pairs), 0) < lax.broadcasted_iota(
        jnp.int32, (pairs, pairs), 1
    )
    named = owners.astype(jnp.float32)
    same = transposed_by_eye(named) == named
    slots = jnp.sum(jnp.where(same & earlier, 1.0, 0.0), axis=0, keepdims=True).astype(jnp.int32)
    target_ref[...] = owners * capacity + slots
    query = lax.broadcasted_iota(jnp.int32, ids.shape, 1) // (pairs // per_device)
    tagged = (jnp.bitwise_and(ids, pass_dev - 1) * per_device + query + 1).astype(jnp.float32)
    down = lax.broadcasted_iota(jnp.int32, (slots_ref.shape[0], pairs), 0)
    lane = lax.broadcasted_iota(jnp.int32, slots_ref.shape, 1)
    found = jnp.zeros(slots_ref.shape, jnp.float32)
    for slot in range(capacity):
        chosen = jnp.where((down == owners) & (slots == slot), tagged, 0.0)
        found = jnp.where(lane == slot, jnp.sum(chosen, axis=1, keepdims=True), found)
    slots_ref[...] = found.astype(jnp.int32)


def slots_by_owner(cand, devices, pass_dev, capacity):
    vmem = pl.BlockSpec(memory_space=pltpu.VMEM)
    return pl.pallas_call(
        functools.partial(slots_kernel, pass_dev, capacity),
        in_specs=[vmem],
        out_specs=[vmem] * 2,
        out_shape=[
            jax.ShapeDtypeStruct((devices, capacity), jnp.int32),
            jax.ShapeDtypeStruct((1, cand.size), jnp.int32),
        ],
        compiler_params=pltpu.CompilerParams(vmem_limit_bytes=4 * MIB),
        name="slots_by_owner",
    )(cand)


def score_kernel(
    sizes,
    me_ref,
    ids,
    levels_hbm,
    cent_hbm,
    words_hbm,
    codes_hbm,
    lens_hbm,
    *rest,
):
    group_count, cent_count, per_device, query_len, capacity, pass_dev, cand_count = sizes
    query_hbm = rest[:group_count]
    (out_ref, staged, table, words, query_rows, query_t, own_t, dense, embed, maxima, codes, word_stage,
     code_stage, *more) = rest[group_count:]
    code_slots, more = more[:SLOTS], more[SLOTS:]
    (levels_ref, lens, work, work_quad, table_sem, words_sem, query_sem, small_sem,
     slot_sem) = more
    sources = ids.shape[0]
    items = sources * capacity
    tiles = words.shape[0] // (pass_dev * SUB)
    tile_tokens = SUB * FIELDS
    quad_sources = LANES // (per_device * query_len)
    quads = sources // quad_sources
    group_quads = cent_count // quad_sources
    per_bits = per_device.bit_length() - 1
    tile_bits = tiles.bit_length() - 1
    row_at = (pass_dev * tiles - 1).bit_length()
    lane_at = row_at + (items * tiles).bit_length()
    last_at = lane_at + (quad_sources * per_device - 1).bit_length()
    assert last_at + (tiles * tile_tokens - 1).bit_length() < 32
    next_tile = 1 + (1 << row_at) - (tile_tokens << last_at)
    parts = min(quads, PARTS)
    part_rows = staged.shape[0] // parts
    part_quads = quads // parts
    word_parts = words_sem.shape[0]
    part_words = words.shape[0] // word_parts

    def table_copy(part):
        rows = pl.ds(pl.multiple_of(part * part_rows, part_rows), part_rows)
        return pltpu.make_async_copy(cent_hbm.at[rows, :], staged.at[rows, :], table_sem.at[part])

    def words_copy(part):
        rows = pl.ds(part * part_words, part_words)
        return pltpu.make_async_copy(words_hbm.at[rows, :], words.at[rows, :], words_sem.at[part])

    def start_table(part, carry):
        table_copy(part).start()
        return carry

    group = jnp.bitwise_and(me_ref[0], group_count - 1)

    def query_copy(apart):
        return pltpu.make_async_copy(
            query_hbm[apart], query_rows.at[jnp.bitwise_xor(group, apart)], query_sem.at[apart]
        )

    lens_copy = pltpu.make_async_copy(lens_hbm, lens, small_sem.at[0])
    codes_copy = pltpu.make_async_copy(codes_hbm, codes, small_sem.at[1])
    levels_copy = pltpu.make_async_copy(levels_hbm, levels_ref, small_sem.at[2])
    lens_copy.start()
    levels_copy.start()
    for apart in range(group_count):
        query_copy(apart).start()
    lax.fori_loop(0, parts, start_table, 0)
    codes_copy.start()
    for part in range(word_parts):
        words_copy(part).start()

    maxima[...] = jnp.full(maxima.shape, MASKED, jnp.float32)
    query_copy(0).wait()
    own_t[...] = jnp.transpose(query_rows[group].astype(jnp.float32)).astype(jnp.bfloat16)
    lens_copy.wait()
    for apart in range(1, group_count):
        query_copy(apart).wait()

    spare = ((items * tiles) << row_at) - (1 << last_at)

    def fill(quad, count):
        block = query_rows[quad // group_quads, pl.ds(quad % group_quads * LANES, LANES), :]
        query_t[quad] = jnp.transpose(block.astype(jnp.float32)).astype(jnp.bfloat16)
        start = count
        found = []
        for part in range(quad_sources):
            cent = quad % group_quads * quad_sources + part
            source = cent * group_count + quad // group_quads
            rows = jnp.left_shift(source * (capacity * tiles), row_at)
            for slot in range(capacity):
                tag = ids[source, slot] - 1
                lane = part * per_device + jnp.bitwise_and(tag, per_device - 1)
                entry = rows + jnp.left_shift(lane, lane_at) + ((slot * tiles) << row_at)
                found.append((tag, jnp.right_shift(jnp.maximum(tag, 0), per_bits), entry))
        lengths = [lens[passage] for _, passage, _ in found]
        for (tag, passage, entry), length in zip(found, lengths):
            entry = entry + jnp.left_shift(passage, tile_bits) + jnp.left_shift(length - 1, last_at)
            for tile in range(tiles):
                work[count + tile] = entry + tile * next_tile
            blocks = jnp.right_shift(length + tile_tokens - 1, tile_tokens.bit_length() - 1)
            count = count + jnp.where(tag >= 0, blocks, 0)
        for index in range(ALIGN):
            work[count + index] = spare
        count = (count + ALIGN - 1) // ALIGN * ALIGN
        for index in range(quad_sources * capacity * tiles // ALIGN):
            work_quad[start // ALIGN + index] = quad
        return count

    def prepare(part, carry):
        count, best = carry
        table_copy(part).wait()
        rows = pl.ds(pl.multiple_of(part * part_rows, part_rows), part_rows)
        scores = jnp.dot(staged[rows, :], own_t[...], preferred_element_type=jnp.float32)
        best = jnp.maximum(best, jnp.max(scores.reshape(part_rows // SUB, SUB, scores.shape[1]), axis=0))
        table[rows, :] = staged[rows, :].astype(jnp.float32)
        for index in range(part_quads):
            count = fill(part * part_quads + index, count)
        return count, best

    lowest = jnp.full((SUB, own_t.shape[1]), -jnp.inf, jnp.float32)
    total, token_best = lax.fori_loop(0, parts, prepare, (0, lowest))
    token_best = jnp.max(token_best, axis=0, keepdims=True)
    for index in range((SLOTS + 1) * BLOCKS):
        work[total + index] = spare
    for index in range(2 * BLOCKS // ALIGN):
        work_quad[total // ALIGN + index] = 0
    chunks = jnp.maximum((total + BLOCKS - 1) // BLOCKS, 2)
    codes_copy.wait()
    levels_copy.wait()
    for part in range(word_parts):
        words_copy(part).wait()

    sub = lax.broadcasted_iota(jnp.int32, (SUB, LANES), 0)
    position = jnp.concatenate([sub * FIELDS + field for field in range(FIELDS)], axis=0)
    row_blocks = LANES // tile_tokens
    lane_tile = lax.broadcasted_iota(jnp.int32, (1, LANES), 1) // tile_tokens
    lane_group = lax.broadcasted_iota(jnp.int32, (1, LANES), 1) // query_len
    level = [levels_ref[index : index + 1, :] for index in range(FIELDS)]

    def score(chunk):
        scores = []
        for part in range(BLOCKS // ALIGN):
            rows = embed[part * ALIGN * tile_tokens : (part + 1) * ALIGN * tile_tokens, :]
            quad = work_quad[chunk * (BLOCKS // ALIGN) + part]
            scores.append(jnp.dot(rows, query_t[quad], preferred_element_type=jnp.float32))
        for index in range(BLOCKS):
            entry = work[chunk * BLOCKS + index]
            inner = index % ALIGN
            block = scores[index // ALIGN][inner * tile_tokens : (inner + 1) * tile_tokens]
            kept = jnp.where(position <= jnp.right_shift(entry, last_at), block, MASKED)
            best = jnp.max(kept, axis=0, keepdims=True)
            row = jnp.bitwise_and(jnp.right_shift(entry, row_at), (1 << (lane_at - row_at)) - 1)
            lane = jnp.bitwise_and(jnp.right_shift(entry, lane_at), (1 << (last_at - lane_at)) - 1)
            maxima[pl.ds(row, 1), :] = jnp.where(lane_group == lane, best, 0.0)

    def slot_copy(slot):
        return pltpu.make_async_copy(code_stage.at[slot], code_slots[slot], slot_sem.at[slot])

    def fetch_codes(chunk, slot):
        places = []
        for row in range(BLOCKS // row_blocks):
            together = jnp.zeros((1, LANES), jnp.int32)
            for index in range(row_blocks):
                entry = work[chunk * BLOCKS + row * row_blocks + index]
                place = jnp.bitwise_and(entry, (1 << row_at) - 1)
                passage = jnp.right_shift(place, tile_bits)
                shift = jnp.bitwise_and(index - place, row_blocks - 1) * tile_tokens
                moved = pltpu.roll(codes[pl.ds(passage, 1), :], shift, 1)
                together = jnp.where(lane_tile == index, moved, together)
                places.append(place)
            code_stage[slot, row : row + 1, :] = together
        return places

    def fetch_words(places, slot):
        for block, place in enumerate(places):
            rows = pl.ds(pl.multiple_of(place * SUB, SUB), SUB)
            word_stage[slot, block * SUB : (block + 1) * SUB, :] = words[rows, :]

    def decode(slot):
        for index in range(BLOCKS):
            word = word_stage[slot, index * SUB : (index + 1) * SUB, :]
            for field in range(FIELDS):
                rows = jnp.zeros((SUB, LANES), jnp.float32)
                for row in range(SUB):
                    place = index % row_blocks * tile_tokens + row * FIELDS + field
                    code = code_slots[slot][index // row_blocks, place]
                    rows = jnp.where(sub == row, table[pl.ds(code, SUB, stride=0), :], rows)
                low = jnp.bitwise_and(word, 1 << (2 * field)) != 0
                high = jnp.bitwise_and(word, 2 << (2 * field)) != 0
                residual = jnp.where(
                    high, jnp.where(low, level[3], level[2]), jnp.where(low, level[1], level[0])
                )
                base = index * tile_tokens + field * SUB
                dense[base : base + SUB, :] = rows + residual

    def normalize():
        for index in range(BLOCKS):
            rows = slice(index * tile_tokens, (index + 1) * tile_tokens)
            block = dense[rows, :]
            inverse = lax.rsqrt(jnp.sum(block * block, axis=1, keepdims=True) + 1e-06)
            embed[rows, :] = (block * inverse).astype(jnp.bfloat16)

    dense[...] = jnp.zeros(dense.shape, dense.dtype)
    embed[...] = jnp.zeros(embed.shape, embed.dtype)
    for slot in range(SLOTS):
        fetch_words(fetch_codes(slot, slot), slot)
        if slot < 2:
            slot_copy(slot).start()
        elif slot < SLOTS - 1:
            pl.when(slot < chunks)(slot_copy(slot).start)

    def step(group, carry):
        for slot in range(SLOTS):
            chunk = SLOTS * group + slot
            pl.when(chunk + SLOTS - 1 < chunks)(slot_copy((slot + SLOTS - 1) % SLOTS).start)

            @pl.when(chunk < chunks)
            def _(chunk=chunk, slot=slot):
                slot_copy(slot).wait()
                score(jnp.maximum(chunk - 2, 0))
                normalize()
                places = fetch_codes(chunk + SLOTS, slot)
                decode(slot)
                fetch_words(places, slot)

        return carry

    lax.fori_loop(0, (chunks + SLOTS - 1) // SLOTS, step, 0)
    score(chunks - 2)
    normalize()
    score(chunks - 1)

    best = maxima[pl.ds(0, items, stride=tiles), :]
    for tile in range(1, tiles):
        best = jnp.maximum(best, maxima[pl.ds(tile, items, stride=tiles), :])
    sums = jnp.sum(best, axis=1, keepdims=True) / query_len
    item_down = lax.broadcasted_iota(jnp.int32, (items, LANES), 0)
    item_slot = lax.broadcasted_iota(jnp.int32, (items, LANES), 1)
    spread = jnp.where(item_down % capacity == item_slot, sums, 0.0)
    source_down = lax.broadcasted_iota(jnp.int32, (sources, items), 0)
    item_across = lax.broadcasted_iota(jnp.int32, (sources, items), 1)
    gather = (item_across // capacity == source_down).astype(jnp.float32)
    by_source = jnp.dot(
        gather, spread, precision=lax.Precision.HIGHEST, preferred_element_type=jnp.float32
    )
    best_lanes = token_best.shape[1]
    for source in range(sources):
        out_ref[source, :, :best_lanes] = token_best
        out_ref[source, :, best_lanes:] = by_source[source : source + 1, :]


def owner_scores(me, slots, query_parts, centroids, token_codes, resid_words, lengths, levels, sizes):
    capacity = sizes[4]
    sources = slots.shape[0]
    group_count = len(query_parts)
    group_rows = query_parts[0].shape[0]
    cent_dev, width = centroids.shape
    pass_dev, plen = token_codes.shape
    packed = resid_words.shape[1]
    tiles = packed // SUB
    items = sources * capacity
    quads = group_count * group_rows // LANES
    work_size = items * tiles + quads * ALIGN + (SLOTS + 1) * BLOCKS
    any_space = pl.BlockSpec(memory_space=pl.ANY)
    in_hbm = pl.BlockSpec(memory_space=pltpu.HBM)
    pinned = [
        pltpu.with_memory_space_constraint(array, pltpu.HBM)
        for array in (levels, centroids, resid_words.reshape(pass_dev * packed, width), token_codes, lengths, query_parts[0])
    ]
    vmem = pl.BlockSpec(memory_space=pltpu.VMEM)
    tokens = items * plen
    return pl.pallas_call(
        functools.partial(score_kernel, sizes),
        in_specs=[pl.BlockSpec(memory_space=pltpu.SMEM)] * 2 + [in_hbm] * 6 + [any_space] * (group_count - 1),
        out_specs=vmem,
        out_shape=jax.ShapeDtypeStruct((sources, 1, group_rows + LANES), jnp.float32),
        scratch_shapes=[
            pltpu.VMEM((cent_dev, width), jnp.bfloat16),
            pltpu.VMEM((cent_dev + SUB, width), jnp.float32),
            pltpu.VMEM((pass_dev * packed, width), jnp.int32),
            pltpu.VMEM((group_count, group_rows, width), jnp.bfloat16),
            pltpu.VMEM((quads, width, LANES), jnp.bfloat16),
            pltpu.VMEM((width, group_rows), jnp.bfloat16),
            pltpu.VMEM((BLOCKS * SUB * FIELDS, width), jnp.float32),
            pltpu.VMEM((BLOCKS * SUB * FIELDS, width), jnp.bfloat16),
            pltpu.VMEM((items * tiles + SUB, LANES), jnp.float32),
            pltpu.VMEM((pass_dev, plen), jnp.int32),
            pltpu.VMEM((SLOTS, BLOCKS * SUB, LANES), jnp.int32),
            pltpu.VMEM((SLOTS, BLOCKS * SUB * FIELDS // LANES, LANES), jnp.int32),
            *[pltpu.SMEM((BLOCKS * SUB * FIELDS // LANES, LANES), jnp.int32)] * SLOTS,
            pltpu.VMEM(levels.shape, jnp.float32),
            pltpu.SMEM((pass_dev,), jnp.int32),
            pltpu.SMEM((work_size,), jnp.int32),
            pltpu.SMEM((work_size // ALIGN + items * tiles // quads,), jnp.int32),
            pltpu.SemaphoreType.DMA((min(quads, PARTS),)),
            pltpu.SemaphoreType.DMA((4,)),
            pltpu.SemaphoreType.DMA((group_count,)),
            pltpu.SemaphoreType.DMA((3,)),
            pltpu.SemaphoreType.DMA((SLOTS,)),
        ],
        compiler_params=pltpu.CompilerParams(vmem_limit_bytes=44 * MIB),
        cost_estimate=pl.CostEstimate(
            flops=2 * (tokens * LANES + cent_dev * group_rows) * width, bytes_accessed=2 * cent_dev * width * 2, transcendentals=tokens
        ),
        name="owner_scores",
    )(
        me, slots, *pinned, *query_parts[1:]
    )


def finish_kernel(sizes, me_ref, back_ref, target_ref, best_out, score_out):
    group_count, cent_count, _, query_len, capacity, _, _ = sizes
    group = jnp.bitwise_and(me_ref[0], group_count - 1)
    best_lanes = best_out.shape[0] * query_len
    best = back_ref[group, :, :best_lanes]
    for cent in range(1, cent_count):
        best = jnp.maximum(best, back_ref[cent * group_count + group, :, :best_lanes])
    for index in range(best_out.shape[0]):
        best_out[index : index + 1, :] = best[:, index * query_len : (index + 1) * query_len]
    back = back_ref[:, 0, best_lanes:]
    target = target_ref[...]
    owner = lax.broadcasted_iota(jnp.int32, (back.shape[0], target.shape[1]), 0)
    found = jnp.zeros(owner.shape, jnp.float32)
    for slot in range(capacity):
        found = found + jnp.where(owner * capacity + slot == target, back[:, slot : slot + 1], 0.0)
    scores = jnp.sum(found, axis=0, keepdims=True)
    width = score_out.shape[1]
    for index in range(score_out.shape[0]):
        score_out[index : index + 1, :] = scores[:, index * width : (index + 1) * width]


def finish(me, back, target, group_rows, sizes):
    _, _, per_device, query_len, _, _, cand_count = sizes
    vmem = pl.BlockSpec(memory_space=pltpu.VMEM)
    return pl.pallas_call(
        functools.partial(finish_kernel, sizes),
        in_specs=[pl.BlockSpec(memory_space=pltpu.SMEM), vmem, vmem],
        out_specs=[vmem] * 2,
        out_shape=[
            jax.ShapeDtypeStruct((group_rows, query_len), jnp.float32),
            jax.ShapeDtypeStruct((per_device, cand_count), jnp.float32),
        ],
        compiler_params=pltpu.CompilerParams(vmem_limit_bytes=4 * MIB),
        name="finish",
    )(me, back, target)


def shards(queries, centroids, candidates, token_codes, resid_words, lengths, levels):
    group_rows, query_len, width = queries.shape
    pass_dev = token_codes.shape[0]
    per_device, cand_count = candidates.shape[2:]
    pair_count = per_device * cand_count
    cent_count = lax.axis_size("cent")
    group_count = lax.axis_size("grp")
    devices = cent_count * group_count
    capacity = max(2, 2 * pair_count // devices)
    sizes = (group_count, cent_count, per_device, query_len, capacity, pass_dev, cand_count)
    cand = candidates.reshape(per_device, cand_count)
    query_rows = queries.reshape(group_rows * query_len, width)
    me = (lax.axis_index("cent") * group_count + lax.axis_index("grp")).astype(jnp.int32).reshape(1)
    slots, target = slots_by_owner(cand, devices, pass_dev, capacity)
    slots = lax.all_to_all(slots, ("cent", "grp"), split_axis=0, concat_axis=0, tiled=True)
    query_parts = [query_rows]
    for apart in range(1, group_count):
        pairs = [(index, index ^ apart) for index in range(group_count)]
        query_parts.append(lax.ppermute(query_rows, "grp", pairs))
    reply = owner_scores(
        me, slots, query_parts, centroids, token_codes, resid_words, lengths, levels, sizes
    )
    back = lax.all_to_all(reply, ("cent", "grp"), split_axis=0, concat_axis=0, tiled=True)
    token_best, scores = finish(me, back, target, group_rows, sizes)
    return (token_best, scores.reshape(1, 1, per_device, cand_count))


def solution(mesh):
    placed = (
        P("grp", None, None),
        P("cent", None),
        P("grp", "cent", None, None),
        P(("cent", "grp"), None),
        P(("cent", "grp"), None, None),
        P(("cent", "grp")),
        P(),
    )
    return jax.shard_map(
        shards,
        mesh=mesh,
        in_specs=placed,
        out_specs=(P("grp", None), P("grp", "cent", None, None)),
        check_vma=False,
    )
```

```python
import functools

import jax
import jax.numpy as jnp
from jax import lax
from jax.experimental import pallas as pl
from jax.experimental.pallas import tpu as pltpu
from jax.sharding import PartitionSpec as P

MASKED = -1000000000.0
LANES = 128
SUB = 8
FIELDS = 4
BLOCKS = 16
ALIGN = 4
SLOTS = 4
PARTS = 8
MIB = 1 << 20


def transposed_by_eye(row):
    size = row.shape[1]
    down = lax.broadcasted_iota(jnp.int32, (size, size), 0)
    across = lax.broadcasted_iota(jnp.int32, (size, size), 1)
    return jnp.sum(jnp.where(down == across, row, 0.0), axis=1, keepdims=True)


def one_row(rows):
    return jnp.concatenate([rows[index : index + 1, :] for index in range(rows.shape[0])], axis=1)


def slots_kernel(pass_dev, capacity, cand_ref, slots_ref, target_ref):
    per_device = cand_ref.shape[0]
    ids = one_row(cand_ref[...])
    pairs = ids.shape[1]
    owners = jnp.right_shift(ids, pass_dev.bit_length() - 1)
    earlier = lax.broadcasted_iota(jnp.int32, (pairs, pairs), 0) < lax.broadcasted_iota(
        jnp.int32, (pairs, pairs), 1
    )
    named = owners.astype(jnp.float32)
    same = transposed_by_eye(named) == named
    slots = jnp.sum(jnp.where(same & earlier, 1.0, 0.0), axis=0, keepdims=True).astype(jnp.int32)
    target_ref[...] = owners * capacity + slots
    query = lax.broadcasted_iota(jnp.int32, ids.shape, 1) // (pairs // per_device)
    tagged = (jnp.bitwise_and(ids, pass_dev - 1) * per_device + query + 1).astype(jnp.float32)
    down = lax.broadcasted_iota(jnp.int32, (slots_ref.shape[0], pairs), 0)
    lane = lax.broadcasted_iota(jnp.int32, slots_ref.shape, 1)
    found = jnp.zeros(slots_ref.shape, jnp.float32)
    for slot in range(capacity):
        chosen = jnp.where((down == owners) & (slots == slot), tagged, 0.0)
        found = jnp.where(lane == slot, jnp.sum(chosen, axis=1, keepdims=True), found)
    slots_ref[...] = found.astype(jnp.int32)


def slots_by_owner(cand, devices, pass_dev, capacity):
    vmem = pl.BlockSpec(memory_space=pltpu.VMEM)
    return pl.pallas_call(
        functools.partial(slots_kernel, pass_dev, capacity),
        in_specs=[vmem],
        out_specs=[vmem] * 2,
        out_shape=[
            jax.ShapeDtypeStruct((devices, capacity), jnp.int32),
            jax.ShapeDtypeStruct((1, cand.size), jnp.int32),
        ],
        compiler_params=pltpu.CompilerParams(vmem_limit_bytes=4 * MIB),
        name="slots_by_owner",
    )(cand)


def score_kernel(
    sizes,
    me_ref,
    ids,
    levels_hbm,
    cent_hbm,
    words_hbm,
    codes_hbm,
    lens_hbm,
    *rest,
):
    group_count, cent_count, per_device, query_len, capacity, pass_dev, cand_count = sizes
    query_hbm = rest[:group_count]
    (out_ref, staged, table, words, query_rows, query_t, own_t, dense, embed, maxima, codes, word_stage,
     code_stage, *more) = rest[group_count:]
    code_slots, more = more[:SLOTS], more[SLOTS:]
    (levels_ref, lens, work, work_quad, table_sem, words_sem, query_sem, small_sem,
     slot_sem) = more
    sources = ids.shape[0]
    items = sources * capacity
    tiles = words.shape[0] // (pass_dev * SUB)
    tile_tokens = SUB * FIELDS
    quad_sources = LANES // (per_device * query_len)
    quads = sources // quad_sources
    group_quads = cent_count // quad_sources
    per_bits = per_device.bit_length() - 1
    tile_bits = tiles.bit_length() - 1
    row_at = (pass_dev * tiles - 1).bit_length()
    lane_at = row_at + (items * tiles).bit_length()
    last_at = lane_at + (quad_sources * per_device - 1).bit_length()
    assert last_at + (tiles * tile_tokens - 1).bit_length() < 32
    next_tile = 1 + (1 << row_at) - (tile_tokens << last_at)
    parts = min(quads, PARTS)
    part_rows = staged.shape[0] // parts
    part_quads = quads // parts
    word_parts = words_sem.shape[0]
    part_words = words.shape[0] // word_parts

    def table_copy(part):
        rows = pl.ds(pl.multiple_of(part * part_rows, part_rows), part_rows)
        return pltpu.make_async_copy(cent_hbm.at[rows, :], staged.at[rows, :], table_sem.at[part])

    def words_copy(part):
        rows = pl.ds(part * part_words, part_words)
        return pltpu.make_async_copy(words_hbm.at[rows, :], words.at[rows, :], words_sem.at[part])

    def start_table(part, carry):
        table_copy(part).start()
        return carry

    group = jnp.bitwise_and(me_ref[0], group_count - 1)

    def query_copy(apart):
        return pltpu.make_async_copy(
            query_hbm[apart], query_rows.at[jnp.bitwise_xor(group, apart)], query_sem.at[apart]
        )

    lens_copy = pltpu.make_async_copy(lens_hbm, lens, small_sem.at[0])
    codes_copy = pltpu.make_async_copy(codes_hbm, codes, small_sem.at[1])
    levels_copy = pltpu.make_async_copy(levels_hbm, levels_ref, small_sem.at[2])
    lens_copy.start()
    levels_copy.start()
    for apart in range(group_count):
        query_copy(apart).start()
    lax.fori_loop(0, parts, start_table, 0)
    codes_copy.start()
    for part in range(word_parts):
        words_copy(part).start()

    maxima[...] = jnp.full(maxima.shape, MASKED, jnp.float32)
    query_copy(0).wait()
    own_t[...] = jnp.transpose(query_rows[group].astype(jnp.float32)).astype(jnp.bfloat16)
    lens_copy.wait()
    for apart in range(1, group_count):
        query_copy(apart).wait()

    spare = ((items * tiles) << row_at) - (1 << last_at)

    def fill(quad, count):
        block = query_rows[quad // group_quads, pl.ds(quad % group_quads * LANES, LANES), :]
        query_t[quad] = jnp.transpose(block.astype(jnp.float32)).astype(jnp.bfloat16)
        start = count
        found = []
        for part in range(quad_sources):
            cent = quad % group_quads * quad_sources + part
            source = cent * group_count + quad // group_quads
            rows = jnp.left_shift(source * (capacity * tiles), row_at)
            for slot in range(capacity):
                tag = ids[source, slot] - 1
                lane = part * per_device + jnp.bitwise_and(tag, per_device - 1)
                entry = rows + jnp.left_shift(lane, lane_at) + ((slot * tiles) << row_at)
                found.append((tag, jnp.right_shift(jnp.maximum(tag, 0), per_bits), entry))
        lengths = [lens[passage] for _, passage, _ in found]
        for (tag, passage, entry), length in zip(found, lengths):
            entry = entry + jnp.left_shift(passage, tile_bits) + jnp.left_shift(length - 1, last_at)
            for tile in range(tiles):
                work[count + tile] = entry + tile * next_tile
            blocks = jnp.right_shift(length + tile_tokens - 1, tile_tokens.bit_length() - 1)
            count = count + jnp.where(tag >= 0, blocks, 0)
        for index in range(ALIGN):
            work[count + index] = spare
        count = (count + ALIGN - 1) // ALIGN * ALIGN
        for index in range(quad_sources * capacity * tiles // ALIGN):
            work_quad[start // ALIGN + index] = quad
        return count

    def prepare(part, carry):
        count, best = carry
        table_copy(part).wait()
        rows = pl.ds(pl.multiple_of(part * part_rows, part_rows), part_rows)
        scores = jnp.dot(staged[rows, :], own_t[...], preferred_element_type=jnp.float32)
        best = jnp.maximum(best, jnp.max(scores.reshape(part_rows // SUB, SUB, scores.shape[1]), axis=0))
        table[rows, :] = staged[rows, :].astype(jnp.float32)
        for index in range(part_quads):
            count = fill(part * part_quads + index, count)
        return count, best

    lowest = jnp.full((SUB, own_t.shape[1]), -jnp.inf, jnp.float32)
    total, token_best = lax.fori_loop(0, parts, prepare, (0, lowest))
    token_best = jnp.max(token_best, axis=0, keepdims=True)
    for index in range((SLOTS + 2) * BLOCKS):
        work[total + index] = spare
    for index in range(2 * BLOCKS // ALIGN):
        work_quad[total // ALIGN + index] = 0
    chunks = jnp.maximum((total + BLOCKS - 1) // BLOCKS, 2)
    codes_copy.wait()
    levels_copy.wait()
    for part in range(word_parts):
        words_copy(part).wait()

    sub = lax.broadcasted_iota(jnp.int32, (SUB, LANES), 0)
    position = jnp.concatenate([sub * FIELDS + field for field in range(FIELDS)], axis=0)
    row_blocks = LANES // tile_tokens
    lane_tile = lax.broadcasted_iota(jnp.int32, (1, LANES), 1) // tile_tokens
    lane_group = lax.broadcasted_iota(jnp.int32, (1, LANES), 1) // query_len
    level = [levels_ref[index : index + 1, :] for index in range(FIELDS)]

    def score(chunk):
        scores = []
        for part in range(BLOCKS // ALIGN):
            rows = embed[part * ALIGN * tile_tokens : (part + 1) * ALIGN * tile_tokens, :]
            quad = work_quad[chunk * (BLOCKS // ALIGN) + part]
            scores.append(jnp.dot(rows, query_t[quad], preferred_element_type=jnp.float32))
        for index in range(BLOCKS):
            entry = work[chunk * BLOCKS + index]
            inner = index % ALIGN
            block = scores[index // ALIGN][inner * tile_tokens : (inner + 1) * tile_tokens]
            kept = jnp.where(position <= jnp.right_shift(entry, last_at), block, MASKED)
            best = jnp.max(kept, axis=0, keepdims=True)
            row = jnp.bitwise_and(jnp.right_shift(entry, row_at), (1 << (lane_at - row_at)) - 1)
            lane = jnp.bitwise_and(jnp.right_shift(entry, lane_at), (1 << (last_at - lane_at)) - 1)
            maxima[pl.ds(row, 1), :] = jnp.where(lane_group == lane, best, 0.0)

    def slot_copy(slot):
        return pltpu.make_async_copy(code_stage.at[slot], code_slots[slot], slot_sem.at[slot])

    def fetch_codes(chunk, slot):
        places = []
        for row in range(BLOCKS // row_blocks):
            together = jnp.zeros((1, LANES), jnp.int32)
            for index in range(row_blocks):
                entry = work[chunk * BLOCKS + row * row_blocks + index]
                place = jnp.bitwise_and(entry, (1 << row_at) - 1)
                passage = jnp.right_shift(place, tile_bits)
                shift = jnp.bitwise_and(index - place, row_blocks - 1) * tile_tokens
                moved = pltpu.roll(codes[pl.ds(passage, 1), :], shift, 1)
                together = jnp.where(lane_tile == index, moved, together)
                places.append(place)
            code_stage[slot, row : row + 1, :] = together
        return places

    def fetch_words(places, slot):
        for block, place in enumerate(places):
            rows = pl.ds(pl.multiple_of(place * SUB, SUB), SUB)
            word_stage[slot, block * SUB : (block + 1) * SUB, :] = words[rows, :]

    def decode(slot):
        for index in range(BLOCKS):
            word = word_stage[slot, index * SUB : (index + 1) * SUB, :]
            for field in range(FIELDS):
                rows = jnp.zeros((SUB, LANES), jnp.float32)
                for row in range(SUB):
                    place = index % row_blocks * tile_tokens + row * FIELDS + field
                    code = code_slots[slot][index // row_blocks, place]
                    rows = jnp.where(sub == row, table[pl.ds(code, SUB, stride=0), :], rows)
                low = jnp.bitwise_and(word, 1 << (2 * field)) != 0
                high = jnp.bitwise_and(word, 2 << (2 * field)) != 0
                residual = jnp.where(
                    high, jnp.where(low, level[3], level[2]), jnp.where(low, level[1], level[0])
                )
                base = index * tile_tokens + field * SUB
                dense[base : base + SUB, :] = rows + residual

    def normalize():
        for index in range(BLOCKS):
            rows = slice(index * tile_tokens, (index + 1) * tile_tokens)
            block = dense[rows, :]
            inverse = lax.rsqrt(jnp.sum(block * block, axis=1, keepdims=True) + 1e-06)
            embed[rows, :] = (block * inverse).astype(jnp.bfloat16)

    dense[...] = jnp.zeros(dense.shape, dense.dtype)
    embed[...] = jnp.zeros(embed.shape, embed.dtype)
    for slot in range(SLOTS):
        fetch_words(fetch_codes(slot, slot), slot)
        if slot < 2:
            slot_copy(slot).start()
        elif slot < SLOTS - 1:
            pl.when(slot < chunks)(slot_copy(slot).start)

    best_lanes = token_best.shape[1]
    for source in range(sources):
        out_ref[source, :, :best_lanes] = token_best

    def step(group, carry):
        for slot in range(SLOTS):
            chunk = SLOTS * group + slot
            pl.when(chunk + SLOTS - 1 < chunks)(slot_copy((slot + SLOTS - 1) % SLOTS).start)

            @pl.when(chunk < chunks)
            def _(chunk=chunk, slot=slot):
                slot_copy(slot).wait()
                score(jnp.maximum(chunk - 2, 0))
                normalize()
                places = fetch_codes(chunk + SLOTS, slot)
                decode(slot)
                fetch_words(places, slot)

        return carry

    lax.fori_loop(0, (chunks + SLOTS - 1) // SLOTS, step, 0)
    score(chunks - 2)
    normalize()
    score(chunks - 1)

    best = maxima[pl.ds(0, items, stride=tiles), :]
    for tile in range(1, tiles):
        best = jnp.maximum(best, maxima[pl.ds(tile, items, stride=tiles), :])
    sums = jnp.sum(best, axis=1, keepdims=True) / query_len
    item_down = lax.broadcasted_iota(jnp.int32, (items, LANES), 0)
    item_slot = lax.broadcasted_iota(jnp.int32, (items, LANES), 1)
    spread = jnp.where(item_down % capacity == item_slot, sums, 0.0)
    source_down = lax.broadcasted_iota(jnp.int32, (sources, items), 0)
    item_across = lax.broadcasted_iota(jnp.int32, (sources, items), 1)
    gather = (item_across // capacity == source_down).astype(jnp.float32)
    by_source = jnp.dot(
        gather, spread, precision=lax.Precision.HIGHEST, preferred_element_type=jnp.float32
    )
    for source in range(sources):
        out_ref[source, :, best_lanes:] = by_source[source : source + 1, :]


def owner_scores(me, slots, query_parts, centroids, token_codes, resid_words, lengths, levels, sizes):
    capacity = sizes[4]
    sources = slots.shape[0]
    group_count = len(query_parts)
    group_rows = query_parts[0].shape[0]
    cent_dev, width = centroids.shape
    pass_dev, plen = token_codes.shape
    packed = resid_words.shape[1]
    tiles = packed // SUB
    items = sources * capacity
    quads = group_count * group_rows // LANES
    work_size = items * tiles + quads * ALIGN + (SLOTS + 2) * BLOCKS
    any_space = pl.BlockSpec(memory_space=pl.ANY)
    in_hbm = pl.BlockSpec(memory_space=pltpu.HBM)
    pinned = [
        pltpu.with_memory_space_constraint(array, pltpu.HBM)
        for array in (levels, centroids, resid_words.reshape(pass_dev * packed, width), token_codes, lengths, query_parts[0])
    ]
    vmem = pl.BlockSpec(memory_space=pltpu.VMEM)
    tokens = items * plen
    return pl.pallas_call(
        functools.partial(score_kernel, sizes),
        in_specs=[pl.BlockSpec(memory_space=pltpu.SMEM)] * 2 + [in_hbm] * 6 + [any_space] * (group_count - 1),
        out_specs=vmem,
        out_shape=jax.ShapeDtypeStruct((sources, 1, group_rows + LANES), jnp.float32),
        scratch_shapes=[
            pltpu.VMEM((cent_dev, width), jnp.bfloat16),
            pltpu.VMEM((cent_dev + SUB, width), jnp.float32),
            pltpu.VMEM((pass_dev * packed, width), jnp.int32),
            pltpu.VMEM((group_count, group_rows, width), jnp.bfloat16),
            pltpu.VMEM((quads, width, LANES), jnp.bfloat16),
            pltpu.VMEM((width, group_rows), jnp.bfloat16),
            pltpu.VMEM((BLOCKS * SUB * FIELDS, width), jnp.float32),
            pltpu.VMEM((BLOCKS * SUB * FIELDS, width), jnp.bfloat16),
            pltpu.VMEM((items * tiles + SUB, LANES), jnp.float32),
            pltpu.VMEM((pass_dev, plen), jnp.int32),
            pltpu.VMEM((SLOTS, BLOCKS * SUB, LANES), jnp.int32),
            pltpu.VMEM((SLOTS, BLOCKS * SUB * FIELDS // LANES, LANES), jnp.int32),
            *[pltpu.SMEM((BLOCKS * SUB * FIELDS // LANES, LANES), jnp.int32)] * SLOTS,
            pltpu.VMEM(levels.shape, jnp.float32),
            pltpu.SMEM((pass_dev,), jnp.int32),
            pltpu.SMEM((work_size,), jnp.int32),
            pltpu.SMEM((work_size // ALIGN + items * tiles // quads,), jnp.int32),
            pltpu.SemaphoreType.DMA((min(quads, PARTS),)),
            pltpu.SemaphoreType.DMA((4,)),
            pltpu.SemaphoreType.DMA((group_count,)),
            pltpu.SemaphoreType.DMA((3,)),
            pltpu.SemaphoreType.DMA((SLOTS,)),
        ],
        compiler_params=pltpu.CompilerParams(vmem_limit_bytes=44 * MIB),
        cost_estimate=pl.CostEstimate(
            flops=2 * (tokens * LANES + cent_dev * group_rows) * width, bytes_accessed=2 * cent_dev * width * 2, transcendentals=tokens
        ),
        name="owner_scores",
    )(
        me, slots, *pinned, *query_parts[1:]
    )


def finish_kernel(sizes, me_ref, back_ref, target_ref, best_out, score_out):
    group_count, cent_count, _, query_len, capacity, _, _ = sizes
    group = jnp.bitwise_and(me_ref[0], group_count - 1)
    best_lanes = best_out.shape[0] * query_len
    best = back_ref[group, :, :best_lanes]
    for cent in range(1, cent_count):
        best = jnp.maximum(best, back_ref[cent * group_count + group, :, :best_lanes])
    for index in range(best_out.shape[0]):
        best_out[index : index + 1, :] = best[:, index * query_len : (index + 1) * query_len]
    back = back_ref[:, 0, best_lanes:]
    target = target_ref[...]
    owner = lax.broadcasted_iota(jnp.int32, (back.shape[0], target.shape[1]), 0)
    found = jnp.zeros(owner.shape, jnp.float32)
    for slot in range(capacity):
        found = found + jnp.where(owner * capacity + slot == target, back[:, slot : slot + 1], 0.0)
    scores = jnp.sum(found, axis=0, keepdims=True)
    width = score_out.shape[1]
    for index in range(score_out.shape[0]):
        score_out[index : index + 1, :] = scores[:, index * width : (index + 1) * width]


def finish(me, back, target, group_rows, sizes):
    _, _, per_device, query_len, _, _, cand_count = sizes
    vmem = pl.BlockSpec(memory_space=pltpu.VMEM)
    return pl.pallas_call(
        functools.partial(finish_kernel, sizes),
        in_specs=[pl.BlockSpec(memory_space=pltpu.SMEM), vmem, vmem],
        out_specs=[vmem] * 2,
        out_shape=[
            jax.ShapeDtypeStruct((group_rows, query_len), jnp.float32),
            jax.ShapeDtypeStruct((per_device, cand_count), jnp.float32),
        ],
        compiler_params=pltpu.CompilerParams(vmem_limit_bytes=4 * MIB),
        name="finish",
    )(me, back, target)


def shards(queries, centroids, candidates, token_codes, resid_words, lengths, levels):
    group_rows, query_len, width = queries.shape
    pass_dev = token_codes.shape[0]
    per_device, cand_count = candidates.shape[2:]
    pair_count = per_device * cand_count
    cent_count = lax.axis_size("cent")
    group_count = lax.axis_size("grp")
    devices = cent_count * group_count
    capacity = max(2, 2 * pair_count // devices)
    sizes = (group_count, cent_count, per_device, query_len, capacity, pass_dev, cand_count)
    cand = candidates.reshape(per_device, cand_count)
    query_rows = queries.reshape(group_rows * query_len, width)
    me = (lax.axis_index("cent") * group_count + lax.axis_index("grp")).astype(jnp.int32).reshape(1)
    slots, target = slots_by_owner(cand, devices, pass_dev, capacity)
    slots = lax.all_to_all(slots, ("cent", "grp"), split_axis=0, concat_axis=0, tiled=True)
    query_parts = [query_rows]
    for apart in range(1, group_count):
        pairs = [(index, index ^ apart) for index in range(group_count)]
        query_parts.append(lax.ppermute(query_rows, "grp", pairs))
    reply = owner_scores(
        me, slots, query_parts, centroids, token_codes, resid_words, lengths, levels, sizes
    )
    back = lax.all_to_all(reply, ("cent", "grp"), split_axis=0, concat_axis=0, tiled=True)
    token_best, scores = finish(me, back, target, group_rows, sizes)
    return (token_best, scores.reshape(1, 1, per_device, cand_count))


def solution(mesh):
    placed = (
        P("grp", None, None),
        P("cent", None),
        P("grp", "cent", None, None),
        P(("cent", "grp"), None),
        P(("cent", "grp"), None, None),
        P(("cent", "grp")),
        P(),
    )
    return jax.shard_map(
        shards,
        mesh=mesh,
        in_specs=placed,
        out_specs=(P("grp", None), P("grp", "cent", None, None)),
        check_vma=False,
    )
```

```python
import functools

import jax
import jax.numpy as jnp
from jax import lax
from jax.experimental import pallas as pl
from jax.experimental.pallas import tpu as pltpu
from jax.sharding import PartitionSpec as P

MASKED = -1000000000.0
LANES = 128
SUB = 8
FIELDS = 4
BLOCKS = 16
ALIGN = 4
SLOTS = 4
PARTS = 4
MIB = 1 << 20


def transposed_by_eye(row):
    size = row.shape[1]
    down = lax.broadcasted_iota(jnp.int32, (size, size), 0)
    across = lax.broadcasted_iota(jnp.int32, (size, size), 1)
    return jnp.sum(jnp.where(down == across, row, 0.0), axis=1, keepdims=True)


def one_row(rows):
    return jnp.concatenate([rows[index : index + 1, :] for index in range(rows.shape[0])], axis=1)


def slots_kernel(pass_dev, capacity, cand_ref, slots_ref, target_ref):
    per_device = cand_ref.shape[0]
    ids = one_row(cand_ref[...])
    pairs = ids.shape[1]
    owners = jnp.right_shift(ids, pass_dev.bit_length() - 1)
    earlier = lax.broadcasted_iota(jnp.int32, (pairs, pairs), 0) < lax.broadcasted_iota(
        jnp.int32, (pairs, pairs), 1
    )
    named = owners.astype(jnp.float32)
    same = transposed_by_eye(named) == named
    slots = jnp.sum(jnp.where(same & earlier, 1.0, 0.0), axis=0, keepdims=True).astype(jnp.int32)
    target_ref[...] = owners * capacity + slots
    query = lax.broadcasted_iota(jnp.int32, ids.shape, 1) // (pairs // per_device)
    tagged = (jnp.bitwise_and(ids, pass_dev - 1) * per_device + query + 1).astype(jnp.float32)
    down = lax.broadcasted_iota(jnp.int32, (slots_ref.shape[0], pairs), 0)
    lane = lax.broadcasted_iota(jnp.int32, slots_ref.shape, 1)
    found = jnp.zeros(slots_ref.shape, jnp.float32)
    for slot in range(capacity):
        chosen = jnp.where((down == owners) & (slots == slot), tagged, 0.0)
        found = jnp.where(lane == slot, jnp.sum(chosen, axis=1, keepdims=True), found)
    slots_ref[...] = found.astype(jnp.int32)


def slots_by_owner(cand, devices, pass_dev, capacity):
    vmem = pl.BlockSpec(memory_space=pltpu.VMEM)
    return pl.pallas_call(
        functools.partial(slots_kernel, pass_dev, capacity),
        in_specs=[vmem],
        out_specs=[vmem] * 2,
        out_shape=[
            jax.ShapeDtypeStruct((devices, capacity), jnp.int32),
            jax.ShapeDtypeStruct((1, cand.size), jnp.int32),
        ],
        compiler_params=pltpu.CompilerParams(vmem_limit_bytes=4 * MIB),
        name="slots_by_owner",
    )(cand)


def score_kernel(
    sizes,
    me_ref,
    ids,
    levels_hbm,
    cent_hbm,
    words_hbm,
    codes_hbm,
    lens_hbm,
    *rest,
):
    group_count, cent_count, per_device, query_len, capacity, pass_dev, cand_count = sizes
    query_hbm = rest[:group_count]
    (out_ref, staged, table, words, query_rows, query_t, own_t, dense, embed, maxima, codes, word_stage,
     code_stage, *more) = rest[group_count:]
    code_slots, more = more[:SLOTS], more[SLOTS:]
    (levels_ref, lens, work, work_quad, table_sem, words_sem, query_sem, small_sem,
     slot_sem) = more
    sources = ids.shape[0]
    items = sources * capacity
    tiles = words.shape[0] // (pass_dev * SUB)
    tile_tokens = SUB * FIELDS
    quad_sources = LANES // (per_device * query_len)
    quads = sources // quad_sources
    group_quads = cent_count // quad_sources
    per_bits = per_device.bit_length() - 1
    tile_bits = tiles.bit_length() - 1
    row_at = (pass_dev * tiles - 1).bit_length()
    lane_at = row_at + (items * tiles).bit_length()
    last_at = lane_at + (quad_sources * per_device - 1).bit_length()
    assert last_at + (tiles * tile_tokens - 1).bit_length() < 32
    next_tile = 1 + (1 << row_at) - (tile_tokens << last_at)
    parts = min(quads, PARTS)
    part_rows = staged.shape[0] // parts
    part_quads = quads // parts
    word_parts = words_sem.shape[0]
    part_words = words.shape[0] // word_parts

    def table_copy(part):
        rows = pl.ds(pl.multiple_of(part * part_rows, part_rows), part_rows)
        return pltpu.make_async_copy(cent_hbm.at[rows, :], staged.at[rows, :], table_sem.at[part])

    def words_copy(part):
        rows = pl.ds(part * part_words, part_words)
        return pltpu.make_async_copy(words_hbm.at[rows, :], words.at[rows, :], words_sem.at[part])

    def start_table(part, carry):
        table_copy(part).start()
        return carry

    group = jnp.bitwise_and(me_ref[0], group_count - 1)

    def query_copy(apart):
        return pltpu.make_async_copy(
            query_hbm[apart], query_rows.at[jnp.bitwise_xor(group, apart)], query_sem.at[apart]
        )

    lens_copy = pltpu.make_async_copy(lens_hbm, lens, small_sem.at[0])
    codes_copy = pltpu.make_async_copy(codes_hbm, codes, small_sem.at[1])
    levels_copy = pltpu.make_async_copy(levels_hbm, levels_ref, small_sem.at[2])
    lens_copy.start()
    levels_copy.start()
    for apart in range(group_count):
        query_copy(apart).start()
    lax.fori_loop(0, parts, start_table, 0)
    codes_copy.start()
    for part in range(word_parts):
        words_copy(part).start()

    maxima[...] = jnp.full(maxima.shape, MASKED, jnp.float32)
    query_copy(0).wait()
    own_t[...] = jnp.transpose(query_rows[group].astype(jnp.float32)).astype(jnp.bfloat16)
    lens_copy.wait()
    for apart in range(1, group_count):
        query_copy(apart).wait()

    spare = ((items * tiles) << row_at) - (1 << last_at)

    def fill(quad, count):
        block = query_rows[quad // group_quads, pl.ds(quad % group_quads * LANES, LANES), :]
        query_t[quad] = jnp.transpose(block.astype(jnp.float32)).astype(jnp.bfloat16)
        start = count
        found = []
        for part in range(quad_sources):
            cent = quad % group_quads * quad_sources + part
            source = cent * group_count + quad // group_quads
            rows = jnp.left_shift(source * (capacity * tiles), row_at)
            for slot in range(capacity):
                tag = ids[source, slot] - 1
                lane = part * per_device + jnp.bitwise_and(tag, per_device - 1)
                entry = rows + jnp.left_shift(lane, lane_at) + ((slot * tiles) << row_at)
                found.append((tag, jnp.right_shift(jnp.maximum(tag, 0), per_bits), entry))
        lengths = [lens[passage] for _, passage, _ in found]
        for (tag, passage, entry), length in zip(found, lengths):
            entry = entry + jnp.left_shift(passage, tile_bits) + jnp.left_shift(length - 1, last_at)
            for tile in range(tiles):
                work[count + tile] = entry + tile * next_tile
            blocks = jnp.right_shift(length + tile_tokens - 1, tile_tokens.bit_length() - 1)
            count = count + jnp.where(tag >= 0, blocks, 0)
        for index in range(ALIGN):
            work[count + index] = spare
        count = (count + ALIGN - 1) // ALIGN * ALIGN
        for index in range(quad_sources * capacity * tiles // ALIGN):
            work_quad[start // ALIGN + index] = quad
        return count

    def prepare(part, carry):
        count, best = carry
        table_copy(part).wait()
        rows = pl.ds(pl.multiple_of(part * part_rows, part_rows), part_rows)
        scores = jnp.dot(staged[rows, :], own_t[...], preferred_element_type=jnp.float32)
        best = jnp.maximum(best, jnp.max(scores.reshape(part_rows // SUB, SUB, scores.shape[1]), axis=0))
        table[rows, :] = staged[rows, :].astype(jnp.float32)
        for index in range(part_quads):
            count = fill(part * part_quads + index, count)
        return count, best

    lowest = jnp.full((SUB, own_t.shape[1]), -jnp.inf, jnp.float32)
    total, token_best = lax.fori_loop(0, parts, prepare, (0, lowest))
    token_best = jnp.max(token_best, axis=0, keepdims=True)
    for index in range((SLOTS + 2) * BLOCKS):
        work[total + index] = spare
    for index in range(2 * BLOCKS // ALIGN):
        work_quad[total // ALIGN + index] = 0
    chunks = jnp.maximum((total + BLOCKS - 1) // BLOCKS, 2)
    codes_copy.wait()
    levels_copy.wait()
    for part in range(word_parts):
        words_copy(part).wait()

    sub = lax.broadcasted_iota(jnp.int32, (SUB, LANES), 0)
    position = jnp.concatenate([sub * FIELDS + field for field in range(FIELDS)], axis=0)
    row_blocks = LANES // tile_tokens
    lane_tile = lax.broadcasted_iota(jnp.int32, (1, LANES), 1) // tile_tokens
    lane_group = lax.broadcasted_iota(jnp.int32, (1, LANES), 1) // query_len
    level = [levels_ref[index : index + 1, :] for index in range(FIELDS)]

    def score(chunk):
        scores = []
        for part in range(BLOCKS // ALIGN):
            rows = embed[part * ALIGN * tile_tokens : (part + 1) * ALIGN * tile_tokens, :]
            quad = work_quad[chunk * (BLOCKS // ALIGN) + part]
            scores.append(jnp.dot(rows, query_t[quad], preferred_element_type=jnp.float32))
        for index in range(BLOCKS):
            entry = work[chunk * BLOCKS + index]
            inner = index % ALIGN
            block = scores[index // ALIGN][inner * tile_tokens : (inner + 1) * tile_tokens]
            kept = jnp.where(position <= jnp.right_shift(entry, last_at), block, MASKED)
            best = jnp.max(kept, axis=0, keepdims=True)
            row = jnp.bitwise_and(jnp.right_shift(entry, row_at), (1 << (lane_at - row_at)) - 1)
            lane = jnp.bitwise_and(jnp.right_shift(entry, lane_at), (1 << (last_at - lane_at)) - 1)
            maxima[pl.ds(row, 1), :] = jnp.where(lane_group == lane, best, 0.0)

    def slot_copy(slot):
        return pltpu.make_async_copy(code_stage.at[slot], code_slots[slot], slot_sem.at[slot])

    def fetch_codes(chunk, slot):
        places = []
        for row in range(BLOCKS // row_blocks):
            together = jnp.zeros((1, LANES), jnp.int32)
            for index in range(row_blocks):
                entry = work[chunk * BLOCKS + row * row_blocks + index]
                place = jnp.bitwise_and(entry, (1 << row_at) - 1)
                passage = jnp.right_shift(place, tile_bits)
                shift = jnp.bitwise_and(index - place, row_blocks - 1) * tile_tokens
                moved = pltpu.roll(codes[pl.ds(passage, 1), :], shift, 1)
                together = jnp.where(lane_tile == index, moved, together)
                places.append(place)
            code_stage[slot, row : row + 1, :] = together
        return places

    def fetch_words(places, slot):
        for block, place in enumerate(places):
            rows = pl.ds(pl.multiple_of(place * SUB, SUB), SUB)
            word_stage[slot, block * SUB : (block + 1) * SUB, :] = words[rows, :]

    def decode(slot):
        for index in range(BLOCKS):
            word = word_stage[slot, index * SUB : (index + 1) * SUB, :]
            for field in range(FIELDS):
                rows = jnp.zeros((SUB, LANES), jnp.float32)
                for row in range(SUB):
                    place = index % row_blocks * tile_tokens + row * FIELDS + field
                    code = code_slots[slot][index // row_blocks, place]
                    rows = jnp.where(sub == row, table[pl.ds(code, SUB, stride=0), :], rows)
                low = jnp.bitwise_and(word, 1 << (2 * field)) != 0
                high = jnp.bitwise_and(word, 2 << (2 * field)) != 0
                residual = jnp.where(
                    high, jnp.where(low, level[3], level[2]), jnp.where(low, level[1], level[0])
                )
                base = index * tile_tokens + field * SUB
                dense[base : base + SUB, :] = rows + residual

    def normalize():
        for index in range(BLOCKS):
            rows = slice(index * tile_tokens, (index + 1) * tile_tokens)
            block = dense[rows, :]
            inverse = lax.rsqrt(jnp.sum(block * block, axis=1, keepdims=True) + 1e-06)
            embed[rows, :] = (block * inverse).astype(jnp.bfloat16)

    dense[...] = jnp.zeros(dense.shape, dense.dtype)
    embed[...] = jnp.zeros(embed.shape, embed.dtype)
    for slot in range(SLOTS):
        fetch_words(fetch_codes(slot, slot), slot)
        if slot < 2:
            slot_copy(slot).start()
        elif slot < SLOTS - 1:
            pl.when(slot < chunks)(slot_copy(slot).start)

    best_lanes = token_best.shape[1]
    for source in range(sources):
        out_ref[source, :, :best_lanes] = token_best

    def step(group, carry):
        for slot in range(SLOTS):
            chunk = SLOTS * group + slot
            pl.when(chunk + SLOTS - 1 < chunks)(slot_copy((slot + SLOTS - 1) % SLOTS).start)

            @pl.when(chunk < chunks)
            def _(chunk=chunk, slot=slot):
                slot_copy(slot).wait()
                score(jnp.maximum(chunk - 2, 0))
                normalize()
                places = fetch_codes(chunk + SLOTS, slot)
                decode(slot)
                fetch_words(places, slot)

        return carry

    lax.fori_loop(0, (chunks + SLOTS - 1) // SLOTS, step, 0)
    score(chunks - 2)
    normalize()
    score(chunks - 1)

    best = maxima[pl.ds(0, items, stride=tiles), :]
    for tile in range(1, tiles):
        best = jnp.maximum(best, maxima[pl.ds(tile, items, stride=tiles), :])
    sums = jnp.sum(best, axis=1, keepdims=True) / query_len
    item_down = lax.broadcasted_iota(jnp.int32, (items, LANES), 0)
    item_slot = lax.broadcasted_iota(jnp.int32, (items, LANES), 1)
    spread = jnp.where(item_down % capacity == item_slot, sums, 0.0)
    source_down = lax.broadcasted_iota(jnp.int32, (sources, items), 0)
    item_across = lax.broadcasted_iota(jnp.int32, (sources, items), 1)
    gather = (item_across // capacity == source_down).astype(jnp.float32)
    by_source = jnp.dot(
        gather, spread, precision=lax.Precision.HIGHEST, preferred_element_type=jnp.float32
    )
    for source in range(sources):
        out_ref[source, :, best_lanes:] = by_source[source : source + 1, :]


def owner_scores(me, slots, query_parts, centroids, token_codes, resid_words, lengths, levels, sizes):
    capacity = sizes[4]
    sources = slots.shape[0]
    group_count = len(query_parts)
    group_rows = query_parts[0].shape[0]
    cent_dev, width = centroids.shape
    pass_dev, plen = token_codes.shape
    packed = resid_words.shape[1]
    tiles = packed // SUB
    items = sources * capacity
    quads = group_count * group_rows // LANES
    work_size = items * tiles + quads * ALIGN + (SLOTS + 2) * BLOCKS
    any_space = pl.BlockSpec(memory_space=pl.ANY)
    in_hbm = pl.BlockSpec(memory_space=pltpu.HBM)
    pinned = [
        pltpu.with_memory_space_constraint(array, pltpu.HBM)
        for array in (levels, centroids, resid_words.reshape(pass_dev * packed, width), token_codes, lengths, query_parts[0])
    ]
    vmem = pl.BlockSpec(memory_space=pltpu.VMEM)
    tokens = items * plen
    return pl.pallas_call(
        functools.partial(score_kernel, sizes),
        in_specs=[pl.BlockSpec(memory_space=pltpu.SMEM)] * 2 + [in_hbm] * 6 + [any_space] * (group_count - 1),
        out_specs=vmem,
        out_shape=jax.ShapeDtypeStruct((sources, 1, group_rows + LANES), jnp.float32),
        scratch_shapes=[
            pltpu.VMEM((cent_dev, width), jnp.bfloat16),
            pltpu.VMEM((cent_dev + SUB, width), jnp.float32),
            pltpu.VMEM((pass_dev * packed, width), jnp.int32),
            pltpu.VMEM((group_count, group_rows, width), jnp.bfloat16),
            pltpu.VMEM((quads, width, LANES), jnp.bfloat16),
            pltpu.VMEM((width, group_rows), jnp.bfloat16),
            pltpu.VMEM((BLOCKS * SUB * FIELDS, width), jnp.float32),
            pltpu.VMEM((BLOCKS * SUB * FIELDS, width), jnp.bfloat16),
            pltpu.VMEM((items * tiles + SUB, LANES), jnp.float32),
            pltpu.VMEM((pass_dev, plen), jnp.int32),
            pltpu.VMEM((SLOTS, BLOCKS * SUB, LANES), jnp.int32),
            pltpu.VMEM((SLOTS, BLOCKS * SUB * FIELDS // LANES, LANES), jnp.int32),
            *[pltpu.SMEM((BLOCKS * SUB * FIELDS // LANES, LANES), jnp.int32)] * SLOTS,
            pltpu.VMEM(levels.shape, jnp.float32),
            pltpu.SMEM((pass_dev,), jnp.int32),
            pltpu.SMEM((work_size,), jnp.int32),
            pltpu.SMEM((work_size // ALIGN + items * tiles // quads,), jnp.int32),
            pltpu.SemaphoreType.DMA((min(quads, PARTS),)),
            pltpu.SemaphoreType.DMA((4,)),
            pltpu.SemaphoreType.DMA((group_count,)),
            pltpu.SemaphoreType.DMA((3,)),
            pltpu.SemaphoreType.DMA((SLOTS,)),
        ],
        compiler_params=pltpu.CompilerParams(vmem_limit_bytes=44 * MIB),
        cost_estimate=pl.CostEstimate(
            flops=2 * (tokens * LANES + cent_dev * group_rows) * width, bytes_accessed=2 * cent_dev * width * 2, transcendentals=tokens
        ),
        name="owner_scores",
    )(
        me, slots, *pinned, *query_parts[1:]
    )


def finish_kernel(sizes, me_ref, back_ref, target_ref, best_out, score_out):
    group_count, cent_count, _, query_len, capacity, _, _ = sizes
    group = jnp.bitwise_and(me_ref[0], group_count - 1)
    best_lanes = best_out.shape[0] * query_len
    best = back_ref[group, :, :best_lanes]
    for cent in range(1, cent_count):
        best = jnp.maximum(best, back_ref[cent * group_count + group, :, :best_lanes])
    for index in range(best_out.shape[0]):
        best_out[index : index + 1, :] = best[:, index * query_len : (index + 1) * query_len]
    back = back_ref[:, 0, best_lanes:]
    target = target_ref[...]
    owner = lax.broadcasted_iota(jnp.int32, (back.shape[0], target.shape[1]), 0)
    found = jnp.zeros(owner.shape, jnp.float32)
    for slot in range(capacity):
        found = found + jnp.where(owner * capacity + slot == target, back[:, slot : slot + 1], 0.0)
    scores = jnp.sum(found, axis=0, keepdims=True)
    width = score_out.shape[1]
    for index in range(score_out.shape[0]):
        score_out[index : index + 1, :] = scores[:, index * width : (index + 1) * width]


def finish(me, back, target, group_rows, sizes):
    _, _, per_device, query_len, _, _, cand_count = sizes
    vmem = pl.BlockSpec(memory_space=pltpu.VMEM)
    return pl.pallas_call(
        functools.partial(finish_kernel, sizes),
        in_specs=[pl.BlockSpec(memory_space=pltpu.SMEM), vmem, vmem],
        out_specs=[vmem] * 2,
        out_shape=[
            jax.ShapeDtypeStruct((group_rows, query_len), jnp.float32),
            jax.ShapeDtypeStruct((per_device, cand_count), jnp.float32),
        ],
        compiler_params=pltpu.CompilerParams(vmem_limit_bytes=4 * MIB),
        name="finish",
    )(me, back, target)


def shards(queries, centroids, candidates, token_codes, resid_words, lengths, levels):
    group_rows, query_len, width = queries.shape
    pass_dev = token_codes.shape[0]
    per_device, cand_count = candidates.shape[2:]
    pair_count = per_device * cand_count
    cent_count = lax.axis_size("cent")
    group_count = lax.axis_size("grp")
    devices = cent_count * group_count
    capacity = max(2, 2 * pair_count // devices)
    sizes = (group_count, cent_count, per_device, query_len, capacity, pass_dev, cand_count)
    cand = candidates.reshape(per_device, cand_count)
    query_rows = queries.reshape(group_rows * query_len, width)
    me = (lax.axis_index("cent") * group_count + lax.axis_index("grp")).astype(jnp.int32).reshape(1)
    slots, target = slots_by_owner(cand, devices, pass_dev, capacity)
    slots = lax.all_to_all(slots, ("cent", "grp"), split_axis=0, concat_axis=0, tiled=True)
    query_parts = [query_rows]
    for apart in range(1, group_count):
        pairs = [(index, index ^ apart) for index in range(group_count)]
        query_parts.append(lax.ppermute(query_rows, "grp", pairs))
    reply = owner_scores(
        me, slots, query_parts, centroids, token_codes, resid_words, lengths, levels, sizes
    )
    back = lax.all_to_all(reply, ("cent", "grp"), split_axis=0, concat_axis=0, tiled=True)
    token_best, scores = finish(me, back, target, group_rows, sizes)
    return (token_best, scores.reshape(1, 1, per_device, cand_count))


def solution(mesh):
    placed = (
        P("grp", None, None),
        P("cent", None),
        P("grp", "cent", None, None),
        P(("cent", "grp"), None),
        P(("cent", "grp"), None, None),
        P(("cent", "grp")),
        P(),
    )
    return jax.shard_map(
        shards,
        mesh=mesh,
        in_specs=placed,
        out_specs=(P("grp", None), P("grp", "cent", None, None)),
        check_vma=False,
    )
```
